128 devices in a mesh: dp: 32 (over y, z, core), mp: 4 (over x).
Axes of the slice: x: 4, y: 4, z: 4, core: 2. Of those that a mesh axis runs over, the one named last changes fastest.
Arguments:
- grads: bfloat16 [32, 16, 512, 512], P('dp', 'mp'), may hold values from -1000 to 1000, as said below
- block_owner: int32 [4, 4], P('mp'), may hold values from 0 to 63, as said below
- refresh_to: int32 [32, 4, 2], P('dp', 'mp'), may hold values from -1 to 3, as said below
- accum_old: float32 [32, 4, 2, 2, 512, 512], P('dp', 'mp'), may hold values from -0.006 to 60, as said below
- roots_old: float32 [32, 4, 2, 2, 512, 512], P('dp', 'mp'), may hold values from -1 to 1, as said below
Outputs:
- accum_new: float32 [32, 4, 2, 2, 512, 512], P('dp', 'mp')
- roots_new: float32 [32, 4, 2, 2, 512, 512], P('dp', 'mp')
- update: bfloat16 [16, 512, 512], P('mp')
The draws below stay inside these ranges and needn't reach their ends.
Inputs may be any that keep to these rules, and one draw needn't show every extreme that they name: `grads`: entries are bounded gradient values; rows and columns of a block have different scales. block_owner[c, k] = d * 2 + j puts block k of column c in slot j of dp device d of that column; positions differ within a column; in every column one device holds 2 blocks. `refresh_to`: -1 where the slot holds no block or keeps its previous roots, else a value from 0 to 3; the device holding 2 blocks refreshes all of them. `accum_old`: each matrix is symmetric with a dominant positive diagonal. `roots_old`: each matrix is symmetric with a positive diagonal.
All inputs are finite; a program needn't handle non-finite values.
Results may differ from the reference program's by a relative error of at most 0.0004.
Values may be sent and summed in bfloat16 or wider, within the bound.
A program may use at most 320 MiB of HBM per device.

```python
import math
import jax
import jax.numpy as jnp
from jax import lax

BS = 512
KB = 4
SLOTS = 2
ITERS = 3
NB = 16
N_DP = 32
N_MP = 4


def log_uniform(key, shape, lower, upper):
    return jnp.exp(jax.random.uniform(key, shape, jnp.float32, math.log(lower), math.log(upper)))


def owner_layout(key):

    def one_column(column_key):
        keys = jax.random.split(column_key, 6)
        devices = jax.random.permutation(keys[0], N_DP).astype(jnp.int32)
        ordering = jax.random.permutation(keys[1], KB).astype(jnp.int32)
        targets = jax.random.permutation(keys[2], N_MP).astype(jnp.int32)
        position = jnp.arange(KB, dtype=jnp.int32)
        heavy = position < SLOTS
        others = devices[jnp.clip(position - SLOTS + 1, 0, N_DP - 1)]
        holder = jnp.where(heavy, devices[0], others)
        slot_index = jnp.where(heavy, position, jax.random.randint(keys[3], (KB,), 0, SLOTS, dtype=jnp.int32))
        refresh = jnp.where(heavy, 1, jax.random.randint(keys[4], (KB,), 0, 2, dtype=jnp.int32))
        chosen = jnp.where(heavy, targets[jnp.clip(position, 0, N_MP - 1)], jax.random.randint(keys[5], (KB,), 0, N_MP, dtype=jnp.int32))
        worker = jnp.where(refresh > 0, chosen, -1)
        owner = jnp.zeros((KB,), jnp.int32).at[ordering].set(holder * SLOTS + slot_index)
        return (owner, holder, slot_index, worker)
    owner, holder, slot_index, worker = jax.vmap(one_column)(jax.random.split(key, N_MP))
    column_ids = jnp.broadcast_to(jnp.arange(N_MP, dtype=jnp.int32)[:, None], (N_MP, KB))
    table = jnp.full((N_MP, N_DP, SLOTS), -1, jnp.int32).at[column_ids, holder, slot_index].set(worker)
    return (owner, jnp.transpose(table, (1, 0, 2)))


def symmetric_field(key, shape, diag_low, diag_high, off_scale):
    keys = jax.random.split(key, 2)
    diagonal = log_uniform(keys[0], shape[:-1], diag_low, diag_high)
    rough = jax.random.uniform(keys[1], shape, jnp.float32, -1.0, 1.0)
    rough = 0.5 * (rough + jnp.swapaxes(rough, -1, -2)) * off_scale
    identity = jnp.eye(shape[-1], dtype=jnp.float32)
    return rough * (1.0 - identity) + identity * diagonal[..., None]


def draw_block_owner(key, part):
    return owner_layout(key)[0]


def draw_refresh_to(key, part):
    return owner_layout(key)[1]


def draw_grads(key, part):
    key = jax.random.fold_in(key, 11)
    keys = jax.random.split(key, 3)
    noise_part = jnp.clip(jax.random.normal(keys[0], (N_DP, NB, BS, BS), jnp.float32), -5.0, 5.0)
    ramp = 1.0 + 2.0 * jnp.arange(NB, dtype=jnp.float32) / max(NB - 1, 1)
    row_scale = log_uniform(keys[1], (NB, BS, 1), 1.0, 4.0)
    column_scale = log_uniform(keys[2], (NB, 1, BS), 1.0, 4.0)
    return (noise_part * row_scale * column_scale * ramp[:, None, None]).astype(jnp.bfloat16)


def draw_accum_old(key, part):
    key = jax.random.fold_in(key, 12)
    return symmetric_field(key, (N_DP, N_MP, SLOTS, 2, BS, BS), 4.0, 60.0, 0.006)


def draw_roots_old(key, part):
    key = jax.random.fold_in(key, 13)
    return symmetric_field(key, (N_DP, N_MP, SLOTS, 2, BS, BS), 0.3, 1.0, 0.3 / math.sqrt(BS))


def setup_inputs(seed: int = 0) -> dict:
    streams_of = jax.random.split(jax.random.key(seed), 6)
    grads = draw_grads(jax.random.fold_in(streams_of[5], 71), 0)
    block_owner = draw_block_owner(jax.random.fold_in(streams_of[5], 71), 0)
    refresh_to = draw_refresh_to(jax.random.fold_in(streams_of[5], 71), 0)
    accum_old = draw_accum_old(jax.random.fold_in(streams_of[5], 71), 0)
    roots_old = draw_roots_old(jax.random.fold_in(streams_of[5], 71), 0)
    return {"grads": grads, "block_owner": block_owner, "refresh_to": refresh_to, "accum_old": accum_old, "roots_old": roots_old}


decay_rate = 0.8
epsilon = 1e-06
highest_precision = lax.Precision.HIGHEST

def inverse_root(matrix):
    order_size = matrix.shape[-1]
    identity = jnp.eye(order_size, dtype=matrix.dtype)
    norm_scale = order_size * jnp.sqrt(jnp.mean(matrix * matrix) + epsilon)
    current = matrix / norm_scale
    factor = (5.0 * identity - current) / 4.0
    result = factor * norm_scale ** (-0.25)
    for iteration in range(ITERS - 1):
        square = jnp.dot(factor, factor, precision=highest_precision)
        fourth = jnp.dot(square, square, precision=highest_precision)
        current = jnp.dot(fourth, current, precision=highest_precision)
        factor = (5.0 * identity - current) / 4.0
        result = jnp.dot(result, factor, precision=highest_precision)
    return result

def reference(grads, block_owner, refresh_to, accum_old, roots_old):
    accum_new = accum_old
    roots_new = roots_old
    products = []
    update_square = jnp.float32(0.0)
    for column in range(N_MP):
        for block in range(KB):
            index_block = column * KB + block
            position = block_owner[column, block]
            device = position // SLOTS
            slot_index = position % SLOTS
            gradient = grads[:, index_block].astype(jnp.float32)
            left = jnp.einsum('iac,ibc->ab', gradient, gradient) / (N_DP * BS)
            right = jnp.einsum('ica,icb->ab', gradient, gradient) / (N_DP * BS)
            grad_sum = lax.optimization_barrier(jnp.sum(gradient, axis=0))
            fresh = jnp.stack([left, right])
            blended = decay_rate * accum_old[device, column, slot_index] + (1.0 - decay_rate) * fresh
            refreshed = jnp.stack([inverse_root(blended[0]), inverse_root(blended[1])])
            roots = jnp.where(refresh_to[device, column, slot_index] >= 0, refreshed, roots_old[device, column, slot_index])
            accum_new = accum_new.at[device, column, slot_index].set(blended)
            roots_new = roots_new.at[device, column, slot_index].set(roots)
            partial_product = jnp.dot(roots[0], grad_sum, precision=highest_precision)
            product = jnp.dot(partial_product, roots[1], precision=highest_precision)
            update_square = update_square + jnp.sum(product * product)
            products.append(product)
    ratio = 1.0 / jnp.sqrt(update_square / float(NB * BS * BS) + epsilon)
    update = (ratio * jnp.stack(products)).astype(jnp.bfloat16)
    return (accum_new, roots_new, update)
```

```python
import functools

import jax
import jax.numpy as jnp
from jax import lax
from jax.experimental import pallas as pl
from jax.experimental.pallas import tpu as pltpu
from jax.sharding import PartitionSpec as P

MESH = pl.DeviceIdType.MESH
F32 = jnp.float32
BF16 = jnp.bfloat16

BS = 512
KB = 4
SLOTS = 2
TL = 128
TILES = [(a, b) for a in range(4) for b in range(a, 4)]
NT = len(TILES)
SP = 5
GP = 4
decay_rate = 0.8
epsilon = 1e-06


def coords():
    d = lax.axis_index("dp")
    return d // 8, (d // 2) % 4, d % 2


def at(y, z, c):
    return {"dp": (y * 4 + z) * 2 + c}


def dot_nt(a, b):
    return lax.dot_general(a, b, (((1,), (1,)), ((), ())), preferred_element_type=F32)


def dot_tn(a, b):
    return lax.dot_general(a, b, (((0,), (0,)), ((), ())), preferred_element_type=F32)


def dot_nn(a, b):
    return lax.dot_general(a, b, (((1,), (0,)), ((), ())), preferred_element_type=F32)


def stats_kernel(
    g_ref, rf_ref, acc_ref, o_ref, gq_ref, pacc_ref, prf_ref,
    praw, st, r1, r2, f3,
    s_raw, s_rf, s_acc, s1, q1, s2, q2, s3, q3, s4, q4, sd, qd, sl,
):
    y, z, c = coords()
    pos1 = z + c * (y - z)
    pos2 = y + c * (z - y)

    def dev1(p):
        return at(y + c * (p - y), p + c * (z - p), c)

    def dev2(p):
        return at(p + c * (y - p), z + c * (p - z), c)

    mate = at(y, z, 1 - c)

    barrier = pltpu.get_barrier_semaphore()
    for o in (1, 2, 3):
        pl.semaphore_signal(barrier, inc=1, device_id=dev1((pos1 + o) % 4), device_id_type=MESH)
        pl.semaphore_signal(barrier, inc=1, device_id=dev2((pos2 + o) % 4), device_id_type=MESH)
    pl.semaphore_signal(barrier, inc=1, device_id=mate, device_id_type=MESH)
    pl.semaphore_wait(barrier, 7)

    def rcopy(src, dst, ss, rs, device):
        return pltpu.make_async_remote_copy(
            src_ref=src, dst_ref=dst, send_sem=ss, recv_sem=rs, device_id=device, device_id_type=MESH
        )

    raw = rcopy(g_ref.at[pl.ds(2 * (1 - c), 2)], praw, s_raw.at[0], s_raw.at[1], mate)
    raw.start()
    accs = [
        rcopy(acc_ref.at[j, 1], pacc_ref.at[j], s_acc.at[0, j], s_acc.at[1, j], mate) for j in range(SLOTS)
    ]
    flags = rcopy(rf_ref, prf_ref, s_rf.at[0], s_rf.at[1], mate)
    flags.start()
    for a in accs:
        a.start()

    def c1(p, o, q):
        return rcopy(st.at[p, q], r1.at[o - 1, q], s1.at[o - 1, q], q1.at[o - 1, q], dev1(p))

    raw.wait()

    def put(p, a, b, block):
        t = TILES.index((a, b))
        for half in range(2):
            h = 2 * t + half
            st[p, h // SP, h % SP] = block[half * 64:(half + 1) * 64]

    def quadrants(p, quad):
        x = quad(0, 0)
        put(p, 0, 0, x[:128, :128])
        put(p, 0, 1, x[:128, 128:])
        put(p, 1, 1, x[128:, 128:])
        x = quad(0, 1)
        put(p, 0, 2, x[:128, :128])
        put(p, 0, 3, x[:128, 128:])
        put(p, 1, 2, x[128:, :128])
        put(p, 1, 3, x[128:, 128:])
        x = quad(1, 1)
        put(p, 2, 2, x[:128, :128])
        put(p, 2, 3, x[:128, 128:])
        put(p, 3, 3, x[128:, 128:])

    @pl.loop(0, 4)
    def _(i):
        p = (pos1 + jnp.where(i == 0, 2, jnp.where(i == 1, 1, jnp.where(i == 2, 3, 0)))) % 4
        o = (pos1 - p + 4) % 4
        blk = p // 2
        lr = p % 2

        @pl.when(lr == 0)
        def _():
            quadrants(
                p,
                lambda a, b: dot_nt(
                    g_ref[2 * c + blk, a * 256:(a + 1) * 256, :], g_ref[2 * c + blk, b * 256:(b + 1) * 256, :]
                )
                + dot_nt(praw[blk, a * 256:(a + 1) * 256, :], praw[blk, b * 256:(b + 1) * 256, :]),
            )

        @pl.when(lr == 1)
        def _():
            quadrants(
                p,
                lambda a, b: dot_tn(
                    g_ref[2 * c + blk, :, a * 256:(a + 1) * 256], g_ref[2 * c + blk, :, b * 256:(b + 1) * 256]
                )
                + dot_tn(praw[blk, :, a * 256:(a + 1) * 256], praw[blk, :, b * 256:(b + 1) * 256]),
            )

        for q in range(4):
            rows = pl.ds(lr * 256 + q * 64, 64)
            total = g_ref[2 * c + blk, rows, :].astype(F32) + praw[blk, rows, :].astype(F32)
            for k in range(GP):
                st[p, q, SP + k] = total[:, k * 128:(k + 1) * 128]

        @pl.when(i < 3)
        def _():
            for k in range(4):
                q = (pos2 + 1 + k) % 4
                c1(p, o, q).start()

    def c2(q):
        o = (pos2 - q + 4) % 4
        return rcopy(st.at[pos1, q], r2.at[o - 1], s2.at[o - 1], q2.at[o - 1], dev2(q))

    @pl.loop(1, 5)
    def _(k):
        q = (pos2 + k) % 4
        for o in (1, 2, 3):
            c1(pos1, o, q).wait_recv()
        st[pos1, q] = (st[pos1, q] + r1[0, q]) + (r1[1, q] + r1[2, q])

        @pl.when(k < 4)
        def _():
            c2(q).start()

    for o in (1, 2, 3):
        c2((pos2 + o) % 4).wait_recv()
    f3[pos2] = (st[pos1, pos2] + r2[0]) + (r2[1] + r2[2])

    def c3(o):
        return rcopy(f3.at[pos2], f3.at[pos2], s3.at[o - 1], q3.at[o - 1], dev2((pos2 - o + 4) % 4))

    def c4(o, q):
        return rcopy(
            f3.at[q, pl.ds(0, SP)], o_ref.at[c, pos1, q], s4.at[o - 1, q], q4.at[o - 1, q],
            dev1((pos1 - o + 4) % 4),
        )

    def cd_own(q):
        return rcopy(f3.at[q, pl.ds(0, SP)], o_ref.at[c, pos1, q], sd.at[0, q], qd.at[0, q], mate)

    def cd(o, q):
        p = (pos1 + o) % 4
        return rcopy(o_ref.at[c, p, q], o_ref.at[c, p, q], sd.at[o, q], qd.at[o, q], mate)

    def keep(q):
        return pltpu.make_async_copy(f3.at[q, pl.ds(0, SP)], o_ref.at[c, pos1, q], sl.at[0, q])

    def keep_g(q):
        return pltpu.make_async_copy(f3.at[q, pl.ds(SP, GP)], gq_ref.at[q], sl.at[1, q])

    for o in (2, 1, 3):
        c3(o).start()

    for k, o in ((0, 0), (1, 1), (3, 3), (2, 2)):
        q = (pos2 + k) % 4
        if k:
            rcopy(f3.at[pos2], f3.at[q], s3.at[o - 1], q3.at[o - 1], dev2(q)).wait_recv()
        for oo in (2, 1, 3):
            c4(oo, q).start()
        cd_own(q).start()
        keep(q).start()
        keep_g(q).start()

    for o in (1, 3, 2):
        for k in (0, 1, 3, 2):
            q = (pos2 + k) % 4
            p = (pos1 + o) % 4
            rcopy(
                f3.at[q, pl.ds(0, SP)], o_ref.at[c, p, q], s4.at[o - 1, q], q4.at[o - 1, q], dev1(p)
            ).wait_recv()
            cd(o, q).start()

    flags.wait()
    for a in accs:
        a.wait()
    for k in range(1, 4):
        p = (pos1 + k) % 4
        for q in range(4):
            c1(p, (pos1 - p + 4) % 4, q).wait_send()
        c2((pos2 + k) % 4).wait_send()
        c3(k).wait_send()
    for q in range(4):
        keep(q).wait()
        keep_g(q).wait()
        for o in (1, 2, 3):
            c4(o, q).wait_send()
        own = cd_own(q)
        own.wait_send()
        rcopy(f3.at[q, pl.ds(0, SP)], o_ref.at[1 - c, pos2, q], sd.at[0, q], qd.at[0, q], mate).wait_recv()
        for o in (1, 2, 3):
            cd(o, q).wait_send()
    for q in range(4):
        for o in (1, 2, 3):
            p = (pos2 + o) % 4
            rcopy(o_ref.at[1 - c, p, q], o_ref.at[1 - c, p, q], sd.at[o, q], qd.at[o, q], mate).wait_recv()


def call_stats(grads, refresh, acc):
    dma = pltpu.SemaphoreType.DMA
    return pl.pallas_call(
        stats_kernel,
        name="stats",
        out_shape=(
            jax.ShapeDtypeStruct((2, 4, 4, SP, 64, TL), F32),
            jax.ShapeDtypeStruct((4, GP, 64, TL), F32),
            jax.ShapeDtypeStruct((SLOTS, BS, BS), F32),
            jax.ShapeDtypeStruct((8, TL), jnp.int32),
        ),
        in_specs=[pl.BlockSpec(memory_space=pltpu.VMEM)] * 2 + [pl.BlockSpec(memory_space=pl.ANY)],
        out_specs=(pl.BlockSpec(memory_space=pl.ANY),) * 3 + (pl.BlockSpec(memory_space=pltpu.VMEM),),
        scratch_shapes=[
            pltpu.VMEM((2, BS, BS), BF16),
            pltpu.VMEM((4, 4, SP + GP, 64, TL), F32),
            pltpu.VMEM((3, 4, SP + GP, 64, TL), F32),
            pltpu.VMEM((3, SP + GP, 64, TL), F32),
            pltpu.VMEM((4, SP + GP, 64, TL), F32),
            dma((2,)), dma((2,)), dma((2, SLOTS)),
            dma((3, 4)), dma((3, 4)), dma((3,)), dma((3,)), dma((3,)), dma((3,)),
            dma((3, 4)), dma((3, 4)), dma((4, 4)), dma((4, 4)), dma((2, 4)),
        ],
        compiler_params=pltpu.CompilerParams(
            collective_id=1, has_side_effects=True, vmem_limit_bytes=40 << 20
        ),
    )(grads, refresh, acc)


def split(x):
    hi = x.astype(BF16)
    return hi, (x - hi.astype(F32)).astype(BF16)


def dot3(ah, al, bh, bl):
    return dot_nn(ah, bh) + (dot_nn(ah, bl) + dot_nn(al, bh))


def find_slot(owner_ref, place):
    block = jnp.int32(0)
    alive = jnp.int32(0)
    for k in range(KB):
        hit = (owner_ref[0, k] == place).astype(jnp.int32)
        block = block + k * hit
        alive = alive + hit
    return block, alive


def roots_kernel(
    owner_ref, rf_ref, prf_ref, st_ref, acc_ref, pacc_ref, old_ref,
    new_ref, lroot_ref, rroot_ref,
    flag, a_buf, s_buf, mf, tf, m1f, vf, mh, ml, th, tl, uh, ul, m1h, m1l, vh, vl, xbuf,
    sem_a, sem_s, sem_o, sem_r,
):
    d = lax.axis_index("dp")
    mate = d + 1 - 2 * (d % 2)
    for j in range(SLOTS):
        blk, alive = find_slot(owner_ref, d * SLOTS + j)
        fresh = alive * (rf_ref[0, j] >= 0).astype(jnp.int32)
        pblk, palive = find_slot(owner_ref, mate * SLOTS + j)
        pfresh = palive * (prf_ref[0, j] >= 0).astype(jnp.int32)
        flag[0, j], flag[0, 4 + j], flag[0, 2 + j] = blk, blk, pblk
        flag[1, j], flag[1, 4 + j], flag[1, 2 + j] = alive, alive, pfresh
        flag[2, j], flag[2, 2 + j] = fresh, pfresh

    flag[3, 0] = jnp.int32(0)

    def old(i):
        if 2 <= i < 4:
            return pacc_ref.at[i - 2]
        return acc_ref.at[i % 2, i // 4]

    for i in (0, 1, 2, 3, 4, 5):
        pltpu.make_async_copy(old(i), a_buf.at[i], sem_a.at[i]).start()
        lr = 0 if i < 2 else 1
        pltpu.make_async_copy(st_ref.at[flag[0, i], lr], s_buf.at[i], sem_s.at[i]).start()
    for j in range(SLOTS):
        @pl.when(flag[2, j] == 0)
        def _():
            pltpu.make_async_copy(old_ref.at[j, 0], lroot_ref.at[j], sem_r.at[j]).start()

    @pl.loop(0, 6)
    def _(i):
        pltpu.make_async_copy(acc_ref.at[0, 0], a_buf.at[i], sem_a.at[i]).wait()
        pltpu.make_async_copy(st_ref.at[0, 0], s_buf.at[i], sem_s.at[i]).wait()

        @pl.when(flag[1, i] == 1)
        def _():
            for t, (a, b) in enumerate(TILES):
                fresh = s_buf[i, t] * F32((1.0 - decay_rate) / 16384.0)
                ra, rb = pl.ds(a * TL, TL), pl.ds(b * TL, TL)
                a_buf[i, ra, rb] = decay_rate * a_buf[i, ra, rb] + fresh
                if a != b:
                    a_buf[i, rb, ra] = decay_rate * a_buf[i, rb, ra] + fresh.T

    outs = [pltpu.make_async_copy(a_buf.at[i], new_ref.at[i % 2, i // 4], sem_o.at[i]) for i in (0, 1, 4, 5)]
    for o in outs:
        o.start()

    half = BS // 2
    c4 = 625.0 / 256.0

    def each(fn):
        @pl.loop(0, 2)
        def _(h):
            fn(pl.ds(pl.multiple_of(h * half, half), half))

    def put(ref, hi, lo, rows, x):
        if ref is not None:
            ref[rows, :] = x
        hi[rows, :], lo[rows, :] = split(x)

    def mul(rows, ah, al, bh, bl):
        return dot3(ah[rows, :], al[rows, :], bh[...], bl[...])

    @pl.loop(0, 4)
    def _(t):
        @pl.when(flag[2, t] == 1)
        def _():
            a = a_buf[t]
            square = jnp.sum(a * a, axis=0, keepdims=True)
            mean = jnp.sum(square, axis=1, keepdims=True) * (1.0 / (BS * BS))
            scale = BS * jnp.sqrt(mean + epsilon)
            inverse = 1.0 / scale
            outer = 1.0 / jnp.sqrt(jnp.sqrt(scale))

            def start(rows):
                put(mf, mh, ml, rows, a_buf[t, rows, :] * inverse)

            each(start)

            def first(rows):
                q = mul(rows, mh, ml, mh, ml)
                put(tf, th, tl, rows, (q - 10.0 * mf[rows, :]) * (1.0 / 16.0))

            each(first)

            def second(rows):
                q = mul(rows, th, tl, th, tl)
                put(None, uh, ul, rows, (25.0 / 8.0) * tf[rows, :] + q)

            each(second)

            def third(rows):
                q = mul(rows, uh, ul, mh, ml)
                put(m1f, m1h, m1l, rows, c4 * mf[rows, :] + q)

            each(third)

            def fourth(rows):
                q = mul(rows, m1h, m1l, m1h, m1l)
                put(tf, th, tl, rows, (q - 10.0 * m1f[rows, :]) * (1.0 / 16.0))
                q = mul(rows, mh, ml, m1h, m1l)
                put(vf, vh, vl, rows, q * (1.0 / 16.0) - (5.0 / 16.0) * (mf[rows, :] + m1f[rows, :]))

            each(fourth)

            each(second)

            def seventh(rows):
                q = mul(rows, uh, ul, m1h, m1l)
                put(mf, mh, ml, rows, c4 * m1f[rows, :] + q)

            each(seventh)

            @pl.when(flag[3, 0] == 1)
            def _():
                pltpu.make_async_copy(xbuf, rroot_ref.at[0], sem_r.at[2]).wait()

            flag[3, 0] = jnp.int32(1)

            def last(rows):
                q = mul(rows, vh, vl, mh, ml)
                x = 1.25 * vf[rows, :] - (25.0 / 64.0) * mf[rows, :] - 0.25 * q
                r = lax.broadcasted_iota(jnp.int32, (half, BS), 0) + rows.start
                k = lax.broadcasted_iota(jnp.int32, (half, BS), 1)
                xbuf[rows, :] = outer * (x + jnp.where(r == k, F32(125.0 / 64.0), F32(0.0)))

            each(last)

            @pl.when(t < 2)
            def _():
                pltpu.make_async_copy(xbuf, lroot_ref.at[t % 2], sem_r.at[2]).start()

            @pl.when(t >= 2)
            def _():
                pltpu.make_async_copy(xbuf, rroot_ref.at[t % 2], sem_r.at[2]).start()

    @pl.when(flag[3, 0] == 1)
    def _():
        pltpu.make_async_copy(xbuf, rroot_ref.at[0], sem_r.at[2]).wait()
    for j in range(SLOTS):
        @pl.when(flag[2, j] == 0)
        def _():
            pltpu.make_async_copy(old_ref.at[j, 0], lroot_ref.at[j], sem_r.at[j]).wait()
    for o in outs:
        o.wait()


def call_roots(owner, refresh, prefresh, stats, acc, pacc, old):
    dma = pltpu.SemaphoreType.DMA
    anywhere = pl.BlockSpec(memory_space=pl.ANY)
    smem = pl.BlockSpec(memory_space=pltpu.SMEM)
    full = lambda dt: pltpu.VMEM((BS, BS), dt)
    return pl.pallas_call(
        roots_kernel,
        name="roots",
        out_shape=(
            jax.ShapeDtypeStruct((SLOTS, 2, BS, BS), F32),
            jax.ShapeDtypeStruct((SLOTS, BS, BS), F32),
            jax.ShapeDtypeStruct((SLOTS, BS, BS), F32),
        ),
        in_specs=[smem] * 3 + [anywhere] * 4,
        out_specs=(anywhere,) * 3,
        scratch_shapes=[
            pltpu.SMEM((4, 8), jnp.int32),
            pltpu.VMEM((6, BS, BS), F32),
            pltpu.VMEM((6, NT, TL, TL), F32),
        ]
        + [full(F32)] * 4 + [full(BF16)] * 10 + [full(F32)]
        + [dma((6,)), dma((6,)), dma((6,)), dma((3,))],
        compiler_params=pltpu.CompilerParams(vmem_limit_bytes=40 << 20),
        cost_estimate=pl.CostEstimate(flops=20 * 10**9, bytes_accessed=20 << 20, transcendentals=0),
    )(owner, refresh, prefresh, stats, acc, pacc, old)


def product_kernel(
    owner_ref, rf_ref, l_ref, r_ref, old_ref, *rest,
):
    g_refs = rest[:8]
    roots_ref, sq_ref, p_ref, flag, lbuf, rbuf, gbuf, gh, gl, sem = rest[8:]
    d = lax.axis_index("dp")
    c = d % 2
    pos1 = (d // 2) % 4 + c * (d // 8 - (d // 2) % 4)
    pos2 = d // 8 + c * ((d // 2) % 4 - d // 8)
    outs = []
    for j in range(SLOTS):
        blk, alive = find_slot(owner_ref, d * SLOTS + j)
        fresh = alive * (rf_ref[0, j] >= 0).astype(jnp.int32)
        flag[0, j], flag[1, j] = alive, fresh
        pltpu.make_async_copy(l_ref.at[j], lbuf.at[j], sem.at[j, 0]).start()

        @pl.when(fresh == 1)
        def _():
            pltpu.make_async_copy(r_ref.at[j], rbuf.at[j], sem.at[j, 1]).start()

        @pl.when(fresh == 0)
        def _():
            pltpu.make_async_copy(old_ref.at[j, 1], rbuf.at[j], sem.at[j, 1]).start()

        mine = (blk // 2 == c).astype(jnp.int32)
        for h in range(2):
            p = 2 * (blk % 2) + h
            o = lax.rem(p - jnp.where(mine == 1, pos1, pos2) + 4, 4)
            for i in range(8):
                @pl.when((o == i % 4) & (mine == 1 - i // 4))
                def _():
                    pltpu.make_async_copy(g_refs[i], gbuf.at[j, h], sem.at[j, 2 + h]).start()
    for j in range(SLOTS):
        pltpu.make_async_copy(l_ref.at[j], lbuf.at[j], sem.at[j, 0]).wait()
        outs.append(pltpu.make_async_copy(lbuf.at[j], roots_ref.at[j, 0], sem.at[j, 4]))
        outs[-1].start()
    sq_ref[...] = jnp.zeros_like(sq_ref)
    for j in range(SLOTS):
        pltpu.make_async_copy(r_ref.at[j], rbuf.at[j], sem.at[j, 1]).wait()
        for h in range(2):
            pltpu.make_async_copy(g_refs[0], gbuf.at[j, h], sem.at[j, 2 + h]).wait()
        outs.append(pltpu.make_async_copy(rbuf.at[j], roots_ref.at[j, 1], sem.at[j, 5]))
        outs[-1].start()

    @pl.loop(0, SLOTS)
    def _(j):
        @pl.when(flag[0, j] == 1)
        def _():
            for h in range(2):
                for q in range(4):
                    for k in range(4):
                        rows, cols = pl.ds(h * 256 + q * 64, 64), pl.ds(k * TL, TL)
                        gh[0, rows, cols], gl[0, rows, cols] = split(gbuf[j, h, q, k])
            gh[1], gl[1] = split(rbuf[j])

            @pl.loop(0, 2)
            def _(h):
                rows = pl.ds(pl.multiple_of(h * 256, 256), 256)
                ah, al = split(lbuf[j, rows, :])
                t = dot3(ah, al, gh[0], gl[0])
                th, tl = split(t)
                x = dot3(th, tl, gh[1], gl[1])
                p_ref[j, rows, :] = x
                part = jnp.sum((x * x).reshape(32, 8, BS), axis=0)
                sq_ref[...] += (part[:, :128] + part[:, 128:256]) + (part[:, 256:384] + part[:, 384:])

        @pl.when(flag[0, j] == 0)
        def _():
            p_ref[j] = jnp.zeros((BS, BS), F32)

    for o in outs:
        o.wait()


def call_product(owner, refresh, lroot, rroot, old, pieces):
    anywhere = pl.BlockSpec(memory_space=pl.ANY)
    smem = pl.BlockSpec(memory_space=pltpu.SMEM)
    vmem = pl.BlockSpec(memory_space=pltpu.VMEM)
    return pl.pallas_call(
        product_kernel,
        name="product",
        out_shape=(
            jax.ShapeDtypeStruct((SLOTS, 2, BS, BS), F32),
            jax.ShapeDtypeStruct((8, TL), F32),
            jax.ShapeDtypeStruct((SLOTS, BS, BS), F32),
        ),
        in_specs=[smem] * 2 + [anywhere] * 11,
        out_specs=(anywhere, vmem, vmem),
        scratch_shapes=[
            pltpu.SMEM((2, 2), jnp.int32),
            pltpu.VMEM((SLOTS, BS, BS), F32),
            pltpu.VMEM((SLOTS, BS, BS), F32),
            pltpu.VMEM((SLOTS, 2, 4, GP, 64, TL), F32),
            pltpu.VMEM((2, BS, BS), BF16),
            pltpu.VMEM((2, BS, BS), BF16),
            pltpu.SemaphoreType.DMA((SLOTS, 6)),
        ],
        compiler_params=pltpu.CompilerParams(vmem_limit_bytes=40 << 20),
    )(owner, refresh, lroot, rroot, old, *pieces)


def permute(x, n, place):
    pairs = []
    for d in range(n):
        y, z, c = d // 8, (d // 2) % 4, d % 2
        pairs.append((d, place(y, z, c)))
    return lax.ppermute(x, "dp", pairs)


def number(y, z, c):
    return ((y % 4) * 4 + z % 4) * 2 + c


def per_device(grads, block_owner, refresh_to, accum_old, roots_old):
    n_dp = lax.axis_size("dp")
    n_mp = lax.axis_size("mp")
    my_index = lax.axis_index("dp")
    acc, old = accum_old[0, 0], roots_old[0, 0]
    refresh = jnp.pad(refresh_to[0], ((0, 7), (0, TL - SLOTS)))
    stats, gq, pacc, prefresh = call_stats(grads[0], refresh, acc)
    stats = stats.reshape(KB, 2, NT, TL, TL)
    new_accum, lroot, rroot = call_roots(block_owner, refresh, prefresh, stats, acc, pacc, old)
    line = [gq]
    for o in (1, 2, 3):
        line.append(permute(gq, n_dp, lambda y, z, c: number(y - o * c, z - o * (1 - c), c)))
    swap = lambda y, z, c: number(y, z, 1 - c)
    pieces = line + [permute(x, n_dp, swap) for x in line]
    rroot = permute(rroot, n_dp, swap)
    roots, sq, product = call_product(block_owner, refresh, lroot, rroot, old, pieces)

    update_norm = lax.psum(jnp.sum(sq), ("dp", "mp"))
    ratio = 1.0 / jnp.sqrt(update_norm / float(KB * n_mp * BS * BS) + epsilon)
    scaled = (ratio * product).astype(BF16)
    places = jnp.arange(n_dp * SLOTS, dtype=jnp.int32).reshape(n_dp, SLOTS)
    chooser = places[:, :, None] == block_owner[0][None, None, :]
    sending = scaled.reshape(SLOTS, n_dp, BS // n_dp, BS)
    gotten = lax.all_to_all(sending, "dp", split_axis=1, concat_axis=1, tiled=True)
    picked = jnp.einsum(
        "djk,jdrc->krc", chooser.astype(BF16), gotten, preferred_element_type=F32
    ).astype(BF16)
    update = lax.all_gather(picked, "dp", axis=1, tiled=True)
    return (new_accum[None, None], roots[None, None], update)


def solution(mesh):
    in_specs = (
        P("dp", "mp", None, None),
        P("mp", None),
        P("dp", "mp", None),
        P("dp", "mp", None, None, None, None),
        P("dp", "mp", None, None, None, None),
    )
    out_specs = (
        P("dp", "mp", None, None, None, None),
        P("dp", "mp", None, None, None, None),
        P("mp", None, None),
    )
    return jax.shard_map(
        per_device, mesh=mesh, in_specs=in_specs, out_specs=out_specs, check_vma=False
    )
```

```python
import functools

import jax
import jax.numpy as jnp
from jax import lax
from jax.experimental import pallas as pl
from jax.experimental.pallas import tpu as pltpu
from jax.sharding import PartitionSpec as P

MESH = pl.DeviceIdType.MESH
F32 = jnp.float32
BF16 = jnp.bfloat16

BS = 512
KB = 4
SLOTS = 2
TL = 128
TILES = [(a, b) for a in range(4) for b in range(a, 4)]
NT = len(TILES)
SP = 5
GP = 4
decay_rate = 0.8
epsilon = 1e-06


def coords():
    d = lax.axis_index("dp")
    return d // 8, (d // 2) % 4, d % 2


def at(y, z, c):
    return {"dp": (y * 4 + z) * 2 + c}


def dot_nt(a, b):
    return lax.dot_general(a, b, (((1,), (1,)), ((), ())), preferred_element_type=F32)


def dot_tn(a, b):
    return lax.dot_general(a, b, (((0,), (0,)), ((), ())), preferred_element_type=F32)


def dot_nn(a, b):
    return lax.dot_general(a, b, (((1,), (0,)), ((), ())), preferred_element_type=F32)


def stats_kernel(
    g_ref, rf_ref, acc_ref, o_ref, gq_ref, pacc_ref, prf_ref,
    praw, st, r1, r2, f3,
    s_raw, s_rf, s_acc, s1, q1, s2, q2, s3, q3, s4, q4, sd, qd, sl,
):
    y, z, c = coords()
    pos1 = z + c * (y - z)
    pos2 = y + c * (z - y)

    def dev1(p):
        return at(y + c * (p - y), p + c * (z - p), c)

    def dev2(p):
        return at(p + c * (y - p), z + c * (p - z), c)

    mate = at(y, z, 1 - c)

    barrier = pltpu.get_barrier_semaphore()
    for o in (1, 2, 3):
        pl.semaphore_signal(barrier, inc=1, device_id=dev1((pos1 + o) % 4), device_id_type=MESH)
        pl.semaphore_signal(barrier, inc=1, device_id=dev2((pos2 + o) % 4), device_id_type=MESH)
    pl.semaphore_signal(barrier, inc=1, device_id=mate, device_id_type=MESH)
    pl.semaphore_wait(barrier, 7)

    def rcopy(src, dst, ss, rs, device):
        return pltpu.make_async_remote_copy(
            src_ref=src, dst_ref=dst, send_sem=ss, recv_sem=rs, device_id=device, device_id_type=MESH
        )

    raw = rcopy(g_ref.at[pl.ds(2 * (1 - c), 2)], praw, s_raw.at[0], s_raw.at[1], mate)
    raw.start()
    accs = [
        rcopy(acc_ref.at[j, 1], pacc_ref.at[j], s_acc.at[0, j], s_acc.at[1, j], mate) for j in range(SLOTS)
    ]
    flags = rcopy(rf_ref, prf_ref, s_rf.at[0], s_rf.at[1], mate)
    flags.start()
    for a in accs:
        a.start()

    def c1(p, o, q):
        return rcopy(st.at[p, q], r1.at[o - 1, q], s1.at[o - 1, q], q1.at[o - 1, q], dev1(p))

    raw.wait()

    def put(p, a, b, block):
        t = TILES.index((a, b))
        for half in range(2):
            h = 2 * t + half
            st[p, h // SP, h % SP] = block[half * 64:(half + 1) * 64]

    def quadrants(p, quad):
        x = quad(0, 0)
        put(p, 0, 0, x[:128, :128])
        put(p, 0, 1, x[:128, 128:])
        put(p, 1, 1, x[128:, 128:])
        x = quad(0, 1)
        put(p, 0, 2, x[:128, :128])
        put(p, 0, 3, x[:128, 128:])
        put(p, 1, 2, x[128:, :128])
        put(p, 1, 3, x[128:, 128:])
        x = quad(1, 1)
        put(p, 2, 2, x[:128, :128])
        put(p, 2, 3, x[:128, 128:])
        put(p, 3, 3, x[128:, 128:])

    @pl.loop(0, 4)
    def _(i):
        p = (pos1 + jnp.where(i == 0, 2, jnp.where(i == 1, 1, jnp.where(i == 2, 3, 0)))) % 4
        o = (pos1 - p + 4) % 4
        blk = p // 2
        lr = p % 2

        @pl.when(lr == 0)
        def _():
            quadrants(
                p,
                lambda a, b: dot_nt(
                    g_ref[2 * c + blk, a * 256:(a + 1) * 256, :], g_ref[2 * c + blk, b * 256:(b + 1) * 256, :]
                )
                + dot_nt(praw[blk, a * 256:(a + 1) * 256, :], praw[blk, b * 256:(b + 1) * 256, :]),
            )

        @pl.when(lr == 1)
        def _():
            quadrants(
                p,
                lambda a, b: dot_tn(
                    g_ref[2 * c + blk, :, a * 256:(a + 1) * 256], g_ref[2 * c + blk, :, b * 256:(b + 1) * 256]
                )
                + dot_tn(praw[blk, :, a * 256:(a + 1) * 256], praw[blk, :, b * 256:(b + 1) * 256]),
            )

        for q in range(4):
            rows = pl.ds(lr * 256 + q * 64, 64)
            total = g_ref[2 * c + blk, rows, :].astype(F32) + praw[blk, rows, :].astype(F32)
            for k in range(GP):
                st[p, q, SP + k] = total[:, k * 128:(k + 1) * 128]

        @pl.when(i < 3)
        def _():
            for k in range(4):
                q = (pos2 + 1 + k) % 4
                c1(p, o, q).start()

    def c2(q):
        o = (pos2 - q + 4) % 4
        return rcopy(st.at[pos1, q], r2.at[o - 1], s2.at[o - 1], q2.at[o - 1], dev2(q))

    @pl.loop(1, 5)
    def _(k):
        q = (pos2 + k) % 4
        for o in (1, 2, 3):
            c1(pos1, o, q).wait_recv()
        st[pos1, q] = (st[pos1, q] + r1[0, q]) + (r1[1, q] + r1[2, q])

        @pl.when(k < 4)
        def _():
            c2(q).start()

    for o in (1, 2, 3):
        c2((pos2 + o) % 4).wait_recv()
    f3[pos2] = (st[pos1, pos2] + r2[0]) + (r2[1] + r2[2])

    def c3(o):
        return rcopy(f3.at[pos2], f3.at[pos2], s3.at[o - 1], q3.at[o - 1], dev2((pos2 - o + 4) % 4))

    def c4(o, q):
        return rcopy(
            f3.at[q, pl.ds(0, SP)], o_ref.at[c, pos1, q], s4.at[o - 1, q], q4.at[o - 1, q],
            dev1((pos1 - o + 4) % 4),
        )

    def cd_own(q):
        return rcopy(f3.at[q, pl.ds(0, SP)], o_ref.at[c, pos1, q], sd.at[0, q], qd.at[0, q], mate)

    def cd(o, q):
        p = (pos1 + o) % 4
        return rcopy(o_ref.at[c, p, q], o_ref.at[c, p, q], sd.at[o, q], qd.at[o, q], mate)

    def keep(q):
        return pltpu.make_async_copy(f3.at[q, pl.ds(0, SP)], o_ref.at[c, pos1, q], sl.at[0, q])

    def keep_g(q):
        return pltpu.make_async_copy(f3.at[q, pl.ds(SP, GP)], gq_ref.at[q], sl.at[1, q])

    for o in (2, 1, 3):
        c3(o).start()

    for k, o in ((0, 0), (1, 1), (3, 3), (2, 2)):
        q = (pos2 + k) % 4
        if k:
            rcopy(f3.at[pos2], f3.at[q], s3.at[o - 1], q3.at[o - 1], dev2(q)).wait_recv()
        for oo in (2, 1, 3):
            c4(oo, q).start()
        cd_own(q).start()
        keep(q).start()
        keep_g(q).start()

    for o in (1, 3, 2):
        for k in (0, 1, 3, 2):
            q = (pos2 + k) % 4
            p = (pos1 + o) % 4
            rcopy(
                f3.at[q, pl.ds(0, SP)], o_ref.at[c, p, q], s4.at[o - 1, q], q4.at[o - 1, q], dev1(p)
            ).wait_recv()
            cd(o, q).start()

    flags.wait()
    for a in accs:
        a.wait()
    for k in range(1, 4):
        p = (pos1 + k) % 4
        for q in range(4):
            c1(p, (pos1 - p + 4) % 4, q).wait_send()
        c2((pos2 + k) % 4).wait_send()
        c3(k).wait_send()
    for q in range(4):
        keep(q).wait()
        keep_g(q).wait()
        for o in (1, 2, 3):
            c4(o, q).wait_send()
        own = cd_own(q)
        own.wait_send()
        rcopy(f3.at[q, pl.ds(0, SP)], o_ref.at[1 - c, pos2, q], sd.at[0, q], qd.at[0, q], mate).wait_recv()
        for o in (1, 2, 3):
            cd(o, q).wait_send()
    for q in range(4):
        for o in (1, 2, 3):
            p = (pos2 + o) % 4
            rcopy(o_ref.at[1 - c, p, q], o_ref.at[1 - c, p, q], sd.at[o, q], qd.at[o, q], mate).wait_recv()


def call_stats(grads, refresh, acc):
    dma = pltpu.SemaphoreType.DMA
    return pl.pallas_call(
        stats_kernel,
        name="stats",
        out_shape=(
            jax.ShapeDtypeStruct((2, 4, 4, SP, 64, TL), F32),
            jax.ShapeDtypeStruct((4, GP, 64, TL), F32),
            jax.ShapeDtypeStruct((SLOTS, BS, BS), F32),
            jax.ShapeDtypeStruct((8, TL), jnp.int32),
        ),
        in_specs=[pl.BlockSpec(memory_space=pltpu.VMEM)] * 2 + [pl.BlockSpec(memory_space=pl.ANY)],
        out_specs=(pl.BlockSpec(memory_space=pl.ANY),) * 3 + (pl.BlockSpec(memory_space=pltpu.VMEM),),
        scratch_shapes=[
            pltpu.VMEM((2, BS, BS), BF16),
            pltpu.VMEM((4, 4, SP + GP, 64, TL), F32),
            pltpu.VMEM((3, 4, SP + GP, 64, TL), F32),
            pltpu.VMEM((3, SP + GP, 64, TL), F32),
            pltpu.VMEM((4, SP + GP, 64, TL), F32),
            dma((2,)), dma((2,)), dma((2, SLOTS)),
            dma((3, 4)), dma((3, 4)), dma((3,)), dma((3,)), dma((3,)), dma((3,)),
            dma((3, 4)), dma((3, 4)), dma((4, 4)), dma((4, 4)), dma((2, 4)),
        ],
        compiler_params=pltpu.CompilerParams(
            collective_id=1, has_side_effects=True, vmem_limit_bytes=40 << 20
        ),
    )(grads, refresh, acc)


def split(x):
    hi = x.astype(BF16)
    return hi, (x - hi.astype(F32)).astype(BF16)


def dot3(ah, al, bh, bl):
    return dot_nn(ah, bh) + (dot_nn(ah, bl) + dot_nn(al, bh))


def find_slot(owner_ref, place):
    block = jnp.int32(0)
    alive = jnp.int32(0)
    for k in range(KB):
        hit = (owner_ref[0, k] == place).astype(jnp.int32)
        block = block + k * hit
        alive = alive + hit
    return block, alive


def roots_kernel(
    owner_ref, rf_ref, prf_ref, st_ref, acc_ref, pacc_ref, old_ref,
    new_ref, lroot_ref, rroot_ref,
    flag, a_buf, s_buf, mf, tf, m1f, vf, mh, ml, th, tl, uh, ul, m1h, m1l, vh, vl, xbuf,
    sem_a, sem_s, sem_o, sem_r,
):
    d = lax.axis_index("dp")
    mate = d + 1 - 2 * (d % 2)
    for j in range(SLOTS):
        blk, alive = find_slot(owner_ref, d * SLOTS + j)
        fresh = alive * (rf_ref[0, j] >= 0).astype(jnp.int32)
        pblk, palive = find_slot(owner_ref, mate * SLOTS + j)
        pfresh = palive * (prf_ref[0, j] >= 0).astype(jnp.int32)
        flag[0, j], flag[0, 4 + j], flag[0, 2 + j] = blk, blk, pblk
        flag[1, j], flag[1, 4 + j], flag[1, 2 + j] = alive, alive, pfresh
        flag[2, j], flag[2, 2 + j] = fresh, pfresh

    flag[3, 0] = jnp.int32(0)

    def old(i):
        if 2 <= i < 4:
            return pacc_ref.at[i - 2]
        return acc_ref.at[i % 2, i // 4]

    for i in (0, 1, 2, 3, 4, 5):
        pltpu.make_async_copy(old(i), a_buf.at[i], sem_a.at[i]).start()
        lr = 0 if i < 2 else 1
        pltpu.make_async_copy(st_ref.at[flag[0, i], lr], s_buf.at[i], sem_s.at[i]).start()
    for j in range(SLOTS):
        @pl.when(flag[2, j] == 0)
        def _():
            pltpu.make_async_copy(old_ref.at[j, 0], lroot_ref.at[j], sem_r.at[j]).start()

    @pl.loop(0, 6)
    def _(i):
        pltpu.make_async_copy(acc_ref.at[0, 0], a_buf.at[i], sem_a.at[i]).wait()
        pltpu.make_async_copy(st_ref.at[0, 0], s_buf.at[i], sem_s.at[i]).wait()

        @pl.when(flag[1, i] == 1)
        def _():
            for t, (a, b) in enumerate(TILES):
                fresh = s_buf[i, t] * F32((1.0 - decay_rate) / 16384.0)
                ra, rb = pl.ds(a * TL, TL), pl.ds(b * TL, TL)
                a_buf[i, ra, rb] = decay_rate * a_buf[i, ra, rb] + fresh
                if a != b:
                    a_buf[i, rb, ra] = decay_rate * a_buf[i, rb, ra] + fresh.T

    outs = [pltpu.make_async_copy(a_buf.at[i], new_ref.at[i % 2, i // 4], sem_o.at[i]) for i in (0, 1, 4, 5)]
    for o in outs:
        o.start()

    half = BS // 2
    c4 = 625.0 / 256.0

    def each(fn):
        @pl.loop(0, 2)
        def _(h):
            fn(pl.ds(pl.multiple_of(h * half, half), half))

    def put(ref, hi, lo, rows, x):
        if ref is not None:
            ref[rows, :] = x
        hi[rows, :], lo[rows, :] = split(x)

    def mul(rows, ah, al, bh, bl):
        return dot3(ah[rows, :], al[rows, :], bh[...], bl[...])

    @pl.loop(0, 4)
    def _(t):
        @pl.when(flag[2, t] == 1)
        def _():
            a = a_buf[t]
            square = jnp.sum(a * a, axis=0, keepdims=True)
            mean = jnp.sum(square, axis=1, keepdims=True) * (1.0 / (BS * BS))
            scale = BS * jnp.sqrt(mean + epsilon)
            inverse = 1.0 / scale
            outer = 1.0 / jnp.sqrt(jnp.sqrt(scale))

            def start(rows):
                put(mf, mh, ml, rows, a_buf[t, rows, :] * inverse)

            each(start)

            def first(rows):
                q = mul(rows, mh, ml, mh, ml)
                put(tf, th, tl, rows, (q - 10.0 * mf[rows, :]) * (1.0 / 16.0))

            each(first)

            def second(rows):
                q = mul(rows, th, tl, th, tl)
                put(None, uh, ul, rows, (25.0 / 8.0) * tf[rows, :] + q)

            each(second)

            def third(rows):
                q = mul(rows, uh, ul, mh, ml)
                put(m1f, m1h, m1l, rows, c4 * mf[rows, :] + q)

            each(third)

            def fourth(rows):
                q = mul(rows, m1h, m1l, m1h, m1l)
                put(tf, th, tl, rows, (q - 10.0 * m1f[rows, :]) * (1.0 / 16.0))
                q = mul(rows, mh, ml, m1h, m1l)
                put(vf, vh, vl, rows, q * (1.0 / 16.0) - (5.0 / 16.0) * (mf[rows, :] + m1f[rows, :]))

            each(fourth)

            each(second)

            def seventh(rows):
                q = mul(rows, uh, ul, m1h, m1l)
                put(mf, mh, ml, rows, c4 * m1f[rows, :] + q)

            each(seventh)

            @pl.when(flag[3, 0] == 1)
            def _():
                pltpu.make_async_copy(xbuf, rroot_ref.at[0], sem_r.at[2]).wait()

            flag[3, 0] = jnp.int32(1)

            def last(rows):
                q = mul(rows, vh, vl, mh, ml)
                x = 1.25 * vf[rows, :] - (25.0 / 64.0) * mf[rows, :] - 0.25 * q
                r = lax.broadcasted_iota(jnp.int32, (half, BS), 0) + rows.start
                k = lax.broadcasted_iota(jnp.int32, (half, BS), 1)
                xbuf[rows, :] = outer * (x + jnp.where(r == k, F32(125.0 / 64.0), F32(0.0)))

            each(last)

            @pl.when(t < 2)
            def _():
                pltpu.make_async_copy(xbuf, lroot_ref.at[t % 2], sem_r.at[2]).start()

            @pl.when(t >= 2)
            def _():
                pltpu.make_async_copy(xbuf, rroot_ref.at[t % 2], sem_r.at[2]).start()

    @pl.when(flag[3, 0] == 1)
    def _():
        pltpu.make_async_copy(xbuf, rroot_ref.at[0], sem_r.at[2]).wait()
    for j in range(SLOTS):
        @pl.when(flag[2, j] == 0)
        def _():
            pltpu.make_async_copy(old_ref.at[j, 0], lroot_ref.at[j], sem_r.at[j]).wait()
    for o in outs:
        o.wait()


def call_roots(owner, refresh, prefresh, stats, acc, pacc, old):
    dma = pltpu.SemaphoreType.DMA
    anywhere = pl.BlockSpec(memory_space=pl.ANY)
    smem = pl.BlockSpec(memory_space=pltpu.SMEM)
    full = lambda dt: pltpu.VMEM((BS, BS), dt)
    return pl.pallas_call(
        roots_kernel,
        name="roots",
        out_shape=(
            jax.ShapeDtypeStruct((SLOTS, 2, BS, BS), F32),
            jax.ShapeDtypeStruct((SLOTS, BS, BS), F32),
            jax.ShapeDtypeStruct((SLOTS, BS, BS), F32),
        ),
        in_specs=[smem] * 3 + [anywhere] * 4,
        out_specs=(anywhere,) * 3,
        scratch_shapes=[
            pltpu.SMEM((4, 8), jnp.int32),
            pltpu.VMEM((6, BS, BS), F32),
            pltpu.VMEM((6, NT, TL, TL), F32),
        ]
        + [full(F32)] * 4 + [full(BF16)] * 10 + [full(F32)]
        + [dma((6,)), dma((6,)), dma((6,)), dma((3,))],
        compiler_params=pltpu.CompilerParams(vmem_limit_bytes=40 << 20),
        cost_estimate=pl.CostEstimate(flops=20 * 10**9, bytes_accessed=20 << 20, transcendentals=0),
    )(owner, refresh, prefresh, stats, acc, pacc, old)


def product_kernel(
    owner_ref, rf_ref, l_ref, r_ref, old_ref, *rest,
):
    g_refs = rest[:8]
    roots_ref, sq_ref, p_ref, flag, lbuf, rbuf, gbuf, gh, gl, sem = rest[8:]
    d = lax.axis_index("dp")
    c = d % 2
    pos1 = (d // 2) % 4 + c * (d // 8 - (d // 2) % 4)
    pos2 = d // 8 + c * ((d // 2) % 4 - d // 8)
    outs = []
    for j in range(SLOTS):
        blk, alive = find_slot(owner_ref, d * SLOTS + j)
        fresh = alive * (rf_ref[0, j] >= 0).astype(jnp.int32)
        flag[0, j], flag[1, j] = alive, fresh
        pltpu.make_async_copy(l_ref.at[j], lbuf.at[j], sem.at[j, 0]).start()

        @pl.when(fresh == 1)
        def _():
            pltpu.make_async_copy(r_ref.at[j], rbuf.at[j], sem.at[j, 1]).start()

        @pl.when(fresh == 0)
        def _():
            pltpu.make_async_copy(old_ref.at[j, 1], rbuf.at[j], sem.at[j, 1]).start()

        mine = (blk // 2 == c).astype(jnp.int32)
        for h in range(2):
            p = 2 * (blk % 2) + h
            o = lax.rem(p - jnp.where(mine == 1, pos1, pos2) + 4, 4)
            for i in range(8):
                @pl.when((o == i % 4) & (mine == 1 - i // 4))
                def _():
                    pltpu.make_async_copy(g_refs[i], gbuf.at[j, h], sem.at[j, 2 + h]).start()
    for j in range(SLOTS):
        pltpu.make_async_copy(l_ref.at[j], lbuf.at[j], sem.at[j, 0]).wait()
        outs.append(pltpu.make_async_copy(lbuf.at[j], roots_ref.at[j, 0], sem.at[j, 4]))
        outs[-1].start()
    sq_ref[...] = jnp.zeros_like(sq_ref)
    for j in range(SLOTS):
        pltpu.make_async_copy(r_ref.at[j], rbuf.at[j], sem.at[j, 1]).wait()
        for h in range(2):
            pltpu.make_async_copy(g_refs[0], gbuf.at[j, h], sem.at[j, 2 + h]).wait()
        outs.append(pltpu.make_async_copy(rbuf.at[j], roots_ref.at[j, 1], sem.at[j, 5]))
        outs[-1].start()

    @pl.loop(0, SLOTS)
    def _(j):
        @pl.when(flag[0, j] == 1)
        def _():
            for h in range(2):
                for q in range(4):
                    for k in range(4):
                        rows, cols = pl.ds(h * 256 + q * 64, 64), pl.ds(k * TL, TL)
                        gh[0, rows, cols], gl[0, rows, cols] = split(gbuf[j, h, q, k])
            gh[1], gl[1] = split(rbuf[j])

            @pl.loop(0, 2)
            def _(h):
                rows = pl.ds(pl.multiple_of(h * 256, 256), 256)
                ah, al = split(lbuf[j, rows, :])
                t = dot3(ah, al, gh[0], gl[0])
                th, tl = split(t)
                x = dot3(th, tl, gh[1], gl[1])
                p_ref[j, rows, :] = x
                part = jnp.sum((x * x).reshape(32, 8, BS), axis=0)
                sq_ref[...] += (part[:, :128] + part[:, 128:256]) + (part[:, 256:384] + part[:, 384:])

        @pl.when(flag[0, j] == 0)
        def _():
            p_ref[j] = jnp.zeros((BS, BS), F32)

    for o in outs:
        o.wait()


def call_product(owner, refresh, lroot, rroot, old, pieces):
    anywhere = pl.BlockSpec(memory_space=pl.ANY)
    smem = pl.BlockSpec(memory_space=pltpu.SMEM)
    vmem = pl.BlockSpec(memory_space=pltpu.VMEM)
    return pl.pallas_call(
        product_kernel,
        name="product",
        out_shape=(
            jax.ShapeDtypeStruct((SLOTS, 2, BS, BS), F32),
            jax.ShapeDtypeStruct((8, TL), F32),
            jax.ShapeDtypeStruct((SLOTS, BS, BS), F32),
        ),
        in_specs=[smem] * 2 + [anywhere] * 11,
        out_specs=(anywhere, vmem, vmem),
        scratch_shapes=[
            pltpu.SMEM((2, 2), jnp.int32),
            pltpu.VMEM((SLOTS, BS, BS), F32),
            pltpu.VMEM((SLOTS, BS, BS), F32),
            pltpu.VMEM((SLOTS, 2, 4, GP, 64, TL), F32),
            pltpu.VMEM((2, BS, BS), BF16),
            pltpu.VMEM((2, BS, BS), BF16),
            pltpu.SemaphoreType.DMA((SLOTS, 6)),
        ],
        compiler_params=pltpu.CompilerParams(vmem_limit_bytes=40 << 20),
    )(owner, refresh, lroot, rroot, old, *pieces)


def tail_kernel(
    n_mp, owner_ref, p_ref, sq_ref, up_ref,
    na, nb, pbuf, sb, r1, r2, f3,
    s_a, q_a, s_b, q_b, s_p, q_p, s_own, s1, q1, s2, q2, s3, q3, s4, q4, sd, qd, sl,
):
    y, z, c = coords()
    x = lax.axis_index("mp")
    pos1 = z + c * (y - z)
    pos2 = y + c * (z - y)
    plane = y * 4 + z
    pair = x * 2 + c

    def dev1(p):
        return at(y + c * (p - y), p + c * (z - p), c)

    def dev2(p):
        return at(p + c * (y - p), z + c * (p - z), c)

    mate = at(y, z, 1 - c)

    def in_plane(n):
        return {"dp": n * 2 + c}

    def in_pair(n):
        return {"dp": plane * 2 + n % 2, "mp": n // 2}

    barrier = pltpu.get_barrier_semaphore()
    for o in range(1, 16):
        pl.semaphore_signal(barrier, inc=1, device_id=in_plane((plane + o) % 16), device_id_type=MESH)
    for o in range(1, 2 * n_mp):
        pl.semaphore_signal(barrier, inc=1, device_id=in_pair((pair + o) % (2 * n_mp)), device_id_type=MESH)
    pl.semaphore_wait(barrier, 15 + 2 * n_mp - 1)

    def rcopy(src, dst, ss, rs, device):
        return pltpu.make_async_remote_copy(
            src_ref=src, dst_ref=dst, send_sem=ss, recv_sem=rs, device_id=device, device_id_type=MESH
        )

    na[plane] = sq_ref[...]

    def ca(o):
        return rcopy(na.at[plane], na.at[plane], s_a.at[o - 1], q_a.at[o - 1], in_plane((plane - o + 16) % 16))

    for o in range(1, 16):
        ca(o).start()

    def halves(j):
        return rcopy(
            p_ref.at[j, pl.ds((1 - c) * 256, 256)], pbuf.at[SLOTS + j], s_p.at[j], q_p.at[j], mate
        )

    def own(j):
        return pltpu.make_async_copy(p_ref.at[j, pl.ds(c * 256, 256)], pbuf.at[j], s_own.at[j])

    for j in range(SLOTS):
        halves(j).start()
        own(j).start()
    pbuf[2 * SLOTS] = jnp.zeros((256, BS), F32)
    for o in range(1, 16):
        ca(o).wait_recv()
    total = na[0]
    for n in range(1, 16):
        total = total + na[n]
    nb[pair] = total

    def cb(o):
        n = 2 * n_mp
        return rcopy(nb.at[pair], nb.at[pair], s_b.at[o - 1], q_b.at[o - 1], in_pair((pair - o + n) % n))

    for o in range(1, 2 * n_mp):
        cb(o).start()
    for j in range(SLOTS):
        halves(j).wait_recv()
        own(j).wait()
    for o in range(1, 2 * n_mp):
        cb(o).wait_recv()
    total = nb[0]
    for n in range(1, 2 * n_mp):
        total = total + nb[n]
    square = jnp.sum(jnp.sum(total, axis=0, keepdims=True), axis=1, keepdims=True)
    ratio = 1.0 / jnp.sqrt(square / float(KB * n_mp * BS * BS) + epsilon)

    base = (plane * 2 + c) * SLOTS
    mate_base = (plane * 2 + 1 - c) * SLOTS
    index = []
    for k in range(KB):
        place = owner_ref[0, k]
        n = jnp.int32(2 * SLOTS)
        for j in range(SLOTS):
            n = n + (j - 2 * SLOTS) * (place == base + j).astype(jnp.int32)
            n = n + (j - SLOTS) * (place == mate_base + j).astype(jnp.int32)
        index.append(n)

    def c1(p, o):
        return rcopy(sb.at[p], r1.at[o - 1], s1.at[o - 1], q1.at[o - 1], dev1(p))

    @pl.loop(0, 4)
    def _(i):
        p = (pos1 + jnp.where(i == 0, 2, jnp.where(i == 1, 1, jnp.where(i == 2, 3, 0)))) % 4
        o = (pos1 - p + 4) % 4
        for k in range(KB):
            for q in range(4):
                block = pbuf[index[k], pl.ds(p * 64 + q * 16, 16), :]
                sb[p, q, k] = (ratio * block).astype(BF16)

        @pl.when(i < 3)
        def _():
            c1(p, o).start()

    def c2(q):
        o = (pos2 - q + 4) % 4
        return rcopy(sb.at[pos1, q], r2.at[o - 1], s2.at[o - 1], q2.at[o - 1], dev2(q))

    for o in (1, 2, 3):
        c1(pos1, o).wait_recv()

    @pl.loop(1, 5)
    def _(k):
        q = (pos2 + k) % 4
        sb[pos1, q] = (sb[pos1, q] + r1[0, q]) + (r1[1, q] + r1[2, q])

        @pl.when(k < 4)
        def _():
            c2(q).start()

    for o in (1, 2, 3):
        c2((pos2 + o) % 4).wait_recv()
    f3[pos2] = (sb[pos1, pos2] + r2[0]) + (r2[1] + r2[2])

    def c3(o):
        return rcopy(f3.at[pos2], f3.at[pos2], s3.at[o - 1], q3.at[o - 1], dev2((pos2 - o + 4) % 4))

    def out(core, p, q):
        return up_ref.at[:, pl.ds(core * 256 + p * 64 + q * 16, 16), :]

    def c4(o, q):
        return rcopy(
            f3.at[q], out(c, pos1, q), s4.at[o - 1, q], q4.at[o - 1, q], dev1((pos1 - o + 4) % 4)
        )

    def cd_own(q):
        return rcopy(f3.at[q], out(c, pos1, q), sd.at[0, q], qd.at[0, q], mate)

    def cd(o, q):
        p = (pos1 + o) % 4
        return rcopy(out(c, p, q), out(c, p, q), sd.at[o, q], qd.at[o, q], mate)

    def keep(q):
        return pltpu.make_async_copy(f3.at[q], out(c, pos1, q), sl.at[q])

    for o in (2, 1, 3):
        c3(o).start()
    for k in (0, 1, 3, 2):
        q = (pos2 + k) % 4
        if k:
            rcopy(f3.at[pos2], f3.at[q], s3.at[k - 1], q3.at[k - 1], dev2(q)).wait_recv()
        for o in (2, 1, 3):
            c4(o, q).start()
        cd_own(q).start()
        keep(q).start()
    for o in (1, 3, 2):
        for k in (0, 1, 3, 2):
            q = (pos2 + k) % 4
            p = (pos1 + o) % 4
            rcopy(f3.at[q], out(c, p, q), s4.at[o - 1, q], q4.at[o - 1, q], dev1(p)).wait_recv()
            cd(o, q).start()

    for o in range(1, 16):
        ca(o).wait_send()
    for o in range(1, 2 * n_mp):
        cb(o).wait_send()
    for j in range(SLOTS):
        halves(j).wait_send()
    for k in range(1, 4):
        p = (pos1 + k) % 4
        c1(p, (pos1 - p + 4) % 4).wait_send()
        c2((pos2 + k) % 4).wait_send()
        c3(k).wait_send()
    for q in range(4):
        keep(q).wait()
        for o in (1, 2, 3):
            c4(o, q).wait_send()
            cd(o, q).wait_send()
        cd_own(q).wait_send()
        for o in range(4):
            p = (pos2 + o) % 4
            rcopy(f3.at[q], out(1 - c, p, q), sd.at[o, q], qd.at[o, q], mate).wait_recv()


def call_tail(owner, product, sq, n_mp):
    dma = pltpu.SemaphoreType.DMA
    return pl.pallas_call(
        functools.partial(tail_kernel, n_mp),
        name="tail",
        out_shape=jax.ShapeDtypeStruct((KB, BS, BS), BF16),
        in_specs=[pl.BlockSpec(memory_space=pltpu.SMEM)] + [pl.BlockSpec(memory_space=pltpu.VMEM)] * 2,
        out_specs=pl.BlockSpec(memory_space=pl.ANY),
        scratch_shapes=[
            pltpu.VMEM((16, 8, TL), F32),
            pltpu.VMEM((2 * n_mp, 8, TL), F32),
            pltpu.VMEM((2 * SLOTS + 1, 256, BS), F32),
            pltpu.VMEM((4, 4, KB, 16, BS), BF16),
            pltpu.VMEM((3, 4, KB, 16, BS), BF16),
            pltpu.VMEM((3, KB, 16, BS), BF16),
            pltpu.VMEM((4, KB, 16, BS), BF16),
            dma((15,)), dma((15,)), dma((2 * n_mp - 1,)), dma((2 * n_mp - 1,)),
            dma((SLOTS,)), dma((SLOTS,)), dma((SLOTS,)),
            dma((3,)), dma((3,)), dma((3,)), dma((3,)), dma((3,)), dma((3,)),
            dma((3, 4)), dma((3, 4)), dma((4, 4)), dma((4, 4)), dma((4,)),
        ],
        compiler_params=pltpu.CompilerParams(
            collective_id=2, has_side_effects=True, vmem_limit_bytes=40 << 20
        ),
    )(owner, product, sq)


def permute(x, n, place):
    pairs = []
    for d in range(n):
        y, z, c = d // 8, (d // 2) % 4, d % 2
        pairs.append((d, place(y, z, c)))
    return lax.ppermute(x, "dp", pairs)


def number(y, z, c):
    return ((y % 4) * 4 + z % 4) * 2 + c


def per_device(grads, block_owner, refresh_to, accum_old, roots_old):
    n_dp = lax.axis_size("dp")
    n_mp = lax.axis_size("mp")
    acc, old = accum_old[0, 0], roots_old[0, 0]
    refresh = jnp.pad(refresh_to[0], ((0, 7), (0, TL - SLOTS)))
    stats, gq, pacc, prefresh = call_stats(grads[0], refresh, acc)
    stats = stats.reshape(KB, 2, NT, TL, TL)
    new_accum, lroot, rroot = call_roots(block_owner, refresh, prefresh, stats, acc, pacc, old)
    line = [gq]
    for o in (1, 2, 3):
        line.append(permute(gq, n_dp, lambda y, z, c: number(y - o * c, z - o * (1 - c), c)))
    swap = lambda y, z, c: number(y, z, 1 - c)
    pieces = line + [permute(x, n_dp, swap) for x in line]
    rroot = permute(rroot, n_dp, swap)
    roots, sq, product = call_product(block_owner, refresh, lroot, rroot, old, pieces)

    update = call_tail(block_owner, product, sq, n_mp)
    return (new_accum[None, None], roots[None, None], update)


def solution(mesh):
    in_specs = (
        P("dp", "mp", None, None),
        P("mp", None),
        P("dp", "mp", None),
        P("dp", "mp", None, None, None, None),
        P("dp", "mp", None, None, None, None),
    )
    out_specs = (
        P("dp", "mp", None, None, None, None),
        P("dp", "mp", None, None, None, None),
        P("mp", None, None),
    )
    return jax.shard_map(
        per_device, mesh=mesh, in_specs=in_specs, out_specs=out_specs, check_vma=False
    )
```

```python
import functools

import jax
import jax.numpy as jnp
from jax import lax
from jax.experimental import pallas as pl
from jax.experimental.pallas import tpu as pltpu
from jax.sharding import PartitionSpec as P

MESH = pl.DeviceIdType.MESH
F32 = jnp.float32
BF16 = jnp.bfloat16

BS = 512
KB = 4
SLOTS = 2
TL = 128
TILES = [(a, b) for a in range(4) for b in range(a, 4)]
NT = len(TILES)
SP = 5
GP = 4
decay_rate = 0.8
epsilon = 1e-06


def coords():
    d = lax.axis_index("dp")
    return d // 8, (d // 2) % 4, d % 2


def at(y, z, c):
    return {"dp": (y * 4 + z) * 2 + c}


def dot_nt(a, b):
    return lax.dot_general(a, b, (((1,), (1,)), ((), ())), preferred_element_type=F32)


def dot_tn(a, b):
    return lax.dot_general(a, b, (((0,), (0,)), ((), ())), preferred_element_type=F32)


def dot_nn(a, b):
    return lax.dot_general(a, b, (((1,), (0,)), ((), ())), preferred_element_type=F32)


W0 = 25 / 16
W1 = -5 / 16 - 3125 / 4096
W2 = 3125 / 4096
W3 = -1250 / 4096
W4 = 250 / 4096
W5 = -25 / 4096
W6 = 1 / 4096


def split(x):
    hi = x.astype(BF16)
    return hi, (x - hi.astype(F32)).astype(BF16)


def dot3(ah, al, bh, bl):
    return dot_nn(ah, bh) + (dot_nn(ah, bl) + dot_nn(al, bh))


def find_slot(owner_ref, place):
    block = jnp.int32(0)
    alive = jnp.int32(0)
    for k in range(KB):
        hit = (owner_ref[0, k] == place).astype(jnp.int32)
        block = jnp.where(hit == 1, k, block)
        alive = jnp.maximum(alive, hit)
    return block, alive


def inverse_root(a_ref, store, bufs):
    mf, m2f, nf, zf, mh, ml, ah, al, bh, bl, ch, cl = bufs
    a = a_ref[...]
    square = jnp.sum(a * a, axis=0, keepdims=True)
    mean = jnp.sum(square, axis=1, keepdims=True) * (1.0 / (BS * BS))
    scale = BS * jnp.sqrt(mean + epsilon)
    inverse = 1.0 / scale
    outer = 1.0 / jnp.sqrt(jnp.sqrt(scale))
    lo, up = slice(0, 256), slice(256, 512)

    def put(f, h, l, v, rows, cols):
        for x, r, k in ((v, rows, cols),) if rows is cols else ((v, rows, cols), (v.T, cols, rows)):
            hi = x.astype(BF16)
            h[r, k] = hi
            if f is not None:
                f[r, k] = x
            if l is not None:
                l[r, k] = (x - hi.astype(F32)).astype(BF16)

    def multiply(lh, ll, rh, rl, then):
        for rows, cols in ((lo, lo), (lo, up), (up, up)):
            if rl is None:
                q = dot_nn(lh[rows, :], rh[:, cols])
            else:
                q = dot3(lh[rows, :], ll[rows, :], rh[:, cols], rl[:, cols])
            then(q, rows, cols)

    for rows in (lo, up):
        x = a_ref[rows, :] * inverse
        mf[rows, :] = x
        mh[rows, :], ml[rows, :] = split(x)
    multiply(mh, ml, mh, ml, lambda q, r, k: put(m2f, ah, al, q, r, k))

    def third(q, r, k):
        m, m2 = mf[r, k], m2f[r, k]
        nf[r, k] = W1 * m + W2 * m2 + W3 * q
        put(None, bh, None, q, r, k)
        put(None, ch, None, W4 * m + W5 * m2 + W6 * q, r, k)

    multiply(ah, al, mh, ml, third)
    multiply(ch, None, bh, None, lambda q, r, k: put(nf, ah, al, nf[r, k] + q, r, k))
    multiply(ah, al, mh, ml, lambda q, r, k: put(zf, ch, cl, W0 * mf[r, k] + q, r, k))
    multiply(ah, al, ah, al, lambda q, r, k: put(m2f, bh, bl, (2 * W0) * nf[r, k] + q, r, k))
    multiply(bh, bl, bh, bl, lambda q, r, k: put(None, ah, al, (2 * W0 * W0) * m2f[r, k] + q, r, k))

    def last(q, r, k):
        x = 1.25 * nf[r, k] - (0.25 * W0**4) * zf[r, k] - 0.25 * q
        if r is k:
            rows = lax.broadcasted_iota(jnp.int32, (256, 256), 0)
            cols = lax.broadcasted_iota(jnp.int32, (256, 256), 1)
            x = x + jnp.where(rows == cols, F32(1.25 * W0), F32(0.0))
        x = outer * x
        store(r, k, x)
        if r is not k:
            store(k, r, x.T)

    multiply(ah, al, ch, cl, last)


class Spread:
    def __init__(self, st, r1, r2, every, sems, place):
        self.st, self.r1, self.r2, self.all = st, r1, r2, every
        self.s1, self.q1, self.s2, self.q2, self.s3, self.q3, self.s4, self.q4, self.sd, self.qd = sems
        self.c, self.pos1, self.pos2, self.dev1, self.dev2, self.mate = place

    def c1(self, p, q):
        o = (self.pos1 - p + 4) % 4 - 1
        return rcopy(
            self.st.at[p, q], self.r1.at[o, q], self.s1.at[o, q], self.q1.at[o, q], self.dev1(p)
        )

    def c2(self, q):
        o = (self.pos2 - q + 4) % 4 - 1
        return rcopy(self.st.at[self.pos1, q], self.r2.at[o], self.s2.at[o], self.q2.at[o], self.dev2(q))

    def c3(self, o, q, device):
        ref = self.all.at[self.c, self.pos1, q]
        return rcopy(ref, ref, self.s3.at[o - 1], self.q3.at[o - 1], device)

    def c4(self, o, p, q, device):
        ref = self.all.at[self.c, p, q]
        return rcopy(ref, ref, self.s4.at[o - 1, q], self.q4.at[o - 1, q], device)

    def cd(self, core, p, q):
        ref = self.all.at[core, p, q]
        return rcopy(ref, ref, self.sd.at[p, q], self.qd.at[p, q], self.mate)

    def send1(self, p):
        for k in range(4):
            self.c1(p, (self.pos2 + 1 + k) % 4).start()

    def add1(self):
        for k in range(1, 5):
            q = (self.pos2 + k) % 4
            for o in (1, 2, 3):
                self.c1((self.pos1 + o) % 4, q).wait_recv()
            self.st[self.pos1, q] = (self.st[self.pos1, q] + self.r1[0, q]) + (self.r1[1, q] + self.r1[2, q])
            if k < 4:
                self.c2(q).start()

    def add2(self):
        for o in (1, 2, 3):
            self.c2((self.pos2 + o) % 4).wait_recv()
        self.all[self.c, self.pos1, self.pos2] = (self.st[self.pos1, self.pos2] + self.r2[0]) + (
            self.r2[1] + self.r2[2]
        )
        for o in (2, 1, 3):
            self.c3(o, self.pos2, self.dev2((self.pos2 - o + 4) % 4)).start()

    def gather2(self):
        for k in (0, 1, 3, 2):
            q = (self.pos2 + k) % 4
            if k:
                self.c3(k, q, self.dev2(q)).wait_recv()
            for o in (2, 1, 3):
                self.c4(o, self.pos1, q, self.dev1((self.pos1 - o + 4) % 4)).start()
            self.cd(self.c, self.pos1, q).start()

    def gather1(self):
        for o in (1, 3, 2):
            p = (self.pos1 + o) % 4
            for k in (0, 1, 3, 2):
                q = (self.pos2 + k) % 4
                self.c4(o, p, q, self.dev1(p)).wait_recv()
                self.cd(self.c, p, q).start()

    def from_mate(self):
        for p in range(4):
            for q in range(4):
                self.cd(1 - self.c, p, q).wait_recv()

    def sent(self):
        for o in (1, 2, 3):
            for q in range(4):
                self.c1((self.pos1 + o) % 4, q).wait_send()
                self.c4(o, self.pos1, q, self.dev1((self.pos1 - o + 4) % 4)).wait_send()
            self.c2((self.pos2 + o) % 4).wait_send()
            self.c3(o, self.pos2, self.dev2((self.pos2 - o + 4) % 4)).wait_send()
        for p in range(4):
            for q in range(4):
                self.cd(self.c, p, q).wait_send()

    @staticmethod
    def sems():
        dma = pltpu.SemaphoreType.DMA
        return [dma((3, 4)), dma((3, 4)), dma((3,)), dma((3,)), dma((3,)), dma((3,)),
                dma((3, 4)), dma((3, 4)), dma((4, 4)), dma((4, 4))]


def rcopy(src, dst, ss, rs, device):
    return pltpu.make_async_remote_copy(
        src_ref=src, dst_ref=dst, send_sem=ss, recv_sem=rs, device_id=device, device_id_type=MESH
    )


def main_kernel(owner_ref, g_ref, acc_ref, new_ref, gs_ref, lroot_ref, rroot_ref, *scratch):
    (praw, sts, sr1, sr2, sall, stg, gr1, gr2, pacc, am, rsend), scratch = scratch[:11], scratch[11:]
    bufs, scratch = scratch[:12], scratch[12:]
    ssem, gsem, (s_raw, s_acc, s_old, s_root) = scratch[:10], scratch[10:20], scratch[20:]
    y, z, c = coords()
    pos1 = z + c * (y - z)
    pos2 = y + c * (z - y)

    def dev1(p):
        return at(y + c * (p - y), p + c * (z - p), c)

    def dev2(p):
        return at(p + c * (y - p), z + c * (p - z), c)

    mate = at(y, z, 1 - c)
    place = (c, pos1, pos2, dev1, dev2, mate)
    stat = Spread(sts, sr1, sr2, sall, ssem, place)
    gsum = Spread(stg, gr1, gr2, gs_ref, gsem, place)

    barrier = pltpu.get_barrier_semaphore()
    for o in (1, 2, 3):
        pl.semaphore_signal(barrier, inc=1, device_id=dev1((pos1 + o) % 4), device_id_type=MESH)
        pl.semaphore_signal(barrier, inc=1, device_id=dev2((pos2 + o) % 4), device_id_type=MESH)
    pl.semaphore_signal(barrier, inc=1, device_id=mate, device_id_type=MESH)
    pl.semaphore_wait(barrier, 7)

    raw = rcopy(g_ref.at[pl.ds(2 * (1 - c), 2)], praw, s_raw.at[0], s_raw.at[1], mate)
    raw.start()
    accs = [rcopy(acc_ref.at[j, 1], pacc.at[j], s_acc.at[0, j], s_acc.at[1, j], mate) for j in range(SLOTS)]
    olds = [pltpu.make_async_copy(acc_ref.at[j], new_ref.at[j], s_old.at[j]) for j in range(SLOTS)]
    raw.wait()
    for a in accs + olds:
        a.start()

    def put(p, a, b, block):
        t = TILES.index((a, b))
        for half in range(2):
            h = 2 * t + half
            sts[p, h // SP, h % SP] = block[half * 64:(half + 1) * 64]

    def quadrants(p, quad):
        x = quad(0, 0)
        put(p, 0, 0, x[:128, :128])
        put(p, 0, 1, x[:128, 128:])
        put(p, 1, 1, x[128:, 128:])
        x = quad(0, 1)
        put(p, 0, 2, x[:128, :128])
        put(p, 0, 3, x[:128, 128:])
        put(p, 1, 2, x[128:, :128])
        put(p, 1, 3, x[128:, 128:])
        x = quad(1, 1)
        put(p, 2, 2, x[:128, :128])
        put(p, 2, 3, x[:128, 128:])
        put(p, 3, 3, x[128:, 128:])

    @pl.loop(0, 4)
    def _(i):
        p = (pos1 + jnp.where(i == 0, 2, jnp.where(i == 1, 1, jnp.where(i == 2, 3, 0)))) % 4
        blk = p // 2

        @pl.when(p % 2 == 0)
        def _():
            quadrants(
                p,
                lambda a, b: dot_nt(
                    g_ref[2 * c + blk, a * 256:(a + 1) * 256, :], g_ref[2 * c + blk, b * 256:(b + 1) * 256, :]
                )
                + dot_nt(praw[blk, a * 256:(a + 1) * 256, :], praw[blk, b * 256:(b + 1) * 256, :]),
            )

        @pl.when(p % 2 == 1)
        def _():
            quadrants(
                p,
                lambda a, b: dot_tn(
                    g_ref[2 * c + blk, :, a * 256:(a + 1) * 256], g_ref[2 * c + blk, :, b * 256:(b + 1) * 256]
                )
                + dot_tn(praw[blk, :, a * 256:(a + 1) * 256], praw[blk, :, b * 256:(b + 1) * 256]),
            )

        @pl.when(i < 3)
        def _():
            stat.send1(p)

    @pl.loop(0, 4)
    def _(i):
        p = (pos1 + jnp.where(i == 0, 2, jnp.where(i == 1, 1, jnp.where(i == 2, 3, 0)))) % 4
        for q in range(4):
            rows = pl.ds((p % 2) * 256 + q * 64, 64)
            total = g_ref[2 * c + p // 2, rows, :].astype(F32) + praw[p // 2, rows, :].astype(F32)
            for k in range(GP):
                stg[p, q, k] = total[:, k * 128:(k + 1) * 128]

        @pl.when(i < 3)
        def _():
            gsum.send1(p)

    stat.add1()
    stat.add2()
    stat.gather2()
    gsum.add1()
    stat.gather1()
    gsum.add2()
    for a in accs:
        a.wait()
    for a in olds:
        a.wait()
    stat.from_mate()

    d = lax.axis_index("dp")
    other = d + 1 - 2 * c

    def blend(dst, src, blk, alive, lr):
        keep = jnp.where(alive == 1, F32(decay_rate), F32(1.0))
        take = jnp.where(alive == 1, F32((1.0 - decay_rate) / 16384.0), F32(0.0))
        for t, (a, b) in enumerate(TILES):
            for half in range(2):
                h = 2 * t + half
                fresh = take * sall[blk // 2, 2 * (blk % 2) + lr, h // SP, h % SP]
                ra, rb = pl.ds(a * TL + half * 64, 64), pl.ds(b * TL, TL)
                dst[ra, rb] = keep * src[ra, rb] + fresh
                if a != b:
                    dst[rb, ra] = keep * src[rb, ra] + fresh.T

    def root(j):
        return rcopy(rsend.at[j], rroot_ref.at[j], s_root.at[0, j], s_root.at[1, j], mate)

    @pl.loop(0, 4)
    def _(t):
        j = t % 2

        @pl.when(t < 2)
        def _():
            blk, _ = find_slot(owner_ref, other * SLOTS + j)
            blend(am, pacc.at[j], blk, jnp.int32(1), 1)

        @pl.when(t >= 2)
        def _():
            blk, alive = find_slot(owner_ref, d * SLOTS + j)
            blend(new_ref.at[j, 0], new_ref.at[j, 0], blk, alive, 0)
            blend(new_ref.at[j, 1], new_ref.at[j, 1], blk, alive, 1)
            am[...] = new_ref[j, 0]

        def store(rows, cols, x):
            @pl.when(t < 2)
            def _():
                rsend[j, rows, cols] = x

            @pl.when(t >= 2)
            def _():
                lroot_ref[j, rows, cols] = x

        inverse_root(am, store, bufs)

        @pl.when(t < 2)
        def _():
            root(j).start()

        @pl.when(t == 0)
        def _():
            gsum.gather2()

        @pl.when(t == 2)
        def _():
            gsum.gather1()

    for j in range(SLOTS):
        root(j).wait()
    gsum.from_mate()
    stat.sent()
    gsum.sent()


def call_main(owner, grads, acc):
    dma = pltpu.SemaphoreType.DMA
    vmem = pl.BlockSpec(memory_space=pltpu.VMEM)
    square = lambda n, dt: pltpu.VMEM(n + (BS, BS), dt)
    return pl.pallas_call(
        main_kernel,
        name="main",
        out_shape=(
            jax.ShapeDtypeStruct((SLOTS, 2, BS, BS), F32),
            jax.ShapeDtypeStruct((2, 4, 4, GP, 64, TL), F32),
            jax.ShapeDtypeStruct((SLOTS, BS, BS), F32),
            jax.ShapeDtypeStruct((SLOTS, BS, BS), F32),
        ),
        in_specs=[pl.BlockSpec(memory_space=pltpu.SMEM), vmem, pl.BlockSpec(memory_space=pl.ANY)],
        out_specs=(vmem,) * 4,
        scratch_shapes=[
            square((2,), BF16),
            pltpu.VMEM((4, 4, SP, 64, TL), F32),
            pltpu.VMEM((3, 4, SP, 64, TL), F32),
            pltpu.VMEM((3, SP, 64, TL), F32),
            pltpu.VMEM((2, 4, 4, SP, 64, TL), F32),
            pltpu.VMEM((4, 4, GP, 64, TL), F32),
            pltpu.VMEM((3, 4, GP, 64, TL), F32),
            pltpu.VMEM((3, GP, 64, TL), F32),
            square((SLOTS,), F32),
            square((), F32),
            square((SLOTS,), F32),
        ]
        + [square((), F32)] * 4 + [square((), BF16)] * 8
        + Spread.sems() + Spread.sems()
        + [dma((2,)), dma((2, SLOTS)), dma((SLOTS,)), dma((2, SLOTS))],
        compiler_params=pltpu.CompilerParams(
            collective_id=1, has_side_effects=True, vmem_limit_bytes=44 << 20
        ),
    )(owner, grads, acc)


def product_kernel(
    owner_ref, rf_ref, new_ref, gs_ref, l_ref, r_ref, old_ref,
    accum_ref, roots_ref, sq_ref, p_ref,
    flag, buf, gh, gl, sem,
):
    d = lax.axis_index("dp")
    accum = pltpu.make_async_copy(new_ref, accum_ref, sem.at[4])
    accum.start()
    for j in range(SLOTS):
        blk, alive = find_slot(owner_ref, d * SLOTS + j)
        fresh = alive * (rf_ref[0, j] >= 0).astype(jnp.int32)
        flag[0, j], flag[1, j], flag[2, j] = blk, alive, fresh
        for i, ref in enumerate((l_ref, r_ref)):
            @pl.when(fresh == 1)
            def _():
                pltpu.make_async_copy(ref.at[j], buf.at[j, i], sem.at[2 * j + i]).start()

            @pl.when(fresh == 0)
            def _():
                pltpu.make_async_copy(old_ref.at[j, i], buf.at[j, i], sem.at[2 * j + i]).start()
    sq_ref[...] = jnp.zeros_like(sq_ref)
    outs = []
    for j in range(SLOTS):
        for i in range(2):
            pltpu.make_async_copy(old_ref.at[j, i], buf.at[j, i], sem.at[2 * j + i]).wait()
        outs.append(pltpu.make_async_copy(buf.at[j], roots_ref.at[j], sem.at[5 + j]))
        outs[-1].start()

    @pl.loop(0, SLOTS)
    def _(j):
        @pl.when(flag[1, j] == 1)
        def _():
            blk = flag[0, j]
            for h in range(2):
                for q in range(4):
                    for k in range(4):
                        rows, cols = pl.ds(h * 256 + q * 64, 64), pl.ds(k * TL, TL)
                        gh[0, rows, cols], gl[0, rows, cols] = split(
                            gs_ref[blk // 2, 2 * (blk % 2) + h, q, k]
                        )
            gh[1], gl[1] = split(buf[j, 1])

            @pl.loop(0, 2)
            def _(h):
                rows = pl.ds(pl.multiple_of(h * 256, 256), 256)
                ah, al = split(buf[j, 0, rows, :])
                t = dot3(ah, al, gh[0], gl[0])
                th, tl = split(t)
                x = dot3(th, tl, gh[1], gl[1])
                p_ref[j, rows, :] = x
                part = jnp.sum((x * x).reshape(32, 8, BS), axis=0)
                sq_ref[...] += (part[:, :128] + part[:, 128:256]) + (part[:, 256:384] + part[:, 384:])

        @pl.when(flag[1, j] == 0)
        def _():
            p_ref[j] = jnp.zeros((BS, BS), F32)

    accum.wait()
    for o in outs:
        o.wait()


def call_product(owner, refresh, new, gs, lroot, rroot, old):
    anywhere = pl.BlockSpec(memory_space=pl.ANY)
    smem = pl.BlockSpec(memory_space=pltpu.SMEM)
    vmem = pl.BlockSpec(memory_space=pltpu.VMEM)
    return pl.pallas_call(
        product_kernel,
        name="product",
        out_shape=(
            jax.ShapeDtypeStruct((SLOTS, 2, BS, BS), F32),
            jax.ShapeDtypeStruct((SLOTS, 2, BS, BS), F32),
            jax.ShapeDtypeStruct((8, TL), F32),
            jax.ShapeDtypeStruct((SLOTS, BS, BS), F32),
        ),
        in_specs=[smem] * 2 + [vmem] * 4 + [anywhere],
        out_specs=(anywhere, anywhere, vmem, vmem),
        scratch_shapes=[
            pltpu.SMEM((3, SLOTS), jnp.int32),
            pltpu.VMEM((SLOTS, 2, BS, BS), F32),
            pltpu.VMEM((2, BS, BS), BF16),
            pltpu.VMEM((2, BS, BS), BF16),
            pltpu.SemaphoreType.DMA((7,)),
        ],
        compiler_params=pltpu.CompilerParams(vmem_limit_bytes=40 << 20),
    )(owner, refresh, new, gs, lroot, rroot, old)


def tail_kernel(
    n_mp, owner_ref, p_ref, sq_ref, up_ref,
    na, nb, pbuf, sb, r1, r2, f3,
    s_a, q_a, s_b, q_b, s_p, q_p, s_own, s1, q1, s2, q2, s3, q3, s4, q4, sd, qd, sl,
):
    y, z, c = coords()
    x = lax.axis_index("mp")
    pos1 = z + c * (y - z)
    pos2 = y + c * (z - y)
    plane = y * 4 + z
    pair = x * 2 + c

    def dev1(p):
        return at(y + c * (p - y), p + c * (z - p), c)

    def dev2(p):
        return at(p + c * (y - p), z + c * (p - z), c)

    mate = at(y, z, 1 - c)

    def in_plane(n):
        return {"dp": n * 2 + c}

    def in_pair(n):
        return {"dp": plane * 2 + n % 2, "mp": n // 2}

    barrier = pltpu.get_barrier_semaphore()
    for o in range(1, 16):
        pl.semaphore_signal(barrier, inc=1, device_id=in_plane((plane + o) % 16), device_id_type=MESH)
    for o in range(1, 2 * n_mp):
        pl.semaphore_signal(barrier, inc=1, device_id=in_pair((pair + o) % (2 * n_mp)), device_id_type=MESH)
    pl.semaphore_wait(barrier, 15 + 2 * n_mp - 1)

    na[plane] = sq_ref[...]

    def ca(o):
        return rcopy(na.at[plane], na.at[plane], s_a.at[o - 1], q_a.at[o - 1], in_plane((plane - o + 16) % 16))

    for o in range(1, 16):
        ca(o).start()

    def halves(j):
        return rcopy(
            p_ref.at[j, pl.ds((1 - c) * 256, 256)], pbuf.at[SLOTS + j], s_p.at[j], q_p.at[j], mate
        )

    def own(j):
        return pltpu.make_async_copy(p_ref.at[j, pl.ds(c * 256, 256)], pbuf.at[j], s_own.at[j])

    for j in range(SLOTS):
        halves(j).start()
        own(j).start()
    pbuf[2 * SLOTS] = jnp.zeros((256, BS), F32)
    for o in range(1, 16):
        ca(o).wait_recv()
    total = na[0]
    for n in range(1, 16):
        total = total + na[n]
    nb[pair] = total

    def cb(o):
        n = 2 * n_mp
        return rcopy(nb.at[pair], nb.at[pair], s_b.at[o - 1], q_b.at[o - 1], in_pair((pair - o + n) % n))

    for o in range(1, 2 * n_mp):
        cb(o).start()
    for j in range(SLOTS):
        halves(j).wait_recv()
        own(j).wait()
    for o in range(1, 2 * n_mp):
        cb(o).wait_recv()
    total = nb[0]
    for n in range(1, 2 * n_mp):
        total = total + nb[n]
    square = jnp.sum(jnp.sum(total, axis=0, keepdims=True), axis=1, keepdims=True)
    ratio = 1.0 / jnp.sqrt(square / float(KB * n_mp * BS * BS) + epsilon)

    base = (plane * 2 + c) * SLOTS
    mate_base = (plane * 2 + 1 - c) * SLOTS
    index = []
    for k in range(KB):
        place = owner_ref[0, k]
        n = jnp.int32(2 * SLOTS)
        for j in range(SLOTS):
            n = n + (j - 2 * SLOTS) * (place == base + j).astype(jnp.int32)
            n = n + (j - SLOTS) * (place == mate_base + j).astype(jnp.int32)
        index.append(n)

    def c1(p, o):
        return rcopy(sb.at[p], r1.at[o - 1], s1.at[o - 1], q1.at[o - 1], dev1(p))

    @pl.loop(0, 4)
    def _(i):
        p = (pos1 + jnp.where(i == 0, 2, jnp.where(i == 1, 1, jnp.where(i == 2, 3, 0)))) % 4
        o = (pos1 - p + 4) % 4
        for k in range(KB):
            for q in range(4):
                block = pbuf[index[k], pl.ds(p * 64 + q * 16, 16), :]
                sb[p, q, k] = (ratio * block).astype(BF16)

        @pl.when(i < 3)
        def _():
            c1(p, o).start()

    def c2(q):
        o = (pos2 - q + 4) % 4
        return rcopy(sb.at[pos1, q], r2.at[o - 1], s2.at[o - 1], q2.at[o - 1], dev2(q))

    for o in (1, 2, 3):
        c1(pos1, o).wait_recv()

    @pl.loop(1, 5)
    def _(k):
        q = (pos2 + k) % 4
        sb[pos1, q] = (sb[pos1, q] + r1[0, q]) + (r1[1, q] + r1[2, q])

        @pl.when(k < 4)
        def _():
            c2(q).start()

    for o in (1, 2, 3):
        c2((pos2 + o) % 4).wait_recv()
    f3[pos2] = (sb[pos1, pos2] + r2[0]) + (r2[1] + r2[2])

    def c3(o):
        return rcopy(f3.at[pos2], f3.at[pos2], s3.at[o - 1], q3.at[o - 1], dev2((pos2 - o + 4) % 4))

    def out(core, p, q):
        return up_ref.at[:, pl.ds(core * 256 + p * 64 + q * 16, 16), :]

    def c4(o, q):
        return rcopy(
            f3.at[q], out(c, pos1, q), s4.at[o - 1, q], q4.at[o - 1, q], dev1((pos1 - o + 4) % 4)
        )

    def cd_own(q):
        return rcopy(f3.at[q], out(c, pos1, q), sd.at[0, q], qd.at[0, q], mate)

    def cd(o, q):
        p = (pos1 + o) % 4
        return rcopy(out(c, p, q), out(c, p, q), sd.at[o, q], qd.at[o, q], mate)

    def keep(q):
        return pltpu.make_async_copy(f3.at[q], out(c, pos1, q), sl.at[q])

    for o in (2, 1, 3):
        c3(o).start()
    for k in (0, 1, 3, 2):
        q = (pos2 + k) % 4
        if k:
            rcopy(f3.at[pos2], f3.at[q], s3.at[k - 1], q3.at[k - 1], dev2(q)).wait_recv()
        for o in (2, 1, 3):
            c4(o, q).start()
        cd_own(q).start()
        keep(q).start()
    for o in (1, 3, 2):
        for k in (0, 1, 3, 2):
            q = (pos2 + k) % 4
            p = (pos1 + o) % 4
            rcopy(f3.at[q], out(c, p, q), s4.at[o - 1, q], q4.at[o - 1, q], dev1(p)).wait_recv()
            cd(o, q).start()

    for o in range(1, 16):
        ca(o).wait_send()
    for o in range(1, 2 * n_mp):
        cb(o).wait_send()
    for j in range(SLOTS):
        halves(j).wait_send()
    for k in range(1, 4):
        p = (pos1 + k) % 4
        c1(p, (pos1 - p + 4) % 4).wait_send()
        c2((pos2 + k) % 4).wait_send()
        c3(k).wait_send()
    for q in range(4):
        keep(q).wait()
        for o in (1, 2, 3):
            c4(o, q).wait_send()
            cd(o, q).wait_send()
        cd_own(q).wait_send()
        for o in range(4):
            p = (pos2 + o) % 4
            rcopy(f3.at[q], out(1 - c, p, q), sd.at[o, q], qd.at[o, q], mate).wait_recv()


def call_tail(owner, product, sq, n_mp):
    dma = pltpu.SemaphoreType.DMA
    return pl.pallas_call(
        functools.partial(tail_kernel, n_mp),
        name="tail",
        out_shape=jax.ShapeDtypeStruct((KB, BS, BS), BF16),
        in_specs=[pl.BlockSpec(memory_space=pltpu.SMEM)] + [pl.BlockSpec(memory_space=pltpu.VMEM)] * 2,
        out_specs=pl.BlockSpec(memory_space=pl.ANY),
        scratch_shapes=[
            pltpu.VMEM((16, 8, TL), F32),
            pltpu.VMEM((2 * n_mp, 8, TL), F32),
            pltpu.VMEM((2 * SLOTS + 1, 256, BS), F32),
            pltpu.VMEM((4, 4, KB, 16, BS), BF16),
            pltpu.VMEM((3, 4, KB, 16, BS), BF16),
            pltpu.VMEM((3, KB, 16, BS), BF16),
            pltpu.VMEM((4, KB, 16, BS), BF16),
            dma((15,)), dma((15,)), dma((2 * n_mp - 1,)), dma((2 * n_mp - 1,)),
            dma((SLOTS,)), dma((SLOTS,)), dma((SLOTS,)),
            dma((3,)), dma((3,)), dma((3,)), dma((3,)), dma((3,)), dma((3,)),
            dma((3, 4)), dma((3, 4)), dma((4, 4)), dma((4, 4)), dma((4,)),
        ],
        compiler_params=pltpu.CompilerParams(
            collective_id=2, has_side_effects=True, vmem_limit_bytes=40 << 20
        ),
    )(owner, product, sq)


def per_device(grads, block_owner, refresh_to, accum_old, roots_old):
    n_mp = lax.axis_size("mp")
    new, gs, lroot, rroot = call_main(block_owner, grads[0], accum_old[0, 0])
    new_accum, roots, sq, product = call_product(
        block_owner, refresh_to[0], new, gs, lroot, rroot, roots_old[0, 0]
    )
    update = call_tail(block_owner, product, sq, n_mp)
    return (new_accum[None, None], roots[None, None], update)


def solution(mesh):
    in_specs = (
        P("dp", "mp", None, None),
        P("mp", None),
        P("dp", "mp", None),
        P("dp", "mp", None, None, None, None),
        P("dp", "mp", None, None, None, None),
    )
    out_specs = (
        P("dp", "mp", None, None, None, None),
        P("dp", "mp", None, None, None, None),
        P("mp", None, None),
    )
    return jax.shard_map(
        per_device, mesh=mesh, in_specs=in_specs, out_specs=out_specs, check_vma=False
    )
```

```python
import functools

import jax
import jax.numpy as jnp
from jax import lax
from jax.experimental import pallas as pl
from jax.experimental.pallas import tpu as pltpu
from jax.sharding import PartitionSpec as P

MESH = pl.DeviceIdType.MESH
F32 = jnp.float32
BF16 = jnp.bfloat16

BS = 512
KB = 4
SLOTS = 2
TL = 128
TILES = [(a, b) for a in range(4) for b in range(a, 4)]
NT = len(TILES)
SP = 5
GP = 4
decay_rate = 0.8
epsilon = 1e-06


def coords():
    d = lax.axis_index("dp")
    return d // 8, (d // 2) % 4, d % 2


def at(y, z, c):
    return {"dp": (y * 4 + z) * 2 + c}


def dot_nt(a, b):
    return lax.dot_general(a, b, (((1,), (1,)), ((), ())), preferred_element_type=F32)


def dot_tn(a, b):
    return lax.dot_general(a, b, (((0,), (0,)), ((), ())), preferred_element_type=F32)


def dot_nn(a, b):
    return lax.dot_general(a, b, (((1,), (0,)), ((), ())), preferred_element_type=F32)


W0 = 25 / 16
W1 = -5 / 16 - 3125 / 4096
W2 = 3125 / 4096
W3 = -1250 / 4096
W4 = 250 / 4096
W5 = -25 / 4096
W6 = 1 / 4096


def split(x):
    hi = x.astype(BF16)
    return hi, (x - hi.astype(F32)).astype(BF16)


def dot3(ah, al, bh, bl):
    return dot_nn(ah, bh) + (dot_nn(ah, bl) + dot_nn(al, bh))


def find_slot(owner_ref, place):
    block = jnp.int32(0)
    alive = jnp.int32(0)
    for k in range(KB):
        hit = (owner_ref[0, k] == place).astype(jnp.int32)
        block = jnp.where(hit == 1, k, block)
        alive = jnp.maximum(alive, hit)
    return block, alive


def inverse_root(a_ref, store, bufs):
    mf, m2f, nf, zf, mh, ml, ah, al, bh, bl, ch, cl = bufs
    a = a_ref[...]
    square = jnp.sum(a * a, axis=0, keepdims=True)
    mean = jnp.sum(square, axis=1, keepdims=True) * (1.0 / (BS * BS))
    scale = BS * jnp.sqrt(mean + epsilon)
    inverse = 1.0 / scale
    outer = 1.0 / jnp.sqrt(jnp.sqrt(scale))
    lo, up = slice(0, 256), slice(256, 512)

    def put(f, h, l, v, rows, cols):
        for x, r, k in ((v, rows, cols),) if rows is cols else ((v, rows, cols), (v.T, cols, rows)):
            hi = x.astype(BF16)
            h[r, k] = hi
            if f is not None:
                f[r, k] = x
            if l is not None:
                l[r, k] = (x - hi.astype(F32)).astype(BF16)

    def multiply(lh, ll, rh, rl, then):
        for rows, cols in ((lo, lo), (lo, up), (up, up)):
            if rl is None:
                q = dot_nn(lh[rows, :], rh[:, cols])
            else:
                q = dot3(lh[rows, :], ll[rows, :], rh[:, cols], rl[:, cols])
            then(q, rows, cols)

    for rows in (lo, up):
        x = a_ref[rows, :] * inverse
        mf[rows, :] = x
        mh[rows, :], ml[rows, :] = split(x)
    multiply(mh, ml, mh, ml, lambda q, r, k: put(m2f, ah, al, q, r, k))

    def third(q, r, k):
        m, m2 = mf[r, k], m2f[r, k]
        nf[r, k] = W1 * m + W2 * m2 + W3 * q
        put(None, bh, None, q, r, k)
        put(None, ch, None, W4 * m + W5 * m2 + W6 * q, r, k)

    multiply(ah, al, mh, ml, third)
    multiply(ch, None, bh, None, lambda q, r, k: put(nf, ah, al, nf[r, k] + q, r, k))
    multiply(ah, al, mh, ml, lambda q, r, k: put(zf, ch, cl, W0 * mf[r, k] + q, r, k))
    multiply(ah, al, ah, al, lambda q, r, k: put(m2f, bh, bl, (2 * W0) * nf[r, k] + q, r, k))
    multiply(bh, bl, bh, bl, lambda q, r, k: put(None, ah, al, (2 * W0 * W0) * m2f[r, k] + q, r, k))

    def last(q, r, k):
        x = 1.25 * nf[r, k] - (0.25 * W0**4) * zf[r, k] - 0.25 * q
        if r is k:
            rows = lax.broadcasted_iota(jnp.int32, (256, 256), 0)
            cols = lax.broadcasted_iota(jnp.int32, (256, 256), 1)
            x = x + jnp.where(rows == cols, F32(1.25 * W0), F32(0.0))
        x = outer * x
        store(r, k, x)
        if r is not k:
            store(k, r, x.T)

    multiply(ah, al, ch, cl, last)


class Spread:
    def __init__(self, st, r1, r2, every, sems, place):
        self.st, self.r1, self.r2, self.all = st, r1, r2, every
        self.s1, self.q1, self.s2, self.q2, self.s3, self.q3, self.s4, self.q4, self.sd, self.qd = sems
        self.c, self.pos1, self.pos2, self.dev1, self.dev2, self.mate = place

    def c1(self, p, q):
        o = (self.pos1 - p + 4) % 4 - 1
        return rcopy(
            self.st.at[p, q], self.r1.at[o, q], self.s1.at[o, q], self.q1.at[o, q], self.dev1(p)
        )

    def c2(self, q):
        o = (self.pos2 - q + 4) % 4 - 1
        return rcopy(self.st.at[self.pos1, q], self.r2.at[o], self.s2.at[o], self.q2.at[o], self.dev2(q))

    def c3(self, o, q, device):
        ref = self.all.at[self.c, self.pos1, q]
        return rcopy(ref, ref, self.s3.at[o - 1], self.q3.at[o - 1], device)

    def c4(self, o, p, q, device):
        ref = self.all.at[self.c, p, q]
        return rcopy(ref, ref, self.s4.at[o - 1, q], self.q4.at[o - 1, q], device)

    def cd(self, core, p, q):
        ref = self.all.at[core, p, q]
        return rcopy(ref, ref, self.sd.at[p, q], self.qd.at[p, q], self.mate)

    def send1(self, p):
        for k in range(4):
            self.c1(p, (self.pos2 + 1 + k) % 4).start()

    def add1(self):
        for k in range(1, 5):
            q = (self.pos2 + k) % 4
            for o in (1, 2, 3):
                self.c1((self.pos1 + o) % 4, q).wait_recv()
            self.st[self.pos1, q] = (self.st[self.pos1, q] + self.r1[0, q]) + (self.r1[1, q] + self.r1[2, q])
            if k < 4:
                self.c2(q).start()

    def add2(self):
        for o in (1, 2, 3):
            self.c2((self.pos2 + o) % 4).wait_recv()
        self.all[self.c, self.pos1, self.pos2] = (self.st[self.pos1, self.pos2] + self.r2[0]) + (
            self.r2[1] + self.r2[2]
        )
        for o in (2, 1, 3):
            self.c3(o, self.pos2, self.dev2((self.pos2 - o + 4) % 4)).start()

    def gather2(self):
        for k in (0, 1, 3, 2):
            q = (self.pos2 + k) % 4
            if k:
                self.c3(k, q, self.dev2(q)).wait_recv()
            for o in (2, 1, 3):
                self.c4(o, self.pos1, q, self.dev1((self.pos1 - o + 4) % 4)).start()
            self.cd(self.c, self.pos1, q).start()

    def gather1(self):
        for o in (1, 3, 2):
            p = (self.pos1 + o) % 4
            for k in (0, 1, 3, 2):
                q = (self.pos2 + k) % 4
                self.c4(o, p, q, self.dev1(p)).wait_recv()
                self.cd(self.c, p, q).start()

    def from_mate(self):
        for p in range(4):
            for q in range(4):
                self.cd(1 - self.c, p, q).wait_recv()

    def sent(self):
        for o in (1, 2, 3):
            for q in range(4):
                self.c1((self.pos1 + o) % 4, q).wait_send()
                self.c4(o, self.pos1, q, self.dev1((self.pos1 - o + 4) % 4)).wait_send()
            self.c2((self.pos2 + o) % 4).wait_send()
            self.c3(o, self.pos2, self.dev2((self.pos2 - o + 4) % 4)).wait_send()
        for p in range(4):
            for q in range(4):
                self.cd(self.c, p, q).wait_send()

    @staticmethod
    def sems():
        dma = pltpu.SemaphoreType.DMA
        return [dma((3, 4)), dma((3, 4)), dma((3,)), dma((3,)), dma((3,)), dma((3,)),
                dma((3, 4)), dma((3, 4)), dma((4, 4)), dma((4, 4))]


def rcopy(src, dst, ss, rs, device):
    return pltpu.make_async_remote_copy(
        src_ref=src, dst_ref=dst, send_sem=ss, recv_sem=rs, device_id=device, device_id_type=MESH
    )


def main_kernel(owner_ref, g_ref, acc_ref, new_ref, gs_ref, lroot_ref, rroot_ref, *scratch):
    (praw, accn, sts, sr1, sr2, sall, stg, gr1, gr2, pacc, am, rsend), scratch = scratch[:12], scratch[12:]
    bufs, scratch = scratch[:12], scratch[12:]
    ssem, gsem, (s_raw, s_acc, s_old, s_root, s_new) = scratch[:10], scratch[10:20], scratch[20:]
    y, z, c = coords()
    pos1 = z + c * (y - z)
    pos2 = y + c * (z - y)

    def dev1(p):
        return at(y + c * (p - y), p + c * (z - p), c)

    def dev2(p):
        return at(p + c * (y - p), z + c * (p - z), c)

    mate = at(y, z, 1 - c)
    place = (c, pos1, pos2, dev1, dev2, mate)
    stat = Spread(sts, sr1, sr2, sall, ssem, place)
    gsum = Spread(stg, gr1, gr2, gs_ref, gsem, place)

    olds = [pltpu.make_async_copy(acc_ref.at[j], accn.at[j], s_old.at[j]) for j in range(SLOTS)]
    for a in olds:
        a.start()
    barrier = pltpu.get_barrier_semaphore()
    for o in (1, 2, 3):
        pl.semaphore_signal(barrier, inc=1, device_id=dev1((pos1 + o) % 4), device_id_type=MESH)
        pl.semaphore_signal(barrier, inc=1, device_id=dev2((pos2 + o) % 4), device_id_type=MESH)
    pl.semaphore_signal(barrier, inc=1, device_id=mate, device_id_type=MESH)
    pl.semaphore_wait(barrier, 7)

    raw = rcopy(g_ref.at[pl.ds(2 * (1 - c), 2)], praw, s_raw.at[0], s_raw.at[1], mate)
    raw.start()
    accs = [rcopy(acc_ref.at[j, 1], pacc.at[j], s_acc.at[0, j], s_acc.at[1, j], mate) for j in range(SLOTS)]
    raw.wait()
    for a in accs:
        a.start()

    def put(p, a, b, block):
        t = TILES.index((a, b))
        for half in range(2):
            h = 2 * t + half
            sts[p, h // SP, h % SP] = block[half * 64:(half + 1) * 64]

    def quadrants(p, quad):
        x = quad(0, 0)
        put(p, 0, 0, x[:128, :128])
        put(p, 0, 1, x[:128, 128:])
        put(p, 1, 1, x[128:, 128:])
        x = quad(0, 1)
        put(p, 0, 2, x[:128, :128])
        put(p, 0, 3, x[:128, 128:])
        put(p, 1, 2, x[128:, :128])
        put(p, 1, 3, x[128:, 128:])
        x = quad(1, 1)
        put(p, 2, 2, x[:128, :128])
        put(p, 2, 3, x[:128, 128:])
        put(p, 3, 3, x[128:, 128:])

    @pl.loop(0, 4)
    def _(i):
        p = (pos1 + jnp.where(i == 0, 2, jnp.where(i == 1, 1, jnp.where(i == 2, 3, 0)))) % 4
        blk = p // 2

        @pl.when(p % 2 == 0)
        def _():
            quadrants(
                p,
                lambda a, b: dot_nt(
                    g_ref[2 * c + blk, a * 256:(a + 1) * 256, :], g_ref[2 * c + blk, b * 256:(b + 1) * 256, :]
                )
                + dot_nt(praw[blk, a * 256:(a + 1) * 256, :], praw[blk, b * 256:(b + 1) * 256, :]),
            )

        @pl.when(p % 2 == 1)
        def _():
            quadrants(
                p,
                lambda a, b: dot_tn(
                    g_ref[2 * c + blk, :, a * 256:(a + 1) * 256], g_ref[2 * c + blk, :, b * 256:(b + 1) * 256]
                )
                + dot_tn(praw[blk, :, a * 256:(a + 1) * 256], praw[blk, :, b * 256:(b + 1) * 256]),
            )

        @pl.when(i < 3)
        def _():
            stat.send1(p)

    @pl.loop(0, 4)
    def _(i):
        p = (pos1 + jnp.where(i == 0, 2, jnp.where(i == 1, 1, jnp.where(i == 2, 3, 0)))) % 4
        for q in range(4):
            rows = pl.ds((p % 2) * 256 + q * 64, 64)
            total = g_ref[2 * c + p // 2, rows, :].astype(F32) + praw[p // 2, rows, :].astype(F32)
            for k in range(GP):
                stg[p, q, k] = total[:, k * 128:(k + 1) * 128]

        @pl.when(i < 3)
        def _():
            gsum.send1(p)

    stat.add1()
    stat.add2()
    stat.gather2()
    gsum.add1()
    stat.gather1()
    gsum.add2()
    for a in accs:
        a.wait()
    for a in olds:
        a.wait()
    stat.from_mate()

    d = lax.axis_index("dp")
    other = d + 1 - 2 * c

    def blend(dst, src, blk, alive, lr):
        keep = jnp.where(alive == 1, F32(decay_rate), F32(1.0))
        take = jnp.where(alive == 1, F32((1.0 - decay_rate) / 16384.0), F32(0.0))
        for t, (a, b) in enumerate(TILES):
            for half in range(2):
                h = 2 * t + half
                fresh = take * sall[blk // 2, 2 * (blk % 2) + lr, h // SP, h % SP]
                ra, rb = pl.ds(a * TL + half * 64, 64), pl.ds(b * TL, TL)
                dst[ra, rb] = keep * src[ra, rb] + fresh
                if a != b:
                    dst[rb, ra] = keep * src[rb, ra] + fresh.T

    def root(j):
        return rcopy(rsend.at[j], rroot_ref.at[j], s_root.at[0, j], s_root.at[1, j], mate)

    def new(j):
        return pltpu.make_async_copy(accn.at[j], new_ref.at[j], s_new.at[j])

    @pl.loop(0, 4)
    def _(t):
        j = t % 2

        @pl.when(t < 2)
        def _():
            blk, _ = find_slot(owner_ref, other * SLOTS + j)
            blend(am, pacc.at[j], blk, jnp.int32(1), 1)

        @pl.when(t >= 2)
        def _():
            blk, alive = find_slot(owner_ref, d * SLOTS + j)
            blend(accn.at[j, 0], accn.at[j, 0], blk, alive, 0)
            blend(accn.at[j, 1], accn.at[j, 1], blk, alive, 1)
            am[...] = accn[j, 0]
            new(j).start()

        def store(rows, cols, x):
            @pl.when(t < 2)
            def _():
                rsend[j, rows, cols] = x

            @pl.when(t >= 2)
            def _():
                lroot_ref[j, rows, cols] = x

        inverse_root(am, store, bufs)

        @pl.when(t < 2)
        def _():
            root(j).start()

        @pl.when(t == 0)
        def _():
            gsum.gather2()

        @pl.when(t == 2)
        def _():
            gsum.gather1()

    for j in range(SLOTS):
        root(j).wait()
        new(j).wait()
    gsum.from_mate()
    stat.sent()
    gsum.sent()


def call_main(owner, grads, acc):
    dma = pltpu.SemaphoreType.DMA
    vmem = pl.BlockSpec(memory_space=pltpu.VMEM)
    hbm = pl.BlockSpec(memory_space=pltpu.HBM)
    square = lambda n, dt: pltpu.VMEM(n + (BS, BS), dt)
    return pl.pallas_call(
        main_kernel,
        name="main",
        out_shape=(
            jax.ShapeDtypeStruct((SLOTS, 2, BS, BS), F32),
            jax.ShapeDtypeStruct((2, 4, 4, GP, 64, TL), F32),
            jax.ShapeDtypeStruct((SLOTS, BS, BS), F32),
            jax.ShapeDtypeStruct((SLOTS, BS, BS), F32),
        ),
        in_specs=[pl.BlockSpec(memory_space=pltpu.SMEM), vmem, hbm],
        out_specs=(hbm, vmem, vmem, vmem),
        scratch_shapes=[
            square((2,), BF16),
            square((SLOTS, 2), F32),
            pltpu.VMEM((4, 4, SP, 64, TL), F32),
            pltpu.VMEM((3, 4, SP, 64, TL), F32),
            pltpu.VMEM((3, SP, 64, TL), F32),
            pltpu.VMEM((2, 4, 4, SP, 64, TL), F32),
            pltpu.VMEM((4, 4, GP, 64, TL), F32),
            pltpu.VMEM((3, 4, GP, 64, TL), F32),
            pltpu.VMEM((3, GP, 64, TL), F32),
            square((SLOTS,), F32),
            square((), F32),
            square((SLOTS,), F32),
        ]
        + [square((), F32)] * 4 + [square((), BF16)] * 8
        + Spread.sems() + Spread.sems()
        + [dma((2,)), dma((2, SLOTS)), dma((SLOTS,)), dma((2, SLOTS)), dma((SLOTS,))],
        compiler_params=pltpu.CompilerParams(
            collective_id=1, has_side_effects=True, vmem_limit_bytes=38 << 20
        ),
    )(owner, grads, acc)


def product_kernel(
    owner_ref, rf_ref, new_ref, gs_ref, l_ref, r_ref, old_ref,
    accum_ref, roots_ref, sq_ref, p_ref,
    flag, gh, gl, sem,
):
    d = lax.axis_index("dp")
    accum = pltpu.make_async_copy(new_ref, accum_ref, sem.at[0])
    accum.start()
    for j in range(SLOTS):
        blk, alive = find_slot(owner_ref, d * SLOTS + j)
        fresh = alive * (rf_ref[0, j] >= 0).astype(jnp.int32)
        flag[0, j], flag[1, j], flag[2, j] = blk, alive, fresh

        @pl.when(fresh == 1)
        def _():
            for i, ref in enumerate((l_ref, r_ref)):
                pltpu.make_async_copy(ref.at[j], roots_ref.at[j, i], sem.at[1 + 2 * j + i]).start()

        @pl.when(fresh == 0)
        def _():
            for i in range(2):
                pltpu.make_async_copy(old_ref.at[j, i], roots_ref.at[j, i], sem.at[1 + 2 * j + i]).start()

    sq_ref[...] = jnp.zeros_like(sq_ref)

    @pl.loop(0, SLOTS)
    def _(j):
        fresh = flag[2, j] == 1

        @pl.when(flag[1, j] == 1)
        def _():
            blk = flag[0, j]
            for h in range(2):
                for q in range(4):
                    for k in range(4):
                        rows, cols = pl.ds(h * 256 + q * 64, 64), pl.ds(k * TL, TL)
                        gh[0, rows, cols], gl[0, rows, cols] = split(
                            gs_ref[blk // 2, 2 * (blk % 2) + h, q, k]
                        )
            gh[1], gl[1] = split(jnp.where(fresh, r_ref[j], old_ref[j, 1]))

            @pl.loop(0, 2)
            def _(h):
                rows = pl.ds(pl.multiple_of(h * 256, 256), 256)
                ah, al = split(jnp.where(fresh, l_ref[j, rows, :], old_ref[j, 0, rows, :]))
                t = dot3(ah, al, gh[0], gl[0])
                th, tl = split(t)
                x = dot3(th, tl, gh[1], gl[1])
                p_ref[j, rows, :] = x
                part = jnp.sum((x * x).reshape(32, 8, BS), axis=0)
                sq_ref[...] += (part[:, :128] + part[:, 128:256]) + (part[:, 256:384] + part[:, 384:])

        @pl.when(flag[1, j] == 0)
        def _():
            p_ref[j] = jnp.zeros((BS, BS), F32)

    accum.wait()
    for j in range(SLOTS):
        for i in range(2):
            pltpu.make_async_copy(old_ref.at[j, i], roots_ref.at[j, i], sem.at[1 + 2 * j + i]).wait()


def call_product(owner, refresh, new, gs, lroot, rroot, old):
    anywhere = pl.BlockSpec(memory_space=pl.ANY)
    smem = pl.BlockSpec(memory_space=pltpu.SMEM)
    vmem = pl.BlockSpec(memory_space=pltpu.VMEM)
    hbm = pl.BlockSpec(memory_space=pltpu.HBM)
    return pl.pallas_call(
        product_kernel,
        name="product",
        out_shape=(
            jax.ShapeDtypeStruct((SLOTS, 2, BS, BS), F32),
            jax.ShapeDtypeStruct((SLOTS, 2, BS, BS), F32),
            jax.ShapeDtypeStruct((8, TL), F32),
            jax.ShapeDtypeStruct((SLOTS, BS, BS), F32),
        ),
        in_specs=[smem] * 2 + [hbm] + [vmem] * 4,
        out_specs=(anywhere, anywhere, vmem, vmem),
        scratch_shapes=[
            pltpu.SMEM((3, SLOTS), jnp.int32),
            pltpu.VMEM((2, BS, BS), BF16),
            pltpu.VMEM((2, BS, BS), BF16),
            pltpu.SemaphoreType.DMA((5,)),
        ],
        compiler_params=pltpu.CompilerParams(vmem_limit_bytes=16 << 20),
    )(owner, refresh, new, gs, lroot, rroot, old)


def tail_kernel(
    n_mp, owner_ref, p_ref, sq_ref, up_ref,
    na, nb, pbuf, sb, r1, r2, f3,
    s_a, q_a, s_b, q_b, s_p, q_p, s_own, s1, q1, s2, q2, s3, q3, s4, q4, sd, qd, sl,
):
    y, z, c = coords()
    x = lax.axis_index("mp")
    pos1 = z + c * (y - z)
    pos2 = y + c * (z - y)
    plane = y * 4 + z
    pair = x * 2 + c

    def dev1(p):
        return at(y + c * (p - y), p + c * (z - p), c)

    def dev2(p):
        return at(p + c * (y - p), z + c * (p - z), c)

    mate = at(y, z, 1 - c)

    def in_plane(n):
        return {"dp": n * 2 + c}

    def in_pair(n):
        return {"dp": plane * 2 + n % 2, "mp": n // 2}

    barrier = pltpu.get_barrier_semaphore()
    for o in range(1, 16):
        pl.semaphore_signal(barrier, inc=1, device_id=in_plane((plane + o) % 16), device_id_type=MESH)
    for o in range(1, 2 * n_mp):
        pl.semaphore_signal(barrier, inc=1, device_id=in_pair((pair + o) % (2 * n_mp)), device_id_type=MESH)
    pl.semaphore_wait(barrier, 15 + 2 * n_mp - 1)

    na[plane] = sq_ref[...]

    def ca(o):
        return rcopy(na.at[plane], na.at[plane], s_a.at[o - 1], q_a.at[o - 1], in_plane((plane - o + 16) % 16))

    for o in range(1, 16):
        ca(o).start()

    def halves(j):
        return rcopy(
            p_ref.at[j, pl.ds((1 - c) * 256, 256)], pbuf.at[SLOTS + j], s_p.at[j], q_p.at[j], mate
        )

    def own(j):
        return pltpu.make_async_copy(p_ref.at[j, pl.ds(c * 256, 256)], pbuf.at[j], s_own.at[j])

    for j in range(SLOTS):
        halves(j).start()
        own(j).start()
    pbuf[2 * SLOTS] = jnp.zeros((256, BS), F32)
    for o in range(1, 16):
        ca(o).wait_recv()
    total = na[0]
    for n in range(1, 16):
        total = total + na[n]
    nb[pair] = total

    def cb(o):
        n = 2 * n_mp
        return rcopy(nb.at[pair], nb.at[pair], s_b.at[o - 1], q_b.at[o - 1], in_pair((pair - o + n) % n))

    for o in range(1, 2 * n_mp):
        cb(o).start()
    for j in range(SLOTS):
        halves(j).wait_recv()
        own(j).wait()
    for o in range(1, 2 * n_mp):
        cb(o).wait_recv()
    total = nb[0]
    for n in range(1, 2 * n_mp):
        total = total + nb[n]
    square = jnp.sum(jnp.sum(total, axis=0, keepdims=True), axis=1, keepdims=True)
    ratio = 1.0 / jnp.sqrt(square / float(KB * n_mp * BS * BS) + epsilon)

    base = (plane * 2 + c) * SLOTS
    mate_base = (plane * 2 + 1 - c) * SLOTS
    index = []
    for k in range(KB):
        place = owner_ref[0, k]
        n = jnp.int32(2 * SLOTS)
        for j in range(SLOTS):
            n = n + (j - 2 * SLOTS) * (place == base + j).astype(jnp.int32)
            n = n + (j - SLOTS) * (place == mate_base + j).astype(jnp.int32)
        index.append(n)

    def c1(p, o):
        return rcopy(sb.at[p], r1.at[o - 1], s1.at[o - 1], q1.at[o - 1], dev1(p))

    @pl.loop(0, 4)
    def _(i):
        p = (pos1 + jnp.where(i == 0, 2, jnp.where(i == 1, 1, jnp.where(i == 2, 3, 0)))) % 4
        o = (pos1 - p + 4) % 4
        for k in range(KB):
            for q in range(4):
                block = pbuf[index[k], pl.ds(p * 64 + q * 16, 16), :]
                sb[p, q, k] = (ratio * block).astype(BF16)

        @pl.when(i < 3)
        def _():
            c1(p, o).start()

    def c2(q):
        o = (pos2 - q + 4) % 4
        return rcopy(sb.at[pos1, q], r2.at[o - 1], s2.at[o - 1], q2.at[o - 1], dev2(q))

    for o in (1, 2, 3):
        c1(pos1, o).wait_recv()

    @pl.loop(1, 5)
    def _(k):
        q = (pos2 + k) % 4
        sb[pos1, q] = (sb[pos1, q] + r1[0, q]) + (r1[1, q] + r1[2, q])

        @pl.when(k < 4)
        def _():
            c2(q).start()

    for o in (1, 2, 3):
        c2((pos2 + o) % 4).wait_recv()
    f3[pos2] = (sb[pos1, pos2] + r2[0]) + (r2[1] + r2[2])

    def c3(o):
        return rcopy(f3.at[pos2], f3.at[pos2], s3.at[o - 1], q3.at[o - 1], dev2((pos2 - o + 4) % 4))

    def out(core, p, q):
        return up_ref.at[:, pl.ds(core * 256 + p * 64 + q * 16, 16), :]

    def c4(o, q):
        return rcopy(
            f3.at[q], out(c, pos1, q), s4.at[o - 1, q], q4.at[o - 1, q], dev1((pos1 - o + 4) % 4)
        )

    def cd_own(q):
        return rcopy(f3.at[q], out(c, pos1, q), sd.at[0, q], qd.at[0, q], mate)

    def cd(o, q):
        p = (pos1 + o) % 4
        return rcopy(out(c, p, q), out(c, p, q), sd.at[o, q], qd.at[o, q], mate)

    def keep(q):
        return pltpu.make_async_copy(f3.at[q], out(c, pos1, q), sl.at[q])

    for o in (2, 1, 3):
        c3(o).start()
    for k in (0, 1, 3, 2):
        q = (pos2 + k) % 4
        if k:
            rcopy(f3.at[pos2], f3.at[q], s3.at[k - 1], q3.at[k - 1], dev2(q)).wait_recv()
        for o in (2, 1, 3):
            c4(o, q).start()
        cd_own(q).start()
        keep(q).start()
    for o in (1, 3, 2):
        for k in (0, 1, 3, 2):
            q = (pos2 + k) % 4
            p = (pos1 + o) % 4
            rcopy(f3.at[q], out(c, p, q), s4.at[o - 1, q], q4.at[o - 1, q], dev1(p)).wait_recv()
            cd(o, q).start()

    for o in range(1, 16):
        ca(o).wait_send()
    for o in range(1, 2 * n_mp):
        cb(o).wait_send()
    for j in range(SLOTS):
        halves(j).wait_send()
    for k in range(1, 4):
        p = (pos1 + k) % 4
        c1(p, (pos1 - p + 4) % 4).wait_send()
        c2((pos2 + k) % 4).wait_send()
        c3(k).wait_send()
    for q in range(4):
        keep(q).wait()
        for o in (1, 2, 3):
            c4(o, q).wait_send()
            cd(o, q).wait_send()
        cd_own(q).wait_send()
        for o in range(4):
            p = (pos2 + o) % 4
            rcopy(f3.at[q], out(1 - c, p, q), sd.at[o, q], qd.at[o, q], mate).wait_recv()


def call_tail(owner, product, sq, n_mp):
    dma = pltpu.SemaphoreType.DMA
    return pl.pallas_call(
        functools.partial(tail_kernel, n_mp),
        name="tail",
        out_shape=jax.ShapeDtypeStruct((KB, BS, BS), BF16),
        in_specs=[pl.BlockSpec(memory_space=pltpu.SMEM)] + [pl.BlockSpec(memory_space=pltpu.VMEM)] * 2,
        out_specs=pl.BlockSpec(memory_space=pl.ANY),
        scratch_shapes=[
            pltpu.VMEM((16, 8, TL), F32),
            pltpu.VMEM((2 * n_mp, 8, TL), F32),
            pltpu.VMEM((2 * SLOTS + 1, 256, BS), F32),
            pltpu.VMEM((4, 4, KB, 16, BS), BF16),
            pltpu.VMEM((3, 4, KB, 16, BS), BF16),
            pltpu.VMEM((3, KB, 16, BS), BF16),
            pltpu.VMEM((4, KB, 16, BS), BF16),
            dma((15,)), dma((15,)), dma((2 * n_mp - 1,)), dma((2 * n_mp - 1,)),
            dma((SLOTS,)), dma((SLOTS,)), dma((SLOTS,)),
            dma((3,)), dma((3,)), dma((3,)), dma((3,)), dma((3,)), dma((3,)),
            dma((3, 4)), dma((3, 4)), dma((4, 4)), dma((4, 4)), dma((4,)),
        ],
        compiler_params=pltpu.CompilerParams(
            collective_id=2, has_side_effects=True, vmem_limit_bytes=16 << 20
        ),
    )(owner, product, sq)


def per_device(grads, block_owner, refresh_to, accum_old, roots_old):
    n_mp = lax.axis_size("mp")
    new, gs, lroot, rroot = call_main(block_owner, grads[0], accum_old[0, 0])
    new_accum, roots, sq, product = call_product(
        block_owner, refresh_to[0], new, gs, lroot, rroot, roots_old[0, 0]
    )
    update = call_tail(block_owner, product, sq, n_mp)
    return (new_accum[None, None], roots[None, None], update)


def solution(mesh):
    in_specs = (
        P("dp", "mp", None, None),
        P("mp", None),
        P("dp", "mp", None),
        P("dp", "mp", None, None, None, None),
        P("dp", "mp", None, None, None, None),
    )
    out_specs = (
        P("dp", "mp", None, None, None, None),
        P("dp", "mp", None, None, None, None),
        P("mp", None, None),
    )
    return jax.shard_map(
        per_device, mesh=mesh, in_specs=in_specs, out_specs=out_specs, check_vma=False
    )
```

```python
import functools

import jax
import jax.numpy as jnp
from jax import lax
from jax.experimental import pallas as pl
from jax.experimental.pallas import tpu as pltpu
from jax.sharding import PartitionSpec as P

MESH = pl.DeviceIdType.MESH
F32 = jnp.float32
BF16 = jnp.bfloat16

BS = 512
KB = 4
SLOTS = 2
TL = 128
TILES = [(a, b) for a in range(4) for b in range(a, 4)]
NT = len(TILES)
SP = 5
GP = 4
decay_rate = 0.8
epsilon = 1e-06


def coords():
    d = lax.axis_index("dp")
    return d // 8, (d // 2) % 4, d % 2


def at(y, z, c):
    return {"dp": (y * 4 + z) * 2 + c}


def dot_nt(a, b):
    return lax.dot_general(a, b, (((1,), (1,)), ((), ())), preferred_element_type=F32)


def dot_tn(a, b):
    return lax.dot_general(a, b, (((0,), (0,)), ((), ())), preferred_element_type=F32)


def dot_nn(a, b):
    return lax.dot_general(a, b, (((1,), (0,)), ((), ())), preferred_element_type=F32)


W0 = 25 / 16
W1 = -5 / 16 - 3125 / 4096
W2 = 3125 / 4096
W3 = -1250 / 4096
W4 = 250 / 4096
W5 = -25 / 4096
W6 = 1 / 4096


def split(x):
    hi = x.astype(BF16)
    return hi, (x - hi.astype(F32)).astype(BF16)


def dot3(ah, al, bh, bl):
    return dot_nn(ah, bh) + (dot_nn(ah, bl) + dot_nn(al, bh))


def find_slot(owner_ref, place):
    block = jnp.int32(0)
    alive = jnp.int32(0)
    for k in range(KB):
        hit = (owner_ref[0, k] == place).astype(jnp.int32)
        block = jnp.where(hit == 1, k, block)
        alive = jnp.maximum(alive, hit)
    return block, alive


def inverse_root(a_ref, store, bufs):
    mf, m2f, nf, zf, mh, ml, ah, al, bh, bl, ch, cl = bufs
    a = a_ref[...]
    square = jnp.sum(a * a, axis=0, keepdims=True)
    mean = jnp.sum(square, axis=1, keepdims=True) * (1.0 / (BS * BS))
    scale = BS * jnp.sqrt(mean + epsilon)
    inverse = 1.0 / scale
    outer = 1.0 / jnp.sqrt(jnp.sqrt(scale))
    lo, up = slice(0, 256), slice(256, 512)

    def put(f, h, l, v, rows, cols):
        for x, r, k in ((v, rows, cols),) if rows is cols else ((v, rows, cols), (v.T, cols, rows)):
            hi = x.astype(BF16)
            h[r, k] = hi
            if f is not None:
                f[r, k] = x
            if l is not None:
                l[r, k] = (x - hi.astype(F32)).astype(BF16)

    def multiply(lh, ll, rh, rl, then):
        for rows, cols in ((lo, lo), (lo, up), (up, up)):
            if rl is None:
                q = dot_nn(lh[rows, :], rh[:, cols])
            else:
                q = dot3(lh[rows, :], ll[rows, :], rh[:, cols], rl[:, cols])
            then(q, rows, cols)

    for rows in (lo, up):
        x = a_ref[rows, :] * inverse
        mf[rows, :] = x
        mh[rows, :], ml[rows, :] = split(x)
    multiply(mh, ml, mh, ml, lambda q, r, k: put(m2f, ah, al, q, r, k))

    def third(q, r, k):
        m, m2 = mf[r, k], m2f[r, k]
        nf[r, k] = W1 * m + W2 * m2 + W3 * q
        put(None, bh, None, q, r, k)
        put(None, ch, None, W4 * m + W5 * m2 + W6 * q, r, k)

    multiply(ah, al, mh, ml, third)
    multiply(ch, None, bh, None, lambda q, r, k: put(nf, ah, al, nf[r, k] + q, r, k))
    multiply(ah, al, mh, ml, lambda q, r, k: put(zf, ch, cl, W0 * mf[r, k] + q, r, k))
    multiply(ah, al, ah, al, lambda q, r, k: put(m2f, bh, bl, (2 * W0) * nf[r, k] + q, r, k))
    multiply(bh, bl, bh, bl, lambda q, r, k: put(None, ah, al, (2 * W0 * W0) * m2f[r, k] + q, r, k))

    def last(q, r, k):
        x = 1.25 * nf[r, k] - (0.25 * W0**4) * zf[r, k] - 0.25 * q
        if r is k:
            rows = lax.broadcasted_iota(jnp.int32, (256, 256), 0)
            cols = lax.broadcasted_iota(jnp.int32, (256, 256), 1)
            x = x + jnp.where(rows == cols, F32(1.25 * W0), F32(0.0))
        x = outer * x
        store(r, k, x)
        if r is not k:
            store(k, r, x.T)

    multiply(ah, al, ch, cl, last)


class Spread:
    def __init__(self, st, r1, r2, every, sems, place):
        self.st, self.r1, self.r2, self.all = st, r1, r2, every
        self.s1, self.q1, self.s2, self.q2, self.s3, self.q3, self.s4, self.q4, self.sd, self.qd = sems
        self.c, self.pos1, self.pos2, self.dev1, self.dev2, self.mate = place

    def c1(self, p, q):
        o = (self.pos1 - p + 4) % 4 - 1
        return rcopy(
            self.st.at[p, q], self.r1.at[o, q], self.s1.at[o, q], self.q1.at[o, q], self.dev1(p)
        )

    def c2(self, q):
        o = (self.pos2 - q + 4) % 4 - 1
        return rcopy(self.st.at[self.pos1, q], self.r2.at[o], self.s2.at[o], self.q2.at[o], self.dev2(q))

    def c3(self, o, q, device):
        ref = self.all.at[self.c, self.pos1, q]
        return rcopy(ref, ref, self.s3.at[o - 1], self.q3.at[o - 1], device)

    def c4(self, o, p, q, device):
        ref = self.all.at[self.c, p, q]
        return rcopy(ref, ref, self.s4.at[o - 1, q], self.q4.at[o - 1, q], device)

    def cd(self, core, p, q):
        ref = self.all.at[core, p, q]
        return rcopy(ref, ref, self.sd.at[p, q], self.qd.at[p, q], self.mate)

    def send1(self, p):
        for k in range(4):
            self.c1(p, (self.pos2 + 1 + k) % 4).start()

    def add1(self):
        for k in range(1, 5):
            q = (self.pos2 + k) % 4
            for o in (1, 2, 3):
                self.c1((self.pos1 + o) % 4, q).wait_recv()
            self.st[self.pos1, q] = (self.st[self.pos1, q] + self.r1[0, q]) + (self.r1[1, q] + self.r1[2, q])
            if k < 4:
                self.c2(q).start()

    def add2(self):
        for o in (1, 2, 3):
            self.c2((self.pos2 + o) % 4).wait_recv()
        self.all[self.c, self.pos1, self.pos2] = (self.st[self.pos1, self.pos2] + self.r2[0]) + (
            self.r2[1] + self.r2[2]
        )
        for o in (2, 1, 3):
            self.c3(o, self.pos2, self.dev2((self.pos2 - o + 4) % 4)).start()

    def gather2(self):
        for k in (0, 1, 3, 2):
            q = (self.pos2 + k) % 4
            if k:
                self.c3(k, q, self.dev2(q)).wait_recv()
            for o in (2, 1, 3):
                self.c4(o, self.pos1, q, self.dev1((self.pos1 - o + 4) % 4)).start()
            self.cd(self.c, self.pos1, q).start()

    def gather1(self):
        for o in (1, 3, 2):
            p = (self.pos1 + o) % 4
            for k in (0, 1, 3, 2):
                q = (self.pos2 + k) % 4
                self.c4(o, p, q, self.dev1(p)).wait_recv()
                self.cd(self.c, p, q).start()

    def from_mate(self):
        for p in range(4):
            for q in range(4):
                self.cd(1 - self.c, p, q).wait_recv()

    def sent(self):
        for o in (1, 2, 3):
            for q in range(4):
                self.c1((self.pos1 + o) % 4, q).wait_send()
                self.c4(o, self.pos1, q, self.dev1((self.pos1 - o + 4) % 4)).wait_send()
            self.c2((self.pos2 + o) % 4).wait_send()
            self.c3(o, self.pos2, self.dev2((self.pos2 - o + 4) % 4)).wait_send()
        for p in range(4):
            for q in range(4):
                self.cd(self.c, p, q).wait_send()

    @staticmethod
    def sems():
        dma = pltpu.SemaphoreType.DMA
        return [dma((3, 4)), dma((3, 4)), dma((3,)), dma((3,)), dma((3,)), dma((3,)),
                dma((3, 4)), dma((3, 4)), dma((4, 4)), dma((4, 4))]


ROWS = SP * 64
GROUP = 16
PACKED = ROWS + 32


def pack(ref, x):
    x = x.reshape(ROWS // GROUP, GROUP, TL)
    top = jnp.maximum(jnp.max(jnp.abs(x), axis=1), 1e-30)
    e = jnp.ceil(jnp.log2(top) * 64.0)
    inverse = 32700.0 * jnp.exp2(e * (-1.0 / 64.0))
    ref[0:ROWS, :] = jnp.round(x * inverse[:, None, :]).reshape(ROWS, TL).astype(jnp.int32).astype(jnp.int16)
    e = jnp.concatenate([e, jnp.zeros((32 - ROWS // GROUP, TL), F32)], axis=0)
    ref[ROWS:PACKED, :] = e.astype(jnp.int32).astype(jnp.int16)


def unpack(ref):
    e = ref[ROWS:PACKED, :].astype(jnp.int32).astype(F32)[: ROWS // GROUP]
    scale = jnp.exp2(e * (1.0 / 64.0)) * (1.0 / 32700.0)
    x = ref[0:ROWS, :].astype(jnp.int32).astype(F32).reshape(ROWS // GROUP, GROUP, TL)
    return (x * scale[:, None, :]).reshape(SP, 64, TL)


class PackedSpread(Spread):
    def __init__(self, raw, *rest):
        super().__init__(*rest)
        self.raw = raw

    def send1(self, p):
        @pl.loop(1, 5)
        def _(k):
            q = (self.pos2 + k) % 4
            pack(self.st.at[p, q], self.raw[p, q])
            self.c1(p, q).start()

    def add1(self):
        @pl.loop(1, 5)
        def _(k):
            q = (self.pos2 + k) % 4
            total = self.raw[self.pos1, q]
            for o in (1, 2, 3):
                self.c1((self.pos1 + o) % 4, q).wait_recv()
            for o in (1, 2, 3):
                total = total + unpack(self.r1.at[o - 1, q])
            self.raw[self.pos1, q] = total

            @pl.when(k < 4)
            def _():
                pack(self.st.at[self.pos1, q], total)
                self.c2(q).start()

    def add2(self):
        total = self.raw[self.pos1, self.pos2]
        for o in (1, 2, 3):
            self.c2((self.pos2 + o) % 4).wait_recv()
        for o in (1, 2, 3):
            total = total + unpack(self.r2.at[o - 1])
        pack(self.all.at[self.c, self.pos1, self.pos2], total)
        for o in (2, 1, 3):
            self.c3(o, self.pos2, self.dev2((self.pos2 - o + 4) % 4)).start()


def rcopy(src, dst, ss, rs, device):
    return pltpu.make_async_remote_copy(
        src_ref=src, dst_ref=dst, send_sem=ss, recv_sem=rs, device_id=device, device_id_type=MESH
    )


def main_kernel(owner_ref, g_ref, acc_ref, new_ref, gs_ref, lroot_ref, rroot_ref, *scratch):
    (praw, accn, raws, sts, sr1, sr2, sall, stg, gr1, gr2, pacc, am, rsend), scratch = scratch[:13], scratch[13:]
    bufs, scratch = scratch[:12], scratch[12:]
    ssem, gsem, (s_raw, s_acc, s_old, s_root, s_new) = scratch[:10], scratch[10:20], scratch[20:]
    y, z, c = coords()
    pos1 = z + c * (y - z)
    pos2 = y + c * (z - y)

    def dev1(p):
        return at(y + c * (p - y), p + c * (z - p), c)

    def dev2(p):
        return at(p + c * (y - p), z + c * (p - z), c)

    mate = at(y, z, 1 - c)
    place = (c, pos1, pos2, dev1, dev2, mate)
    stat = PackedSpread(raws, sts, sr1, sr2, sall, ssem, place)
    gsum = Spread(stg, gr1, gr2, gs_ref, gsem, place)

    olds = [pltpu.make_async_copy(acc_ref.at[j], accn.at[j], s_old.at[j]) for j in range(SLOTS)]
    for a in olds:
        a.start()
    barrier = pltpu.get_barrier_semaphore()
    for o in (1, 2, 3):
        pl.semaphore_signal(barrier, inc=1, device_id=dev1((pos1 + o) % 4), device_id_type=MESH)
        pl.semaphore_signal(barrier, inc=1, device_id=dev2((pos2 + o) % 4), device_id_type=MESH)
    pl.semaphore_signal(barrier, inc=1, device_id=mate, device_id_type=MESH)
    pl.semaphore_wait(barrier, 7)

    raw = rcopy(g_ref.at[pl.ds(2 * (1 - c), 2)], praw, s_raw.at[0], s_raw.at[1], mate)
    raw.start()
    accs = [rcopy(acc_ref.at[j, 1], pacc.at[j], s_acc.at[0, j], s_acc.at[1, j], mate) for j in range(SLOTS)]
    raw.wait()
    for a in accs:
        a.start()

    def put(p, a, b, block):
        t = TILES.index((a, b))
        for half in range(2):
            h = 2 * t + half
            raws[p, h // SP, h % SP] = block[half * 64:(half + 1) * 64]

    def quadrants(p, quad):
        x = quad(0, 0)
        put(p, 0, 0, x[:128, :128])
        put(p, 0, 1, x[:128, 128:])
        put(p, 1, 1, x[128:, 128:])
        x = quad(0, 1)
        put(p, 0, 2, x[:128, :128])
        put(p, 0, 3, x[:128, 128:])
        put(p, 1, 2, x[128:, :128])
        put(p, 1, 3, x[128:, 128:])
        x = quad(1, 1)
        put(p, 2, 2, x[:128, :128])
        put(p, 2, 3, x[:128, 128:])
        put(p, 3, 3, x[128:, 128:])

    @pl.loop(0, 4)
    def _(i):
        p = (pos1 + jnp.where(i == 0, 2, jnp.where(i == 1, 1, jnp.where(i == 2, 3, 0)))) % 4
        blk = p // 2

        @pl.when(p % 2 == 0)
        def _():
            quadrants(
                p,
                lambda a, b: dot_nt(
                    g_ref[2 * c + blk, a * 256:(a + 1) * 256, :], g_ref[2 * c + blk, b * 256:(b + 1) * 256, :]
                )
                + dot_nt(praw[blk, a * 256:(a + 1) * 256, :], praw[blk, b * 256:(b + 1) * 256, :]),
            )

        @pl.when(p % 2 == 1)
        def _():
            quadrants(
                p,
                lambda a, b: dot_tn(
                    g_ref[2 * c + blk, :, a * 256:(a + 1) * 256], g_ref[2 * c + blk, :, b * 256:(b + 1) * 256]
                )
                + dot_tn(praw[blk, :, a * 256:(a + 1) * 256], praw[blk, :, b * 256:(b + 1) * 256]),
            )

        @pl.when(i < 3)
        def _():
            stat.send1(p)

    @pl.loop(0, 4)
    def _(i):
        p = (pos1 + jnp.where(i == 0, 2, jnp.where(i == 1, 1, jnp.where(i == 2, 3, 0)))) % 4
        for q in range(4):
            rows = pl.ds((p % 2) * 256 + q * 64, 64)
            total = g_ref[2 * c + p // 2, rows, :].astype(F32) + praw[p // 2, rows, :].astype(F32)
            for k in range(GP):
                stg[p, q, k] = total[:, k * 128:(k + 1) * 128]

        @pl.when(i < 3)
        def _():
            gsum.send1(p)

    stat.add1()
    stat.add2()
    stat.gather2()
    gsum.add1()
    stat.gather1()
    gsum.add2()
    for a in accs:
        a.wait()
    for a in olds:
        a.wait()
    stat.from_mate()

    d = lax.axis_index("dp")
    other = d + 1 - 2 * c

    def blend(dst, src, blk, alive, lr):
        keep = jnp.where(alive == 1, F32(decay_rate), F32(1.0))
        take = jnp.where(alive == 1, F32((1.0 - decay_rate) / 16384.0), F32(0.0))
        for q in range(4):
            chunk = take * unpack(sall.at[blk // 2, 2 * (blk % 2) + lr, q])
            for n in range(SP):
                h = q * SP + n
                a, b = TILES[h // 2]
                half = h % 2
                fresh = chunk[n]
                ra, rb = pl.ds(a * TL + half * 64, 64), pl.ds(b * TL, TL)
                dst[ra, rb] = keep * src[ra, rb] + fresh
                if a != b:
                    ca = pl.ds(a * TL + half * 64, 64)
                    dst[rb, ca] = keep * src[rb, ca] + fresh.T

    def root(j):
        return rcopy(rsend.at[j], rroot_ref.at[j], s_root.at[0, j], s_root.at[1, j], mate)

    def new(j):
        return pltpu.make_async_copy(accn.at[j], new_ref.at[j], s_new.at[j])

    @pl.loop(0, 4)
    def _(t):
        j = t % 2

        @pl.when(t < 2)
        def _():
            blk, _ = find_slot(owner_ref, other * SLOTS + j)
            blend(am, pacc.at[j], blk, jnp.int32(1), 1)

        @pl.when(t >= 2)
        def _():
            blk, alive = find_slot(owner_ref, d * SLOTS + j)
            blend(accn.at[j, 0], accn.at[j, 0], blk, alive, 0)
            blend(accn.at[j, 1], accn.at[j, 1], blk, alive, 1)
            am[...] = accn[j, 0]
            new(j).start()

        def store(rows, cols, x):
            @pl.when(t < 2)
            def _():
                rsend[j, rows, cols] = x

            @pl.when(t >= 2)
            def _():
                lroot_ref[j, rows, cols] = x

        inverse_root(am, store, bufs)

        @pl.when(t < 2)
        def _():
            root(j).start()

        @pl.when(t == 0)
        def _():
            gsum.gather2()

        @pl.when(t == 2)
        def _():
            gsum.gather1()

    for j in range(SLOTS):
        root(j).wait()
        new(j).wait()
    gsum.from_mate()
    stat.sent()
    gsum.sent()


def call_main(owner, grads, acc):
    dma = pltpu.SemaphoreType.DMA
    vmem = pl.BlockSpec(memory_space=pltpu.VMEM)
    hbm = pl.BlockSpec(memory_space=pltpu.HBM)
    square = lambda n, dt: pltpu.VMEM(n + (BS, BS), dt)
    return pl.pallas_call(
        main_kernel,
        name="main",
        out_shape=(
            jax.ShapeDtypeStruct((SLOTS, 2, BS, BS), F32),
            jax.ShapeDtypeStruct((2, 4, 4, GP, 64, TL), F32),
            jax.ShapeDtypeStruct((SLOTS, BS, BS), F32),
            jax.ShapeDtypeStruct((SLOTS, BS, BS), F32),
        ),
        in_specs=[pl.BlockSpec(memory_space=pltpu.SMEM), vmem, hbm],
        out_specs=(hbm, vmem, vmem, vmem),
        scratch_shapes=[
            square((2,), BF16),
            square((SLOTS, 2), F32),
            pltpu.VMEM((4, 4, SP, 64, TL), F32),
            pltpu.VMEM((4, 4, PACKED, TL), jnp.int16),
            pltpu.VMEM((3, 4, PACKED, TL), jnp.int16),
            pltpu.VMEM((3, PACKED, TL), jnp.int16),
            pltpu.VMEM((2, 4, 4, PACKED, TL), jnp.int16),
            pltpu.VMEM((4, 4, GP, 64, TL), F32),
            pltpu.VMEM((3, 4, GP, 64, TL), F32),
            pltpu.VMEM((3, GP, 64, TL), F32),
            square((SLOTS,), F32),
            square((), F32),
            square((SLOTS,), F32),
        ]
        + [square((), F32)] * 4 + [square((), BF16)] * 8
        + Spread.sems() + Spread.sems()
        + [dma((2,)), dma((2, SLOTS)), dma((SLOTS,)), dma((2, SLOTS)), dma((SLOTS,))],
        compiler_params=pltpu.CompilerParams(
            collective_id=1, has_side_effects=True, vmem_limit_bytes=38 << 20
        ),
    )(owner, grads, acc)


def product_kernel(
    owner_ref, rf_ref, new_ref, gs_ref, l_ref, r_ref, old_ref,
    accum_ref, roots_ref, sq_ref, p_ref,
    flag, gh, gl, sem,
):
    d = lax.axis_index("dp")
    accum = pltpu.make_async_copy(new_ref, accum_ref, sem.at[0])
    accum.start()
    for j in range(SLOTS):
        blk, alive = find_slot(owner_ref, d * SLOTS + j)
        fresh = alive * (rf_ref[0, j] >= 0).astype(jnp.int32)
        flag[0, j], flag[1, j], flag[2, j] = blk, alive, fresh

        @pl.when(fresh == 1)
        def _():
            for i, ref in enumerate((l_ref, r_ref)):
                pltpu.make_async_copy(ref.at[j], roots_ref.at[j, i], sem.at[1 + 2 * j + i]).start()

        @pl.when(fresh == 0)
        def _():
            for i in range(2):
                pltpu.make_async_copy(old_ref.at[j, i], roots_ref.at[j, i], sem.at[1 + 2 * j + i]).start()

    sq_ref[...] = jnp.zeros_like(sq_ref)

    @pl.loop(0, SLOTS)
    def _(j):
        fresh = flag[2, j] == 1

        @pl.when(flag[1, j] == 1)
        def _():
            blk = flag[0, j]
            for h in range(2):
                for q in range(4):
                    for k in range(4):
                        rows, cols = pl.ds(h * 256 + q * 64, 64), pl.ds(k * TL, TL)
                        gh[0, rows, cols], gl[0, rows, cols] = split(
                            gs_ref[blk // 2, 2 * (blk % 2) + h, q, k]
                        )
            gh[1], gl[1] = split(jnp.where(fresh, r_ref[j], old_ref[j, 1]))

            @pl.loop(0, 2)
            def _(h):
                rows = pl.ds(pl.multiple_of(h * 256, 256), 256)
                ah, al = split(jnp.where(fresh, l_ref[j, rows, :], old_ref[j, 0, rows, :]))
                t = dot3(ah, al, gh[0], gl[0])
                th, tl = split(t)
                x = dot3(th, tl, gh[1], gl[1])
                p_ref[j, rows, :] = x
                part = jnp.sum((x * x).reshape(32, 8, BS), axis=0)
                sq_ref[...] += (part[:, :128] + part[:, 128:256]) + (part[:, 256:384] + part[:, 384:])

        @pl.when(flag[1, j] == 0)
        def _():
            p_ref[j] = jnp.zeros((BS, BS), F32)

    accum.wait()
    for j in range(SLOTS):
        for i in range(2):
            pltpu.make_async_copy(old_ref.at[j, i], roots_ref.at[j, i], sem.at[1 + 2 * j + i]).wait()


def call_product(owner, refresh, new, gs, lroot, rroot, old):
    anywhere = pl.BlockSpec(memory_space=pl.ANY)
    smem = pl.BlockSpec(memory_space=pltpu.SMEM)
    vmem = pl.BlockSpec(memory_space=pltpu.VMEM)
    hbm = pl.BlockSpec(memory_space=pltpu.HBM)
    return pl.pallas_call(
        product_kernel,
        name="product",
        out_shape=(
            jax.ShapeDtypeStruct((SLOTS, 2, BS, BS), F32),
            jax.ShapeDtypeStruct((SLOTS, 2, BS, BS), F32),
            jax.ShapeDtypeStruct((8, TL), F32),
            jax.ShapeDtypeStruct((SLOTS, BS, BS), F32),
        ),
        in_specs=[smem] * 2 + [hbm] + [vmem] * 4,
        out_specs=(anywhere, anywhere, vmem, vmem),
        scratch_shapes=[
            pltpu.SMEM((3, SLOTS), jnp.int32),
            pltpu.VMEM((2, BS, BS), BF16),
            pltpu.VMEM((2, BS, BS), BF16),
            pltpu.SemaphoreType.DMA((5,)),
        ],
        compiler_params=pltpu.CompilerParams(vmem_limit_bytes=16 << 20),
    )(owner, refresh, new, gs, lroot, rroot, old)


def tail_kernel(
    n_mp, owner_ref, p_ref, sq_ref, up_ref,
    na, nb, pbuf, sb, r1, r2, f3,
    s_a, q_a, s_b, q_b, s_p, q_p, s_own, s1, q1, s2, q2, s3, q3, s4, q4, sd, qd, sl,
):
    y, z, c = coords()
    x = lax.axis_index("mp")
    pos1 = z + c * (y - z)
    pos2 = y + c * (z - y)
    plane = y * 4 + z
    pair = x * 2 + c

    def dev1(p):
        return at(y + c * (p - y), p + c * (z - p), c)

    def dev2(p):
        return at(p + c * (y - p), z + c * (p - z), c)

    mate = at(y, z, 1 - c)

    def in_plane(n):
        return {"dp": n * 2 + c}

    def in_pair(n):
        return {"dp": plane * 2 + n % 2, "mp": n // 2}

    barrier = pltpu.get_barrier_semaphore()
    for o in range(1, 16):
        pl.semaphore_signal(barrier, inc=1, device_id=in_plane((plane + o) % 16), device_id_type=MESH)
    for o in range(1, 2 * n_mp):
        pl.semaphore_signal(barrier, inc=1, device_id=in_pair((pair + o) % (2 * n_mp)), device_id_type=MESH)
    pl.semaphore_wait(barrier, 15 + 2 * n_mp - 1)

    na[plane] = sq_ref[...]

    def ca(o):
        return rcopy(na.at[plane], na.at[plane], s_a.at[o - 1], q_a.at[o - 1], in_plane((plane - o + 16) % 16))

    for o in range(1, 16):
        ca(o).start()

    def halves(j):
        return rcopy(
            p_ref.at[j, pl.ds((1 - c) * 256, 256)], pbuf.at[SLOTS + j], s_p.at[j], q_p.at[j], mate
        )

    def own(j):
        return pltpu.make_async_copy(p_ref.at[j, pl.ds(c * 256, 256)], pbuf.at[j], s_own.at[j])

    for j in range(SLOTS):
        halves(j).start()
        own(j).start()
    pbuf[2 * SLOTS] = jnp.zeros((256, BS), F32)
    for o in range(1, 16):
        ca(o).wait_recv()
    total = na[0]
    for n in range(1, 16):
        total = total + na[n]
    nb[pair] = total

    def cb(o):
        n = 2 * n_mp
        return rcopy(nb.at[pair], nb.at[pair], s_b.at[o - 1], q_b.at[o - 1], in_pair((pair - o + n) % n))

    for o in range(1, 2 * n_mp):
        cb(o).start()
    for j in range(SLOTS):
        halves(j).wait_recv()
        own(j).wait()
    for o in range(1, 2 * n_mp):
        cb(o).wait_recv()
    total = nb[0]
    for n in range(1, 2 * n_mp):
        total = total + nb[n]
    square = jnp.sum(jnp.sum(total, axis=0, keepdims=True), axis=1, keepdims=True)
    ratio = 1.0 / jnp.sqrt(square / float(KB * n_mp * BS * BS) + epsilon)

    base = (plane * 2 + c) * SLOTS
    mate_base = (plane * 2 + 1 - c) * SLOTS
    index = []
    for k in range(KB):
        place = owner_ref[0, k]
        n = jnp.int32(2 * SLOTS)
        for j in range(SLOTS):
            n = n + (j - 2 * SLOTS) * (place == base + j).astype(jnp.int32)
            n = n + (j - SLOTS) * (place == mate_base + j).astype(jnp.int32)
        index.append(n)

    def c1(p, o):
        return rcopy(sb.at[p], r1.at[o - 1], s1.at[o - 1], q1.at[o - 1], dev1(p))

    @pl.loop(0, 4)
    def _(i):
        p = (pos1 + jnp.where(i == 0, 2, jnp.where(i == 1, 1, jnp.where(i == 2, 3, 0)))) % 4
        o = (pos1 - p + 4) % 4
        for k in range(KB):
            for q in range(4):
                block = pbuf[index[k], pl.ds(p * 64 + q * 16, 16), :]
                sb[p, q, k] = (ratio * block).astype(BF16)

        @pl.when(i < 3)
        def _():
            c1(p, o).start()

    def c2(q):
        o = (pos2 - q + 4) % 4
        return rcopy(sb.at[pos1, q], r2.at[o - 1], s2.at[o - 1], q2.at[o - 1], dev2(q))

    for o in (1, 2, 3):
        c1(pos1, o).wait_recv()

    @pl.loop(1, 5)
    def _(k):
        q = (pos2 + k) % 4
        sb[pos1, q] = (sb[pos1, q] + r1[0, q]) + (r1[1, q] + r1[2, q])

        @pl.when(k < 4)
        def _():
            c2(q).start()

    for o in (1, 2, 3):
        c2((pos2 + o) % 4).wait_recv()
    f3[pos2] = (sb[pos1, pos2] + r2[0]) + (r2[1] + r2[2])

    def c3(o):
        return rcopy(f3.at[pos2], f3.at[pos2], s3.at[o - 1], q3.at[o - 1], dev2((pos2 - o + 4) % 4))

    def out(core, p, q):
        return up_ref.at[:, pl.ds(core * 256 + p * 64 + q * 16, 16), :]

    def c4(o, q):
        return rcopy(
            f3.at[q], out(c, pos1, q), s4.at[o - 1, q], q4.at[o - 1, q], dev1((pos1 - o + 4) % 4)
        )

    def cd_own(q):
        return rcopy(f3.at[q], out(c, pos1, q), sd.at[0, q], qd.at[0, q], mate)

    def cd(o, q):
        p = (pos1 + o) % 4
        return rcopy(out(c, p, q), out(c, p, q), sd.at[o, q], qd.at[o, q], mate)

    def keep(q):
        return pltpu.make_async_copy(f3.at[q], out(c, pos1, q), sl.at[q])

    for o in (2, 1, 3):
        c3(o).start()
    for k in (0, 1, 3, 2):
        q = (pos2 + k) % 4
        if k:
            rcopy(f3.at[pos2], f3.at[q], s3.at[k - 1], q3.at[k - 1], dev2(q)).wait_recv()
        for o in (2, 1, 3):
            c4(o, q).start()
        cd_own(q).start()
        keep(q).start()
    for o in (1, 3, 2):
        for k in (0, 1, 3, 2):
            q = (pos2 + k) % 4
            p = (pos1 + o) % 4
            rcopy(f3.at[q], out(c, p, q), s4.at[o - 1, q], q4.at[o - 1, q], dev1(p)).wait_recv()
            cd(o, q).start()

    for o in range(1, 16):
        ca(o).wait_send()
    for o in range(1, 2 * n_mp):
        cb(o).wait_send()
    for j in range(SLOTS):
        halves(j).wait_send()
    for k in range(1, 4):
        p = (pos1 + k) % 4
        c1(p, (pos1 - p + 4) % 4).wait_send()
        c2((pos2 + k) % 4).wait_send()
        c3(k).wait_send()
    for q in range(4):
        keep(q).wait()
        for o in (1, 2, 3):
            c4(o, q).wait_send()
            cd(o, q).wait_send()
        cd_own(q).wait_send()
        for o in range(4):
            p = (pos2 + o) % 4
            rcopy(f3.at[q], out(1 - c, p, q), sd.at[o, q], qd.at[o, q], mate).wait_recv()


def call_tail(owner, product, sq, n_mp):
    dma = pltpu.SemaphoreType.DMA
    return pl.pallas_call(
        functools.partial(tail_kernel, n_mp),
        name="tail",
        out_shape=jax.ShapeDtypeStruct((KB, BS, BS), BF16),
        in_specs=[pl.BlockSpec(memory_space=pltpu.SMEM)] + [pl.BlockSpec(memory_space=pltpu.VMEM)] * 2,
        out_specs=pl.BlockSpec(memory_space=pl.ANY),
        scratch_shapes=[
            pltpu.VMEM((16, 8, TL), F32),
            pltpu.VMEM((2 * n_mp, 8, TL), F32),
            pltpu.VMEM((2 * SLOTS + 1, 256, BS), F32),
            pltpu.VMEM((4, 4, KB, 16, BS), BF16),
            pltpu.VMEM((3, 4, KB, 16, BS), BF16),
            pltpu.VMEM((3, KB, 16, BS), BF16),
            pltpu.VMEM((4, KB, 16, BS), BF16),
            dma((15,)), dma((15,)), dma((2 * n_mp - 1,)), dma((2 * n_mp - 1,)),
            dma((SLOTS,)), dma((SLOTS,)), dma((SLOTS,)),
            dma((3,)), dma((3,)), dma((3,)), dma((3,)), dma((3,)), dma((3,)),
            dma((3, 4)), dma((3, 4)), dma((4, 4)), dma((4, 4)), dma((4,)),
        ],
        compiler_params=pltpu.CompilerParams(
            collective_id=2, has_side_effects=True, vmem_limit_bytes=16 << 20
        ),
    )(owner, product, sq)


def per_device(grads, block_owner, refresh_to, accum_old, roots_old):
    n_mp = lax.axis_size("mp")
    new, gs, lroot, rroot = call_main(block_owner, grads[0], accum_old[0, 0])
    new_accum, roots, sq, product = call_product(
        block_owner, refresh_to[0], new, gs, lroot, rroot, roots_old[0, 0]
    )
    update = call_tail(block_owner, product, sq, n_mp)
    return (new_accum[None, None], roots[None, None], update)


def solution(mesh):
    in_specs = (
        P("dp", "mp", None, None),
        P("mp", None),
        P("dp", "mp", None),
        P("dp", "mp", None, None, None, None),
        P("dp", "mp", None, None, None, None),
    )
    out_specs = (
        P("dp", "mp", None, None, None, None),
        P("dp", "mp", None, None, None, None),
        P("mp", None, None),
    )
    return jax.shard_map(
        per_device, mesh=mesh, in_specs=in_specs, out_specs=out_specs, check_vma=False
    )
```

```python
import functools

import jax
import jax.numpy as jnp
from jax import lax
from jax.experimental import pallas as pl
from jax.experimental.pallas import tpu as pltpu
from jax.sharding import PartitionSpec as P

MESH = pl.DeviceIdType.MESH
F32 = jnp.float32
BF16 = jnp.bfloat16

BS = 512
KB = 4
SLOTS = 2
TL = 128
TILES = [(a, b) for a in range(4) for b in range(a, 4)]
NT = len(TILES)
SP = 5
GP = 4
decay_rate = 0.8
epsilon = 1e-06


def coords():
    d = lax.axis_index("dp")
    return d // 8, (d // 2) % 4, d % 2


def at(y, z, c):
    return {"dp": (y * 4 + z) * 2 + c}


def dot_nt(a, b):
    return lax.dot_general(a, b, (((1,), (1,)), ((), ())), preferred_element_type=F32)


def dot_tn(a, b):
    return lax.dot_general(a, b, (((0,), (0,)), ((), ())), preferred_element_type=F32)


def dot_nn(a, b):
    return lax.dot_general(a, b, (((1,), (0,)), ((), ())), preferred_element_type=F32)


W0 = 25 / 16
W1 = -5 / 16 - 3125 / 4096
W2 = 3125 / 4096
W3 = -1250 / 4096
W4 = 250 / 4096
W5 = -25 / 4096
W6 = 1 / 4096


def split(x):
    hi = x.astype(BF16)
    return hi, (x - hi.astype(F32)).astype(BF16)


def dot3(ah, al, bh, bl):
    return dot_nn(ah, bh) + (dot_nn(ah, bl) + dot_nn(al, bh))


def find_slot(owner_ref, place):
    block = jnp.int32(0)
    alive = jnp.int32(0)
    for k in range(KB):
        hit = (owner_ref[0, k] == place).astype(jnp.int32)
        block = jnp.where(hit == 1, k, block)
        alive = jnp.maximum(alive, hit)
    return block, alive


def inverse_root(a_ref, store, bufs, hook):
    mf, m2f, nf, zf, mh, ml, ah, al, bh, bl, ch, cl = bufs
    a = a_ref[...]
    square = jnp.sum(a * a, axis=0, keepdims=True)
    mean = jnp.sum(square, axis=1, keepdims=True) * (1.0 / (BS * BS))
    scale = BS * jnp.sqrt(mean + epsilon)
    inverse = 1.0 / scale
    outer = 1.0 / jnp.sqrt(jnp.sqrt(scale))
    lo, up = slice(0, 256), slice(256, 512)

    def put(f, h, l, v, rows, cols):
        for x, r, k in ((v, rows, cols),) if rows is cols else ((v, rows, cols), (v.T, cols, rows)):
            hi = x.astype(BF16)
            h[r, k] = hi
            if f is not None:
                f[r, k] = x
            if l is not None:
                l[r, k] = (x - hi.astype(F32)).astype(BF16)

    def multiply(lh, ll, rh, rl, then):
        for rows, cols in ((lo, lo), (lo, up), (up, up)):
            if rl is None:
                q = dot_nn(lh[rows, :], rh[:, cols])
            else:
                q = dot3(lh[rows, :], ll[rows, :], rh[:, cols], rl[:, cols])
            then(q, rows, cols)

    for rows in (lo, up):
        x = a_ref[rows, :] * inverse
        mf[rows, :] = x
        mh[rows, :], ml[rows, :] = split(x)
    multiply(mh, ml, mh, ml, lambda q, r, k: put(m2f, ah, al, q, r, k))

    def third(q, r, k):
        m, m2 = mf[r, k], m2f[r, k]
        nf[r, k] = W1 * m + W2 * m2 + W3 * q
        put(None, bh, None, q, r, k)
        put(None, ch, None, W4 * m + W5 * m2 + W6 * q, r, k)

    multiply(ah, None, mh, None, third)
    multiply(ch, None, bh, None, lambda q, r, k: put(nf, ah, al, nf[r, k] + q, r, k))
    hook()
    multiply(ah, al, mh, ml, lambda q, r, k: put(zf, ch, cl, W0 * mf[r, k] + q, r, k))
    multiply(ah, al, ah, al, lambda q, r, k: put(m2f, bh, bl, (2 * W0) * nf[r, k] + q, r, k))
    multiply(bh, bl, bh, bl, lambda q, r, k: put(None, ah, al, (2 * W0 * W0) * m2f[r, k] + q, r, k))

    def last(q, r, k):
        x = 1.25 * nf[r, k] - (0.25 * W0**4) * zf[r, k] - 0.25 * q
        if r is k:
            rows = lax.broadcasted_iota(jnp.int32, (256, 256), 0)
            cols = lax.broadcasted_iota(jnp.int32, (256, 256), 1)
            x = x + jnp.where(rows == cols, F32(1.25 * W0), F32(0.0))
        x = outer * x
        store(r, k, x)
        if r is not k:
            store(k, r, x.T)

    multiply(ah, al, ch, cl, last)


class Spread:
    def __init__(self, st, r1, r2, every, sems, place):
        self.st, self.r1, self.r2, self.all = st, r1, r2, every
        self.s1, self.q1, self.s2, self.q2, self.s3, self.q3, self.s4, self.q4, self.sd, self.qd = sems
        self.c, self.pos1, self.pos2, self.dev1, self.dev2, self.mate = place

    def c1(self, p, q):
        o = (self.pos1 - p + 4) % 4 - 1
        return rcopy(
            self.st.at[p, q], self.r1.at[o, q], self.s1.at[o, q], self.q1.at[o, q], self.dev1(p)
        )

    def c2(self, q):
        o = (self.pos2 - q + 4) % 4 - 1
        return rcopy(self.st.at[self.pos1, q], self.r2.at[o], self.s2.at[o], self.q2.at[o], self.dev2(q))

    def c3(self, o, q, device):
        ref = self.all.at[self.c, self.pos1, q]
        return rcopy(ref, ref, self.s3.at[o - 1], self.q3.at[o - 1], device)

    def c4(self, o, p, q, device):
        ref = self.all.at[self.c, p, q]
        return rcopy(ref, ref, self.s4.at[o - 1, q], self.q4.at[o - 1, q], device)

    def cd(self, core, p, q):
        ref = self.all.at[core, p, q]
        return rcopy(ref, ref, self.sd.at[p, q], self.qd.at[p, q], self.mate)

    def send1(self, p):
        for k in range(4):
            self.c1(p, (self.pos2 + 1 + k) % 4).start()

    def add1(self):
        for k in range(1, 5):
            q = (self.pos2 + k) % 4
            for o in (1, 2, 3):
                self.c1((self.pos1 + o) % 4, q).wait_recv()
            self.st[self.pos1, q] = (self.st[self.pos1, q] + self.r1[0, q]) + (self.r1[1, q] + self.r1[2, q])
            if k < 4:
                self.c2(q).start()

    def add2(self):
        for o in (1, 2, 3):
            self.c2((self.pos2 + o) % 4).wait_recv()
        self.all[self.c, self.pos1, self.pos2] = (self.st[self.pos1, self.pos2] + self.r2[0]) + (
            self.r2[1] + self.r2[2]
        )
        for o in (2, 1, 3):
            self.c3(o, self.pos2, self.dev2((self.pos2 - o + 4) % 4)).start()

    def gather2(self):
        for k in (0, 1, 3, 2):
            q = (self.pos2 + k) % 4
            if k:
                self.c3(k, q, self.dev2(q)).wait_recv()
            for o in (1, 3):
                self.c4(o, self.pos1, q, self.dev1((self.pos1 - o + 4) % 4)).start()
            self.cd(self.c, self.pos1, q).start()

    def relay(self):
        for k in (0, 1, 3, 2):
            q = (self.pos2 + k) % 4
            for o in (1, 3):
                p = (self.pos1 + o) % 4
                self.c4(o, p, q, self.dev1(p)).wait_recv()
                if (o == 1) == (k < 2):
                    self.c4(2, p, q, self.dev1((self.pos1 - o + 4) % 4)).start()
                self.cd(self.c, p, q).start()

    def finish(self):
        p = (self.pos1 + 2) % 4
        for k in (0, 1, 3, 2):
            q = (self.pos2 + k) % 4
            self.c4(2, p, q, self.dev1(p)).wait_recv()
            self.cd(self.c, p, q).start()

    def from_mate(self):
        for p in range(4):
            for q in range(4):
                self.cd(1 - self.c, p, q).wait_recv()

    def sent(self):
        for o in (1, 2, 3):
            for q in range(4):
                self.c1((self.pos1 + o) % 4, q).wait_send()
                self.c4(o, self.pos1, q, self.dev1((self.pos1 - o + 4) % 4)).wait_send()
            self.c2((self.pos2 + o) % 4).wait_send()
            self.c3(o, self.pos2, self.dev2((self.pos2 - o + 4) % 4)).wait_send()
        for p in range(4):
            for q in range(4):
                self.cd(self.c, p, q).wait_send()

    @staticmethod
    def sems():
        dma = pltpu.SemaphoreType.DMA
        return [dma((3, 4)), dma((3, 4)), dma((3,)), dma((3,)), dma((3,)), dma((3,)),
                dma((3, 4)), dma((3, 4)), dma((4, 4)), dma((4, 4))]


ROWS = SP * 64
GROUP = 16
PACKED = ROWS + 32


def pack(ref, x):
    x = x.reshape(ROWS // GROUP, GROUP, TL)
    top = jnp.maximum(jnp.max(jnp.abs(x), axis=1), 1e-30)
    e = jnp.ceil(jnp.log2(top) * 64.0)
    inverse = 32700.0 * jnp.exp2(e * (-1.0 / 64.0))
    ref[0:ROWS, :] = jnp.round(x * inverse[:, None, :]).reshape(ROWS, TL).astype(jnp.int32).astype(jnp.int16)
    e = jnp.concatenate([e, jnp.zeros((32 - ROWS // GROUP, TL), F32)], axis=0)
    ref[ROWS:PACKED, :] = e.astype(jnp.int32).astype(jnp.int16)


def unpack(ref):
    e = ref[ROWS:PACKED, :].astype(jnp.int32).astype(F32)[: ROWS // GROUP]
    scale = jnp.exp2(e * (1.0 / 64.0)) * (1.0 / 32700.0)
    x = ref[0:ROWS, :].astype(jnp.int32).astype(F32).reshape(ROWS // GROUP, GROUP, TL)
    return (x * scale[:, None, :]).reshape(SP, 64, TL)


class PackedSpread(Spread):
    def __init__(self, raw, *rest):
        super().__init__(*rest)
        self.raw = raw

    def send1(self, p):
        @pl.loop(1, 5)
        def _(k):
            q = (self.pos2 + k) % 4
            pack(self.st.at[p, q], self.raw[p, q])
            self.c1(p, q).start()

    def add1(self):
        @pl.loop(1, 5)
        def _(k):
            q = (self.pos2 + k) % 4
            total = self.raw[self.pos1, q]
            for o in (1, 2, 3):
                self.c1((self.pos1 + o) % 4, q).wait_recv()
            for o in (1, 2, 3):
                total = total + unpack(self.r1.at[o - 1, q])
            self.raw[self.pos1, q] = total

            @pl.when(k < 4)
            def _():
                pack(self.st.at[self.pos1, q], total)
                self.c2(q).start()

    def add2(self):
        total = self.raw[self.pos1, self.pos2]
        for o in (1, 2, 3):
            self.c2((self.pos2 + o) % 4).wait_recv()
        for o in (1, 2, 3):
            total = total + unpack(self.r2.at[o - 1])
        pack(self.all.at[self.c, self.pos1, self.pos2], total)
        for o in (2, 1, 3):
            self.c3(o, self.pos2, self.dev2((self.pos2 - o + 4) % 4)).start()


def rcopy(src, dst, ss, rs, device):
    return pltpu.make_async_remote_copy(
        src_ref=src, dst_ref=dst, send_sem=ss, recv_sem=rs, device_id=device, device_id_type=MESH
    )


def main_kernel(owner_ref, g_ref, acc_ref, new_ref, gs_ref, lroot_ref, rroot_ref, *scratch):
    (praw, accs_v, raws, sts, sr1, sr2, sall, stg, gr1, gr2, rsend), scratch = scratch[:11], scratch[11:]
    bufs, scratch = scratch[:12], scratch[12:]
    ssem, gsem, (s_raw, s_acc, s_old, s_root, s_new) = scratch[:10], scratch[10:20], scratch[20:]
    y, z, c = coords()
    pos1 = z + c * (y - z)
    pos2 = y + c * (z - y)

    def dev1(p):
        return at(y + c * (p - y), p + c * (z - p), c)

    def dev2(p):
        return at(p + c * (y - p), z + c * (p - z), c)

    mate = at(y, z, 1 - c)
    place = (c, pos1, pos2, dev1, dev2, mate)
    stat = PackedSpread(raws, sts, sr1, sr2, sall, ssem, place)
    gsum = Spread(stg, gr1, gr2, gs_ref, gsem, place)

    olds = [pltpu.make_async_copy(acc_ref.at[j, 0], accs_v.at[SLOTS + j], s_old.at[j]) for j in range(SLOTS)]
    for a in olds:
        a.start()
    barrier = pltpu.get_barrier_semaphore()
    for o in (1, 2, 3):
        pl.semaphore_signal(barrier, inc=1, device_id=dev1((pos1 + o) % 4), device_id_type=MESH)
        pl.semaphore_signal(barrier, inc=1, device_id=dev2((pos2 + o) % 4), device_id_type=MESH)
    pl.semaphore_signal(barrier, inc=1, device_id=mate, device_id_type=MESH)
    pl.semaphore_wait(barrier, 7)

    raw = rcopy(g_ref.at[pl.ds(2 * (1 - c), 2)], praw, s_raw.at[0], s_raw.at[1], mate)
    raw.start()
    accs = [rcopy(acc_ref.at[j, 1], accs_v.at[j], s_acc.at[0, j], s_acc.at[1, j], mate) for j in range(SLOTS)]
    raw.wait()
    for a in accs:
        a.start()

    def put(p, a, b, block):
        t = TILES.index((a, b))
        for half in range(2):
            h = 2 * t + half
            raws[p, h // SP, h % SP] = block[half * 64:(half + 1) * 64]

    def quadrants(p, quad):
        x = quad(0, 0)
        put(p, 0, 0, x[:128, :128])
        put(p, 0, 1, x[:128, 128:])
        put(p, 1, 1, x[128:, 128:])
        x = quad(0, 1)
        put(p, 0, 2, x[:128, :128])
        put(p, 0, 3, x[:128, 128:])
        put(p, 1, 2, x[128:, :128])
        put(p, 1, 3, x[128:, 128:])
        x = quad(1, 1)
        put(p, 2, 2, x[:128, :128])
        put(p, 2, 3, x[:128, 128:])
        put(p, 3, 3, x[128:, 128:])

    @pl.loop(0, 4)
    def _(i):
        p = (pos1 + jnp.where(i == 0, 2, jnp.where(i == 1, 1, jnp.where(i == 2, 3, 0)))) % 4
        blk = p // 2

        @pl.when(p % 2 == 0)
        def _():
            quadrants(
                p,
                lambda a, b: dot_nt(
                    g_ref[2 * c + blk, a * 256:(a + 1) * 256, :], g_ref[2 * c + blk, b * 256:(b + 1) * 256, :]
                )
                + dot_nt(praw[blk, a * 256:(a + 1) * 256, :], praw[blk, b * 256:(b + 1) * 256, :]),
            )

        @pl.when(p % 2 == 1)
        def _():
            quadrants(
                p,
                lambda a, b: dot_tn(
                    g_ref[2 * c + blk, :, a * 256:(a + 1) * 256], g_ref[2 * c + blk, :, b * 256:(b + 1) * 256]
                )
                + dot_tn(praw[blk, :, a * 256:(a + 1) * 256], praw[blk, :, b * 256:(b + 1) * 256]),
            )

        @pl.when(i < 3)
        def _():
            stat.send1(p)

    @pl.loop(0, 4)
    def _(i):
        p = (pos1 + jnp.where(i == 0, 2, jnp.where(i == 1, 1, jnp.where(i == 2, 3, 0)))) % 4
        for q in range(4):
            rows = pl.ds((p % 2) * 256 + q * 64, 64)
            total = g_ref[2 * c + p // 2, rows, :].astype(F32) + praw[p // 2, rows, :].astype(F32)
            for k in range(GP):
                stg[p, q, k] = total[:, k * 128:(k + 1) * 128]

        @pl.when(i < 3)
        def _():
            gsum.send1(p)

    stat.add1()
    stat.add2()
    stat.gather2()
    gsum.add1()
    stat.relay()
    stat.finish()
    for a in accs:
        a.wait()
    for a in olds:
        a.wait()
    stat.from_mate()

    d = lax.axis_index("dp")
    other = d + 1 - 2 * c

    def blend(dst, blk, alive, lr):
        keep = jnp.where(alive == 1, F32(decay_rate), F32(1.0))
        take = jnp.where(alive == 1, F32((1.0 - decay_rate) / 16384.0), F32(0.0))
        for q in range(4):
            chunk = take * unpack(sall.at[blk // 2, 2 * (blk % 2) + lr, q])
            for n in range(SP):
                h = q * SP + n
                a, b = TILES[h // 2]
                half = h % 2
                fresh = chunk[n]
                ra, rb = pl.ds(a * TL + half * 64, 64), pl.ds(b * TL, TL)
                dst[ra, rb] = keep * dst[ra, rb] + fresh
                if a != b:
                    ca = pl.ds(a * TL + half * 64, 64)
                    dst[rb, ca] = keep * dst[rb, ca] + fresh.T

    def root(j):
        return rcopy(rsend.at[j], rroot_ref.at[j], s_root.at[0, j], s_root.at[1, j], mate)

    def left(j):
        return pltpu.make_async_copy(accs_v.at[SLOTS + j], new_ref.at[j, 0], s_new.at[0, j])

    def right(j):
        return rcopy(accs_v.at[j], new_ref.at[j, 1], s_new.at[1, j], s_new.at[2, j], mate)

    @pl.loop(0, 4)
    def _(t):
        j = t % 2

        own = t // 2
        blk, alive = find_slot(owner_ref, (other + own * (d - other)) * SLOTS + j)
        blend(accs_v.at[t], blk, alive, 1 - own)

        @pl.when(t < 2)
        def _():
            right(j).start()

        @pl.when(t >= 2)
        def _():
            left(j).start()

        def store(rows, cols, x):
            @pl.when(t < 2)
            def _():
                rsend[j, rows, cols] = x

            @pl.when(t >= 2)
            def _():
                lroot_ref[j, rows, cols] = x

        def hook():
            @pl.when(t == 0)
            def _():
                gsum.add2()

            @pl.when(t == 2)
            def _():
                gsum.relay()

            @pl.when(t == 3)
            def _():
                gsum.finish()

        inverse_root(accs_v.at[t], store, bufs, hook)

        @pl.when(t == 0)
        def _():
            gsum.gather2()

        @pl.when(t < 2)
        def _():
            root(j).start()

    for j in range(SLOTS):
        root(j).wait()
        left(j).wait()
        right(j).wait()
    gsum.from_mate()
    stat.sent()
    gsum.sent()


def call_main(owner, grads, acc):
    dma = pltpu.SemaphoreType.DMA
    vmem = pl.BlockSpec(memory_space=pltpu.VMEM)
    hbm = pl.BlockSpec(memory_space=pltpu.HBM)
    square = lambda n, dt: pltpu.VMEM(n + (BS, BS), dt)
    return pl.pallas_call(
        main_kernel,
        name="main",
        out_shape=(
            jax.ShapeDtypeStruct((SLOTS, 2, BS, BS), F32),
            jax.ShapeDtypeStruct((2, 4, 4, GP, 64, TL), F32),
            jax.ShapeDtypeStruct((SLOTS, BS, BS), F32),
            jax.ShapeDtypeStruct((SLOTS, BS, BS), F32),
        ),
        in_specs=[pl.BlockSpec(memory_space=pltpu.SMEM), vmem, hbm],
        out_specs=(hbm, vmem, vmem, vmem),
        scratch_shapes=[
            square((2,), BF16),
            square((2 * SLOTS,), F32),
            pltpu.VMEM((4, 4, SP, 64, TL), F32),
            pltpu.VMEM((4, 4, PACKED, TL), jnp.int16),
            pltpu.VMEM((3, 4, PACKED, TL), jnp.int16),
            pltpu.VMEM((3, PACKED, TL), jnp.int16),
            pltpu.VMEM((2, 4, 4, PACKED, TL), jnp.int16),
            pltpu.VMEM((4, 4, GP, 64, TL), F32),
            pltpu.VMEM((3, 4, GP, 64, TL), F32),
            pltpu.VMEM((3, GP, 64, TL), F32),
            square((SLOTS,), F32),
        ]
        + [square((), F32)] * 4 + [square((), BF16)] * 8
        + Spread.sems() + Spread.sems()
        + [dma((2,)), dma((2, SLOTS)), dma((SLOTS,)), dma((2, SLOTS)), dma((3, SLOTS))],
        compiler_params=pltpu.CompilerParams(
            collective_id=1, has_side_effects=True, vmem_limit_bytes=38 << 20
        ),
    )(owner, grads, acc)


def product_kernel(
    owner_ref, rf_ref, new_ref, gs_ref, l_ref, r_ref, old_ref,
    accum_ref, roots_ref, sq_ref, p_ref,
    flag, gh, gl, sem,
):
    d = lax.axis_index("dp")
    accum = pltpu.make_async_copy(new_ref, accum_ref, sem.at[0])
    accum.start()
    for j in range(SLOTS):
        blk, alive = find_slot(owner_ref, d * SLOTS + j)
        fresh = alive * (rf_ref[0, j] >= 0).astype(jnp.int32)
        flag[0, j], flag[1, j], flag[2, j] = blk, alive, fresh

        @pl.when(fresh == 1)
        def _():
            for i, ref in enumerate((l_ref, r_ref)):
                pltpu.make_async_copy(ref.at[j], roots_ref.at[j, i], sem.at[1 + 2 * j + i]).start()

        @pl.when(fresh == 0)
        def _():
            for i in range(2):
                pltpu.make_async_copy(old_ref.at[j, i], roots_ref.at[j, i], sem.at[1 + 2 * j + i]).start()

    sq_ref[...] = jnp.zeros_like(sq_ref)

    @pl.loop(0, SLOTS)
    def _(j):
        fresh = flag[2, j] == 1

        @pl.when(flag[1, j] == 1)
        def _():
            blk = flag[0, j]
            for h in range(2):
                for q in range(4):
                    for k in range(4):
                        rows, cols = pl.ds(h * 256 + q * 64, 64), pl.ds(k * TL, TL)
                        gh[0, rows, cols], gl[0, rows, cols] = split(
                            gs_ref[blk // 2, 2 * (blk % 2) + h, q, k]
                        )
            gh[1], gl[1] = split(jnp.where(fresh, r_ref[j], old_ref[j, 1]))

            @pl.loop(0, 2)
            def _(h):
                rows = pl.ds(pl.multiple_of(h * 256, 256), 256)
                ah, al = split(jnp.where(fresh, l_ref[j, rows, :], old_ref[j, 0, rows, :]))
                t = dot3(ah, al, gh[0], gl[0])
                th, tl = split(t)
                x = dot3(th, tl, gh[1], gl[1])
                p_ref[j, rows, :] = x
                part = jnp.sum((x * x).reshape(32, 8, BS), axis=0)
                sq_ref[...] += (part[:, :128] + part[:, 128:256]) + (part[:, 256:384] + part[:, 384:])

        @pl.when(flag[1, j] == 0)
        def _():
            p_ref[j] = jnp.zeros((BS, BS), F32)

    accum.wait()
    for j in range(SLOTS):
        for i in range(2):
            pltpu.make_async_copy(old_ref.at[j, i], roots_ref.at[j, i], sem.at[1 + 2 * j + i]).wait()


def call_product(owner, refresh, new, gs, lroot, rroot, old):
    anywhere = pl.BlockSpec(memory_space=pl.ANY)
    smem = pl.BlockSpec(memory_space=pltpu.SMEM)
    vmem = pl.BlockSpec(memory_space=pltpu.VMEM)
    hbm = pl.BlockSpec(memory_space=pltpu.HBM)
    return pl.pallas_call(
        product_kernel,
        name="product",
        out_shape=(
            jax.ShapeDtypeStruct((SLOTS, 2, BS, BS), F32),
            jax.ShapeDtypeStruct((SLOTS, 2, BS, BS), F32),
            jax.ShapeDtypeStruct((8, TL), F32),
            jax.ShapeDtypeStruct((SLOTS, BS, BS), F32),
        ),
        in_specs=[smem] * 2 + [hbm] + [vmem] * 4,
        out_specs=(anywhere, anywhere, vmem, vmem),
        scratch_shapes=[
            pltpu.SMEM((3, SLOTS), jnp.int32),
            pltpu.VMEM((2, BS, BS), BF16),
            pltpu.VMEM((2, BS, BS), BF16),
            pltpu.SemaphoreType.DMA((5,)),
        ],
        compiler_params=pltpu.CompilerParams(vmem_limit_bytes=16 << 20),
    )(owner, refresh, new, gs, lroot, rroot, old)


def tail_kernel(
    n_mp, owner_ref, p_ref, sq_ref, up_ref,
    na, nb, pbuf, sb, r1, r2, f3,
    s_a, q_a, s_b, q_b, s_p, q_p, s_own, s1, q1, s2, q2, s3, q3, s4, q4, sd, qd, sl,
):
    y, z, c = coords()
    x = lax.axis_index("mp")
    pos1 = z + c * (y - z)
    pos2 = y + c * (z - y)
    plane = y * 4 + z
    pair = x * 2 + c

    def dev1(p):
        return at(y + c * (p - y), p + c * (z - p), c)

    def dev2(p):
        return at(p + c * (y - p), z + c * (p - z), c)

    mate = at(y, z, 1 - c)

    def in_plane(n):
        return {"dp": n * 2 + c}

    def in_pair(n):
        return {"dp": plane * 2 + n % 2, "mp": n // 2}

    barrier = pltpu.get_barrier_semaphore()
    for o in range(1, 16):
        pl.semaphore_signal(barrier, inc=1, device_id=in_plane((plane + o) % 16), device_id_type=MESH)
    for o in range(1, 2 * n_mp):
        pl.semaphore_signal(barrier, inc=1, device_id=in_pair((pair + o) % (2 * n_mp)), device_id_type=MESH)
    pl.semaphore_wait(barrier, 15 + 2 * n_mp - 1)

    na[plane] = sq_ref[...]

    def ca(o):
        return rcopy(na.at[plane], na.at[plane], s_a.at[o - 1], q_a.at[o - 1], in_plane((plane - o + 16) % 16))

    for o in range(1, 16):
        ca(o).start()

    def halves(j):
        return rcopy(
            p_ref.at[j, pl.ds((1 - c) * 256, 256)], pbuf.at[SLOTS + j], s_p.at[j], q_p.at[j], mate
        )

    def own(j):
        return pltpu.make_async_copy(p_ref.at[j, pl.ds(c * 256, 256)], pbuf.at[j], s_own.at[j])

    for j in range(SLOTS):
        halves(j).start()
        own(j).start()
    pbuf[2 * SLOTS] = jnp.zeros((256, BS), F32)
    for o in range(1, 16):
        ca(o).wait_recv()
    total = na[0]
    for n in range(1, 16):
        total = total + na[n]
    nb[pair] = total

    def cb(o):
        n = 2 * n_mp
        return rcopy(nb.at[pair], nb.at[pair], s_b.at[o - 1], q_b.at[o - 1], in_pair((pair - o + n) % n))

    for o in range(1, 2 * n_mp):
        cb(o).start()
    for j in range(SLOTS):
        halves(j).wait_recv()
        own(j).wait()
    for o in range(1, 2 * n_mp):
        cb(o).wait_recv()
    total = nb[0]
    for n in range(1, 2 * n_mp):
        total = total + nb[n]
    square = jnp.sum(jnp.sum(total, axis=0, keepdims=True), axis=1, keepdims=True)
    ratio = 1.0 / jnp.sqrt(square / float(KB * n_mp * BS * BS) + epsilon)

    base = (plane * 2 + c) * SLOTS
    mate_base = (plane * 2 + 1 - c) * SLOTS
    index = []
    for k in range(KB):
        place = owner_ref[0, k]
        n = jnp.int32(2 * SLOTS)
        for j in range(SLOTS):
            n = n + (j - 2 * SLOTS) * (place == base + j).astype(jnp.int32)
            n = n + (j - SLOTS) * (place == mate_base + j).astype(jnp.int32)
        index.append(n)

    def c1(p, o, q):
        return rcopy(sb.at[p, q], r1.at[o - 1, q], s1.at[o - 1, q], q1.at[o - 1, q], dev1(p))

    @pl.loop(0, 4)
    def _(i):
        p = (pos1 + jnp.where(i == 0, 2, jnp.where(i == 1, 1, jnp.where(i == 2, 3, 0)))) % 4
        o = (pos1 - p + 4) % 4
        for n in range(1, 5):
            q = (pos2 + n) % 4
            for k in range(KB):
                block = pbuf[index[k], pl.ds(p * 64 + q * 16, 16), :]
                sb[p, q, k] = (ratio * block).astype(BF16)

            @pl.when(i < 3)
            def _():
                c1(p, o, q).start()

    def c2(q):
        o = (pos2 - q + 4) % 4
        return rcopy(sb.at[pos1, q], r2.at[o - 1], s2.at[o - 1], q2.at[o - 1], dev2(q))

    @pl.loop(1, 5)
    def _(k):
        q = (pos2 + k) % 4
        for o in (1, 2, 3):
            c1(pos1, o, q).wait_recv()
        sb[pos1, q] = (sb[pos1, q] + r1[0, q]) + (r1[1, q] + r1[2, q])

        @pl.when(k < 4)
        def _():
            c2(q).start()

    for o in (1, 2, 3):
        c2((pos2 + o) % 4).wait_recv()
    f3[pos2] = (sb[pos1, pos2] + r2[0]) + (r2[1] + r2[2])

    def c3(o):
        return rcopy(f3.at[pos2], f3.at[pos2], s3.at[o - 1], q3.at[o - 1], dev2((pos2 - o + 4) % 4))

    def out(core, p, q):
        return up_ref.at[:, pl.ds(core * 256 + p * 64 + q * 16, 16), :]

    def c4(o, q):
        return rcopy(
            f3.at[q], out(c, pos1, q), s4.at[o - 1, q], q4.at[o - 1, q], dev1((pos1 - o + 4) % 4)
        )

    def cd_own(q):
        return rcopy(f3.at[q], out(c, pos1, q), sd.at[0, q], qd.at[0, q], mate)

    def cd(o, q):
        p = (pos1 + o) % 4
        return rcopy(out(c, p, q), out(c, p, q), sd.at[o, q], qd.at[o, q], mate)

    def keep(q):
        return pltpu.make_async_copy(f3.at[q], out(c, pos1, q), sl.at[q])

    for o in (2, 1, 3):
        c3(o).start()
    for k in (0, 1, 3, 2):
        q = (pos2 + k) % 4
        if k:
            rcopy(f3.at[pos2], f3.at[q], s3.at[k - 1], q3.at[k - 1], dev2(q)).wait_recv()
        for o in (1, 3):
            c4(o, q).start()
        cd_own(q).start()
        keep(q).start()

    def onward(o, q):
        ref = out(c, (pos1 + o) % 4, q)
        return rcopy(ref, ref, s4.at[1, q], q4.at[1, q], dev1((pos1 - o + 4) % 4))

    for k in (0, 1, 3, 2):
        q = (pos2 + k) % 4
        for o in (1, 3):
            p = (pos1 + o) % 4
            rcopy(f3.at[q], out(c, p, q), s4.at[o - 1, q], q4.at[o - 1, q], dev1(p)).wait_recv()
            if (o == 1) == (k < 2):
                onward(o, q).start()
            cd(o, q).start()
    for k in (0, 1, 3, 2):
        q = (pos2 + k) % 4
        p = (pos1 + 2) % 4
        rcopy(out(c, p, q), out(c, p, q), s4.at[1, q], q4.at[1, q], dev1(p)).wait_recv()
        cd(2, q).start()

    for o in range(1, 16):
        ca(o).wait_send()
    for o in range(1, 2 * n_mp):
        cb(o).wait_send()
    for j in range(SLOTS):
        halves(j).wait_send()
    for k in range(1, 4):
        p = (pos1 + k) % 4
        for q in range(4):
            c1(p, (pos1 - p + 4) % 4, q).wait_send()
        c2((pos2 + k) % 4).wait_send()
        c3(k).wait_send()
    for q in range(4):
        keep(q).wait()
        for o in (1, 3):
            c4(o, q).wait_send()
        for o in (1, 2, 3):
            cd(o, q).wait_send()
        cd_own(q).wait_send()
        onward(1, q).wait_send()
        for o in range(4):
            p = (pos2 + o) % 4
            rcopy(f3.at[q], out(1 - c, p, q), sd.at[o, q], qd.at[o, q], mate).wait_recv()


def call_tail(owner, product, sq, n_mp):
    dma = pltpu.SemaphoreType.DMA
    return pl.pallas_call(
        functools.partial(tail_kernel, n_mp),
        name="tail",
        out_shape=jax.ShapeDtypeStruct((KB, BS, BS), BF16),
        in_specs=[pl.BlockSpec(memory_space=pltpu.SMEM)] + [pl.BlockSpec(memory_space=pltpu.VMEM)] * 2,
        out_specs=pl.BlockSpec(memory_space=pl.ANY),
        scratch_shapes=[
            pltpu.VMEM((16, 8, TL), F32),
            pltpu.VMEM((2 * n_mp, 8, TL), F32),
            pltpu.VMEM((2 * SLOTS + 1, 256, BS), F32),
            pltpu.VMEM((4, 4, KB, 16, BS), BF16),
            pltpu.VMEM((3, 4, KB, 16, BS), BF16),
            pltpu.VMEM((3, KB, 16, BS), BF16),
            pltpu.VMEM((4, KB, 16, BS), BF16),
            dma((15,)), dma((15,)), dma((2 * n_mp - 1,)), dma((2 * n_mp - 1,)),
            dma((SLOTS,)), dma((SLOTS,)), dma((SLOTS,)),
            dma((3, 4)), dma((3, 4)), dma((3,)), dma((3,)), dma((3,)), dma((3,)),
            dma((3, 4)), dma((3, 4)), dma((4, 4)), dma((4, 4)), dma((4,)),
        ],
        compiler_params=pltpu.CompilerParams(
            collective_id=2, has_side_effects=True, vmem_limit_bytes=16 << 20
        ),
    )(owner, product, sq)


def per_device(grads, block_owner, refresh_to, accum_old, roots_old):
    n_mp = lax.axis_size("mp")
    new, gs, lroot, rroot = call_main(block_owner, grads[0], accum_old[0, 0])
    new_accum, roots, sq, product = call_product(
        block_owner, refresh_to[0], new, gs, lroot, rroot, roots_old[0, 0]
    )
    update = call_tail(block_owner, product, sq, n_mp)
    return (new_accum[None, None], roots[None, None], update)


def solution(mesh):
    in_specs = (
        P("dp", "mp", None, None),
        P("mp", None),
        P("dp", "mp", None),
        P("dp", "mp", None, None, None, None),
        P("dp", "mp", None, None, None, None),
    )
    out_specs = (
        P("dp", "mp", None, None, None, None),
        P("dp", "mp", None, None, None, None),
        P("mp", None, None),
    )
    return jax.shard_map(
        per_device, mesh=mesh, in_specs=in_specs, out_specs=out_specs, check_vma=False
    )
```

```python
import functools

import jax
import jax.numpy as jnp
from jax import lax
from jax.experimental import pallas as pl
from jax.experimental.pallas import tpu as pltpu
from jax.sharding import PartitionSpec as P

MESH = pl.DeviceIdType.MESH
F32 = jnp.float32
BF16 = jnp.bfloat16

BS = 512
KB = 4
SLOTS = 2
TL = 128
TILES = [(a, b) for a in range(4) for b in range(a, 4)]
NT = len(TILES)
SP = 5
GP = 4
decay_rate = 0.8
epsilon = 1e-06


def coords():
    d = lax.axis_index("dp")
    return d // 8, (d // 2) % 4, d % 2


def at(y, z, c):
    return {"dp": (y * 4 + z) * 2 + c}


def dot_nt(a, b):
    return lax.dot_general(a, b, (((1,), (1,)), ((), ())), preferred_element_type=F32)


def dot_tn(a, b):
    return lax.dot_general(a, b, (((0,), (0,)), ((), ())), preferred_element_type=F32)


def dot_nn(a, b):
    return lax.dot_general(a, b, (((1,), (0,)), ((), ())), preferred_element_type=F32)


W0 = 25 / 16
W1 = -5 / 16 - 3125 / 4096
W2 = 3125 / 4096
W3 = -1250 / 4096
W4 = 250 / 4096
W5 = -25 / 4096
W6 = 1 / 4096


def split(x):
    hi = x.astype(BF16)
    return hi, (x - hi.astype(F32)).astype(BF16)


def dot3(ah, al, bh, bl):
    return dot_nn(ah, bh) + (dot_nn(ah, bl) + dot_nn(al, bh))


def find_slot(owner_ref, place):
    block = jnp.int32(0)
    alive = jnp.int32(0)
    for k in range(KB):
        hit = (owner_ref[0, k] == place).astype(jnp.int32)
        block = jnp.where(hit == 1, k, block)
        alive = jnp.maximum(alive, hit)
    return block, alive


def inverse_root(a_ref, store, bufs, hook):
    mf, m2f, nf, zf, mh, ml, ah, al, bh, bl, ch, cl = bufs
    a = a_ref[...]
    square = jnp.sum(a * a, axis=0, keepdims=True)
    mean = jnp.sum(square, axis=1, keepdims=True) * (1.0 / (BS * BS))
    scale = BS * jnp.sqrt(mean + epsilon)
    inverse = 1.0 / scale
    outer = 1.0 / jnp.sqrt(jnp.sqrt(scale))
    lo, up = slice(0, 256), slice(256, 512)

    def put(f, h, l, v, rows, cols):
        for x, r, k in ((v, rows, cols),) if rows is cols else ((v, rows, cols), (v.T, cols, rows)):
            hi = x.astype(BF16)
            h[r, k] = hi
            if f is not None:
                f[r, k] = x
            if l is not None:
                l[r, k] = (x - hi.astype(F32)).astype(BF16)

    def multiply(lh, ll, rh, rl, then):
        for rows, cols in ((lo, lo), (lo, up), (up, up)):
            if rl is None:
                q = dot_nn(lh[rows, :], rh[:, cols])
            else:
                q = dot3(lh[rows, :], ll[rows, :], rh[:, cols], rl[:, cols])
            then(q, rows, cols)

    for rows in (lo, up):
        x = a_ref[rows, :] * inverse
        mf[rows, :] = x
        mh[rows, :], ml[rows, :] = split(x)
    multiply(mh, ml, mh, ml, lambda q, r, k: put(m2f, ah, al, q, r, k))

    def third(q, r, k):
        m, m2 = mf[r, k], m2f[r, k]
        nf[r, k] = W1 * m + W2 * m2 + W3 * q
        put(None, bh, None, q, r, k)
        put(None, ch, None, W4 * m + W5 * m2 + W6 * q, r, k)

    multiply(ah, None, mh, None, third)
    multiply(ch, None, bh, None, lambda q, r, k: put(nf, ah, al, nf[r, k] + q, r, k))
    hook()
    multiply(ah, al, mh, ml, lambda q, r, k: put(zf, ch, cl, W0 * mf[r, k] + q, r, k))
    multiply(ah, al, ah, al, lambda q, r, k: put(m2f, bh, bl, (2 * W0) * nf[r, k] + q, r, k))
    multiply(bh, bl, bh, bl, lambda q, r, k: put(None, ah, al, (2 * W0 * W0) * m2f[r, k] + q, r, k))

    def last(q, r, k):
        x = 1.25 * nf[r, k] - (0.25 * W0**4) * zf[r, k] - 0.25 * q
        if r is k:
            rows = lax.broadcasted_iota(jnp.int32, (256, 256), 0)
            cols = lax.broadcasted_iota(jnp.int32, (256, 256), 1)
            x = x + jnp.where(rows == cols, F32(1.25 * W0), F32(0.0))
        x = outer * x
        store(r, k, x)
        if r is not k:
            store(k, r, x.T)

    multiply(ah, al, ch, cl, last)


class Spread:
    def __init__(self, st, r1, r2, every, sems, place):
        self.st, self.r1, self.r2, self.all = st, r1, r2, every
        self.s1, self.q1, self.s2, self.q2, self.s3, self.q3, self.s4, self.q4, self.sd, self.qd = sems
        self.c, self.pos1, self.pos2, self.dev1, self.dev2, self.mate = place

    def c1(self, p, q):
        o = (self.pos1 - p + 4) % 4 - 1
        return rcopy(
            self.st.at[p, q], self.r1.at[o, q], self.s1.at[o, q], self.q1.at[o, q], self.dev1(p)
        )

    def c2(self, q):
        o = (self.pos2 - q + 4) % 4 - 1
        return rcopy(self.st.at[self.pos1, q], self.r2.at[o], self.s2.at[o], self.q2.at[o], self.dev2(q))

    def c3(self, o, q, device):
        ref = self.all.at[self.c, self.pos1, q]
        return rcopy(ref, ref, self.s3.at[o - 1], self.q3.at[o - 1], device)

    def c4(self, o, p, q, device):
        ref = self.all.at[self.c, p, q]
        return rcopy(ref, ref, self.s4.at[o - 1, q], self.q4.at[o - 1, q], device)

    def cd(self, core, p, q):
        ref = self.all.at[core, p, q]
        return rcopy(ref, ref, self.sd.at[p, q], self.qd.at[p, q], self.mate)

    def send1(self, p):
        for k in range(4):
            self.c1(p, (self.pos2 + 1 + k) % 4).start()

    def add1(self):
        for k in range(1, 5):
            q = (self.pos2 + k) % 4
            for o in (1, 2, 3):
                self.c1((self.pos1 + o) % 4, q).wait_recv()
            self.st[self.pos1, q] = (self.st[self.pos1, q] + self.r1[0, q]) + (self.r1[1, q] + self.r1[2, q])
            if k < 4:
                self.c2(q).start()

    def add2(self):
        for o in (1, 2, 3):
            self.c2((self.pos2 + o) % 4).wait_recv()
        self.all[self.c, self.pos1, self.pos2] = (self.st[self.pos1, self.pos2] + self.r2[0]) + (
            self.r2[1] + self.r2[2]
        )
        for o in (2, 1, 3):
            self.c3(o, self.pos2, self.dev2((self.pos2 - o + 4) % 4)).start()

    def gather2(self):
        for k in (0, 1, 3, 2):
            q = (self.pos2 + k) % 4
            if k:
                self.c3(k, q, self.dev2(q)).wait_recv()
            for o in (1, 3):
                self.c4(o, self.pos1, q, self.dev1((self.pos1 - o + 4) % 4)).start()
            self.cd(self.c, self.pos1, q).start()

    def relay(self):
        for k in (0, 1, 3, 2):
            q = (self.pos2 + k) % 4
            for o in (1, 3):
                p = (self.pos1 + o) % 4
                self.c4(o, p, q, self.dev1(p)).wait_recv()
                if (o == 1) == (k < 2):
                    self.c4(2, p, q, self.dev1((self.pos1 - o + 4) % 4)).start()
                self.cd(self.c, p, q).start()

    def finish(self):
        p = (self.pos1 + 2) % 4
        for k in (0, 1, 3, 2):
            q = (self.pos2 + k) % 4
            self.c4(2, p, q, self.dev1(p)).wait_recv()
            self.cd(self.c, p, q).start()

    def from_mate(self):
        for p in range(4):
            for q in range(4):
                self.cd(1 - self.c, p, q).wait_recv()

    def sent(self):
        for o in (1, 2, 3):
            for q in range(4):
                self.c1((self.pos1 + o) % 4, q).wait_send()
                self.c4(o, self.pos1, q, self.dev1((self.pos1 - o + 4) % 4)).wait_send()
            self.c2((self.pos2 + o) % 4).wait_send()
            self.c3(o, self.pos2, self.dev2((self.pos2 - o + 4) % 4)).wait_send()
        for p in range(4):
            for q in range(4):
                self.cd(self.c, p, q).wait_send()

    @staticmethod
    def sems():
        dma = pltpu.SemaphoreType.DMA
        return [dma((3, 4)), dma((3, 4)), dma((3,)), dma((3,)), dma((3,)), dma((3,)),
                dma((3, 4)), dma((3, 4)), dma((4, 4)), dma((4, 4))]


ROWS = SP * 64
GROUP = 16
PACKED = ROWS + 32


def pack(ref, x):
    x = x.reshape(ROWS // GROUP, GROUP, TL)
    top = jnp.maximum(jnp.max(jnp.abs(x), axis=1), 1e-30)
    e = jnp.ceil(jnp.log2(top) * 64.0)
    inverse = 32700.0 * jnp.exp2(e * (-1.0 / 64.0))
    ref[0:ROWS, :] = jnp.round(x * inverse[:, None, :]).reshape(ROWS, TL).astype(jnp.int32).astype(jnp.int16)
    e = jnp.concatenate([e, jnp.zeros((32 - ROWS // GROUP, TL), F32)], axis=0)
    ref[ROWS:PACKED, :] = e.astype(jnp.int32).astype(jnp.int16)


def unpack(ref):
    e = ref[ROWS:PACKED, :].astype(jnp.int32).astype(F32)[: ROWS // GROUP]
    scale = jnp.exp2(e * (1.0 / 64.0)) * (1.0 / 32700.0)
    x = ref[0:ROWS, :].astype(jnp.int32).astype(F32).reshape(ROWS // GROUP, GROUP, TL)
    return (x * scale[:, None, :]).reshape(SP, 64, TL)


class PackedSpread(Spread):
    def __init__(self, raw, *rest):
        super().__init__(*rest)
        self.raw = raw

    def send1(self, p):
        @pl.loop(1, 5)
        def _(k):
            q = (self.pos2 + k) % 4
            pack(self.st.at[p, q], self.raw[p, q])
            self.c1(p, q).start()

    def add1(self):
        @pl.loop(1, 5)
        def _(k):
            q = (self.pos2 + k) % 4
            total = self.raw[self.pos1, q]
            for o in (1, 2, 3):
                self.c1((self.pos1 + o) % 4, q).wait_recv()
            for o in (1, 2, 3):
                total = total + unpack(self.r1.at[o - 1, q])
            self.raw[self.pos1, q] = total

            @pl.when(k < 4)
            def _():
                pack(self.st.at[self.pos1, q], total)
                self.c2(q).start()

    def add2(self):
        total = self.raw[self.pos1, self.pos2]
        for o in (1, 2, 3):
            self.c2((self.pos2 + o) % 4).wait_recv()
        for o in (1, 2, 3):
            total = total + unpack(self.r2.at[o - 1])
        pack(self.all.at[self.c, self.pos1, self.pos2], total)
        for o in (2, 1, 3):
            self.c3(o, self.pos2, self.dev2((self.pos2 - o + 4) % 4)).start()


def rcopy(src, dst, ss, rs, device):
    return pltpu.make_async_remote_copy(
        src_ref=src, dst_ref=dst, send_sem=ss, recv_sem=rs, device_id=device, device_id_type=MESH
    )


def main_kernel(owner_ref, g_ref, acc_ref, new_ref, gs_ref, lroot_ref, rroot_ref, *scratch):
    (praw, accs_v, raws, sts, sr1, sr2, sall, stg, gr1, gr2, rsend), scratch = scratch[:11], scratch[11:]
    bufs, scratch = scratch[:12], scratch[12:]
    ssem, gsem, (s_raw, s_acc, s_old, s_root, s_new) = scratch[:10], scratch[10:20], scratch[20:]
    y, z, c = coords()
    pos1 = z + c * (y - z)
    pos2 = y + c * (z - y)

    def dev1(p):
        return at(y + c * (p - y), p + c * (z - p), c)

    def dev2(p):
        return at(p + c * (y - p), z + c * (p - z), c)

    mate = at(y, z, 1 - c)
    place = (c, pos1, pos2, dev1, dev2, mate)
    stat = PackedSpread(raws, sts, sr1, sr2, sall, ssem, place)
    gsum = Spread(stg, gr1, gr2, gs_ref, gsem, place)

    olds = [pltpu.make_async_copy(acc_ref.at[j, 0], accs_v.at[SLOTS + j], s_old.at[j]) for j in range(SLOTS)]
    for a in olds:
        a.start()
    barrier = pltpu.get_barrier_semaphore()
    for o in (1, 2, 3):
        pl.semaphore_signal(barrier, inc=1, device_id=dev1((pos1 + o) % 4), device_id_type=MESH)
        pl.semaphore_signal(barrier, inc=1, device_id=dev2((pos2 + o) % 4), device_id_type=MESH)
    pl.semaphore_signal(barrier, inc=1, device_id=mate, device_id_type=MESH)
    pl.semaphore_wait(barrier, 7)

    raw = rcopy(g_ref.at[pl.ds(2 * (1 - c), 2)], praw, s_raw.at[0], s_raw.at[1], mate)
    raw.start()

    def first(p, a, b, block):
        t = TILES.index((a, b))
        for half in range(2):
            h = 2 * t + half
            raws[p, h // SP, h % SP] = block[half * 64:(half + 1) * 64]

    def second(p, a, b, block):
        t = TILES.index((a, b))
        for half in range(2):
            h = 2 * t + half
            raws[p, h // SP, h % SP] += block[half * 64:(half + 1) * 64]

    def quadrants(put, p, quad):
        x = quad(0, 0)
        put(p, 0, 0, x[:128, :128])
        put(p, 0, 1, x[:128, 128:])
        put(p, 1, 1, x[128:, 128:])
        x = quad(0, 1)
        put(p, 0, 2, x[:128, :128])
        put(p, 0, 3, x[:128, 128:])
        put(p, 1, 2, x[128:, :128])
        put(p, 1, 3, x[128:, 128:])
        x = quad(1, 1)
        put(p, 2, 2, x[:128, :128])
        put(p, 2, 3, x[:128, 128:])
        put(p, 3, 3, x[128:, 128:])

    def statistic(put, p, ref, blk):
        @pl.when(p % 2 == 0)
        def _():
            quadrants(
                put, p,
                lambda a, b: dot_nt(ref[blk, a * 256:(a + 1) * 256, :], ref[blk, b * 256:(b + 1) * 256, :]),
            )

        @pl.when(p % 2 == 1)
        def _():
            quadrants(
                put, p,
                lambda a, b: dot_tn(ref[blk, :, a * 256:(a + 1) * 256], ref[blk, :, b * 256:(b + 1) * 256]),
            )

    @pl.loop(0, 4)
    def _(p):
        statistic(first, p, g_ref, 2 * c + p // 2)

    accs = [rcopy(acc_ref.at[j, 1], accs_v.at[j], s_acc.at[0, j], s_acc.at[1, j], mate) for j in range(SLOTS)]
    raw.wait()
    for a in accs:
        a.start()

    @pl.loop(0, 4)
    def _(i):
        p = (pos1 + jnp.where(i == 0, 2, jnp.where(i == 1, 1, jnp.where(i == 2, 3, 0)))) % 4
        statistic(second, p, praw, p // 2)

        @pl.when(i < 3)
        def _():
            stat.send1(p)

    @pl.loop(0, 4)
    def _(i):
        p = (pos1 + jnp.where(i == 0, 2, jnp.where(i == 1, 1, jnp.where(i == 2, 3, 0)))) % 4
        for q in range(4):
            rows = pl.ds((p % 2) * 256 + q * 64, 64)
            total = g_ref[2 * c + p // 2, rows, :].astype(F32) + praw[p // 2, rows, :].astype(F32)
            for k in range(GP):
                stg[p, q, k] = total[:, k * 128:(k + 1) * 128]

        @pl.when(i < 3)
        def _():
            gsum.send1(p)

    stat.add1()
    stat.add2()
    stat.gather2()
    gsum.add1()
    stat.relay()
    stat.finish()
    for a in accs:
        a.wait()
    for a in olds:
        a.wait()
    stat.from_mate()

    d = lax.axis_index("dp")
    other = d + 1 - 2 * c

    def blend(dst, blk, alive, lr):
        keep = jnp.where(alive == 1, F32(decay_rate), F32(1.0))
        take = jnp.where(alive == 1, F32((1.0 - decay_rate) / 16384.0), F32(0.0))
        for q in range(4):
            chunk = take * unpack(sall.at[blk // 2, 2 * (blk % 2) + lr, q])
            for n in range(SP):
                h = q * SP + n
                a, b = TILES[h // 2]
                half = h % 2
                fresh = chunk[n]
                ra, rb = pl.ds(a * TL + half * 64, 64), pl.ds(b * TL, TL)
                dst[ra, rb] = keep * dst[ra, rb] + fresh
                if a != b:
                    ca = pl.ds(a * TL + half * 64, 64)
                    dst[rb, ca] = keep * dst[rb, ca] + fresh.T

    def root(j):
        return rcopy(rsend.at[j], rroot_ref.at[j], s_root.at[0, j], s_root.at[1, j], mate)

    def left(j):
        return pltpu.make_async_copy(accs_v.at[SLOTS + j], new_ref.at[j, 0], s_new.at[0, j])

    def right(j):
        return rcopy(accs_v.at[j], new_ref.at[j, 1], s_new.at[1, j], s_new.at[2, j], mate)

    @pl.loop(0, 4)
    def _(t):
        j = t % 2

        own = t // 2
        blk, alive = find_slot(owner_ref, (other + own * (d - other)) * SLOTS + j)
        blend(accs_v.at[t], blk, alive, 1 - own)

        @pl.when(t < 2)
        def _():
            right(j).start()

        @pl.when(t >= 2)
        def _():
            left(j).start()

        def store(rows, cols, x):
            @pl.when(t < 2)
            def _():
                rsend[j, rows, cols] = x

            @pl.when(t >= 2)
            def _():
                lroot_ref[j, rows, cols] = x

        def hook():
            @pl.when(t == 0)
            def _():
                gsum.add2()

            @pl.when(t == 2)
            def _():
                gsum.relay()

            @pl.when(t == 3)
            def _():
                gsum.finish()

        inverse_root(accs_v.at[t], store, bufs, hook)

        @pl.when(t == 0)
        def _():
            gsum.gather2()

        @pl.when(t < 2)
        def _():
            root(j).start()

    for j in range(SLOTS):
        root(j).wait()
        left(j).wait()
        right(j).wait()
    gsum.from_mate()
    stat.sent()
    gsum.sent()


def call_main(owner, grads, acc):
    dma = pltpu.SemaphoreType.DMA
    vmem = pl.BlockSpec(memory_space=pltpu.VMEM)
    hbm = pl.BlockSpec(memory_space=pltpu.HBM)
    square = lambda n, dt: pltpu.VMEM(n + (BS, BS), dt)
    return pl.pallas_call(
        main_kernel,
        name="main",
        out_shape=(
            jax.ShapeDtypeStruct((SLOTS, 2, BS, BS), F32),
            jax.ShapeDtypeStruct((2, 4, 4, GP, 64, TL), F32),
            jax.ShapeDtypeStruct((SLOTS, BS, BS), F32),
            jax.ShapeDtypeStruct((SLOTS, BS, BS), F32),
        ),
        in_specs=[pl.BlockSpec(memory_space=pltpu.SMEM), vmem, hbm],
        out_specs=(hbm, vmem, vmem, vmem),
        scratch_shapes=[
            square((2,), BF16),
            square((2 * SLOTS,), F32),
            pltpu.VMEM((4, 4, SP, 64, TL), F32),
            pltpu.VMEM((4, 4, PACKED, TL), jnp.int16),
            pltpu.VMEM((3, 4, PACKED, TL), jnp.int16),
            pltpu.VMEM((3, PACKED, TL), jnp.int16),
            pltpu.VMEM((2, 4, 4, PACKED, TL), jnp.int16),
            pltpu.VMEM((4, 4, GP, 64, TL), F32),
            pltpu.VMEM((3, 4, GP, 64, TL), F32),
            pltpu.VMEM((3, GP, 64, TL), F32),
            square((SLOTS,), F32),
        ]
        + [square((), F32)] * 4 + [square((), BF16)] * 8
        + Spread.sems() + Spread.sems()
        + [dma((2,)), dma((2, SLOTS)), dma((SLOTS,)), dma((2, SLOTS)), dma((3, SLOTS))],
        compiler_params=pltpu.CompilerParams(
            collective_id=1, has_side_effects=True, vmem_limit_bytes=38 << 20
        ),
    )(owner, grads, acc)


def product_kernel(
    owner_ref, rf_ref, new_ref, gs_ref, l_ref, r_ref, old_ref,
    accum_ref, roots_ref, sq_ref, p_ref,
    flag, gh, gl, sem,
):
    d = lax.axis_index("dp")
    accum = pltpu.make_async_copy(new_ref, accum_ref, sem.at[0])
    accum.start()
    for j in range(SLOTS):
        blk, alive = find_slot(owner_ref, d * SLOTS + j)
        fresh = alive * (rf_ref[0, j] >= 0).astype(jnp.int32)
        flag[0, j], flag[1, j], flag[2, j] = blk, alive, fresh

        @pl.when(fresh == 1)
        def _():
            for i, ref in enumerate((l_ref, r_ref)):
                pltpu.make_async_copy(ref.at[j], roots_ref.at[j, i], sem.at[1 + 2 * j + i]).start()

        @pl.when(fresh == 0)
        def _():
            for i in range(2):
                pltpu.make_async_copy(old_ref.at[j, i], roots_ref.at[j, i], sem.at[1 + 2 * j + i]).start()

    sq_ref[...] = jnp.zeros_like(sq_ref)

    @pl.loop(0, SLOTS)
    def _(j):
        fresh = flag[2, j] == 1

        @pl.when(flag[1, j] == 1)
        def _():
            blk = flag[0, j]
            for h in range(2):
                for q in range(4):
                    for k in range(4):
                        rows, cols = pl.ds(h * 256 + q * 64, 64), pl.ds(k * TL, TL)
                        gh[0, rows, cols], gl[0, rows, cols] = split(
                            gs_ref[blk // 2, 2 * (blk % 2) + h, q, k]
                        )
            gh[1], gl[1] = split(jnp.where(fresh, r_ref[j], old_ref[j, 1]))

            @pl.loop(0, 2)
            def _(h):
                rows = pl.ds(pl.multiple_of(h * 256, 256), 256)
                ah, al = split(jnp.where(fresh, l_ref[j, rows, :], old_ref[j, 0, rows, :]))
                t = dot3(ah, al, gh[0], gl[0])
                th, tl = split(t)
                x = dot3(th, tl, gh[1], gl[1])
                p_ref[j, rows, :] = x
                part = jnp.sum((x * x).reshape(32, 8, BS), axis=0)
                sq_ref[...] += (part[:, :128] + part[:, 128:256]) + (part[:, 256:384] + part[:, 384:])

        @pl.when(flag[1, j] == 0)
        def _():
            p_ref[j] = jnp.zeros((BS, BS), F32)

    accum.wait()
    for j in range(SLOTS):
        for i in range(2):
            pltpu.make_async_copy(old_ref.at[j, i], roots_ref.at[j, i], sem.at[1 + 2 * j + i]).wait()


def call_product(owner, refresh, new, gs, lroot, rroot, old):
    anywhere = pl.BlockSpec(memory_space=pl.ANY)
    smem = pl.BlockSpec(memory_space=pltpu.SMEM)
    vmem = pl.BlockSpec(memory_space=pltpu.VMEM)
    hbm = pl.BlockSpec(memory_space=pltpu.HBM)
    return pl.pallas_call(
        product_kernel,
        name="product",
        out_shape=(
            jax.ShapeDtypeStruct((SLOTS, 2, BS, BS), F32),
            jax.ShapeDtypeStruct((SLOTS, 2, BS, BS), F32),
            jax.ShapeDtypeStruct((8, TL), F32),
            jax.ShapeDtypeStruct((SLOTS, BS, BS), F32),
        ),
        in_specs=[smem] * 2 + [hbm] + [vmem] * 4,
        out_specs=(anywhere, anywhere, vmem, vmem),
        scratch_shapes=[
            pltpu.SMEM((3, SLOTS), jnp.int32),
            pltpu.VMEM((2, BS, BS), BF16),
            pltpu.VMEM((2, BS, BS), BF16),
            pltpu.SemaphoreType.DMA((5,)),
        ],
        compiler_params=pltpu.CompilerParams(vmem_limit_bytes=16 << 20),
    )(owner, refresh, new, gs, lroot, rroot, old)


def tail_kernel(
    n_mp, owner_ref, p_ref, sq_ref, up_ref,
    na, nb, pbuf, sb, r1, r2, f3,
    s_a, q_a, s_b, q_b, s_p, q_p, s_own, s1, q1, s2, q2, s3, q3, s4, q4, sd, qd, sl,
):
    y, z, c = coords()
    x = lax.axis_index("mp")
    pos1 = z + c * (y - z)
    pos2 = y + c * (z - y)
    plane = y * 4 + z
    pair = x * 2 + c

    def dev1(p):
        return at(y + c * (p - y), p + c * (z - p), c)

    def dev2(p):
        return at(p + c * (y - p), z + c * (p - z), c)

    mate = at(y, z, 1 - c)

    def in_plane(n):
        return {"dp": n * 2 + c}

    def in_pair(n):
        return {"dp": plane * 2 + n % 2, "mp": n // 2}

    barrier = pltpu.get_barrier_semaphore()
    for o in range(1, 16):
        pl.semaphore_signal(barrier, inc=1, device_id=in_plane((plane + o) % 16), device_id_type=MESH)
    for o in range(1, 2 * n_mp):
        pl.semaphore_signal(barrier, inc=1, device_id=in_pair((pair + o) % (2 * n_mp)), device_id_type=MESH)
    pl.semaphore_wait(barrier, 15 + 2 * n_mp - 1)

    na[plane] = sq_ref[...]

    def ca(o):
        return rcopy(na.at[plane], na.at[plane], s_a.at[o - 1], q_a.at[o - 1], in_plane((plane - o + 16) % 16))

    for o in range(1, 16):
        ca(o).start()

    def halves(j):
        return rcopy(
            p_ref.at[j, pl.ds((1 - c) * 256, 256)], pbuf.at[SLOTS + j], s_p.at[j], q_p.at[j], mate
        )

    def own(j):
        return pltpu.make_async_copy(p_ref.at[j, pl.ds(c * 256, 256)], pbuf.at[j], s_own.at[j])

    for j in range(SLOTS):
        halves(j).start()
        own(j).start()
    pbuf[2 * SLOTS] = jnp.zeros((256, BS), F32)
    for o in range(1, 16):
        ca(o).wait_recv()
    total = na[0]
    for n in range(1, 16):
        total = total + na[n]
    nb[pair] = total

    def cb(o):
        n = 2 * n_mp
        return rcopy(nb.at[pair], nb.at[pair], s_b.at[o - 1], q_b.at[o - 1], in_pair((pair - o + n) % n))

    for o in range(1, 2 * n_mp):
        cb(o).start()
    for j in range(SLOTS):
        halves(j).wait_recv()
        own(j).wait()
    for o in range(1, 2 * n_mp):
        cb(o).wait_recv()
    total = nb[0]
    for n in range(1, 2 * n_mp):
        total = total + nb[n]
    square = jnp.sum(jnp.sum(total, axis=0, keepdims=True), axis=1, keepdims=True)
    ratio = 1.0 / jnp.sqrt(square / float(KB * n_mp * BS * BS) + epsilon)

    base = (plane * 2 + c) * SLOTS
    mate_base = (plane * 2 + 1 - c) * SLOTS
    index = []
    for k in range(KB):
        place = owner_ref[0, k]
        n = jnp.int32(2 * SLOTS)
        for j in range(SLOTS):
            n = n + (j - 2 * SLOTS) * (place == base + j).astype(jnp.int32)
            n = n + (j - SLOTS) * (place == mate_base + j).astype(jnp.int32)
        index.append(n)

    def c1(p, o, q):
        return rcopy(sb.at[p, q], r1.at[o - 1, q], s1.at[o - 1, q], q1.at[o - 1, q], dev1(p))

    @pl.loop(0, 4)
    def _(i):
        p = (pos1 + jnp.where(i == 0, 2, jnp.where(i == 1, 1, jnp.where(i == 2, 3, 0)))) % 4
        o = (pos1 - p + 4) % 4
        for n in range(1, 5):
            q = (pos2 + n) % 4
            for k in range(KB):
                block = pbuf[index[k], pl.ds(p * 64 + q * 16, 16), :]
                sb[p, q, k] = (ratio * block).astype(BF16)

            @pl.when(i < 3)
            def _():
                c1(p, o, q).start()

    def c2(q):
        o = (pos2 - q + 4) % 4
        return rcopy(sb.at[pos1, q], r2.at[o - 1], s2.at[o - 1], q2.at[o - 1], dev2(q))

    @pl.loop(1, 5)
    def _(k):
        q = (pos2 + k) % 4
        for o in (1, 2, 3):
            c1(pos1, o, q).wait_recv()
        sb[pos1, q] = (sb[pos1, q] + r1[0, q]) + (r1[1, q] + r1[2, q])

        @pl.when(k < 4)
        def _():
            c2(q).start()

    for o in (1, 2, 3):
        c2((pos2 + o) % 4).wait_recv()
    f3[pos2] = (sb[pos1, pos2] + r2[0]) + (r2[1] + r2[2])

    def c3(o):
        return rcopy(f3.at[pos2], f3.at[pos2], s3.at[o - 1], q3.at[o - 1], dev2((pos2 - o + 4) % 4))

    def out(core, p, q):
        return up_ref.at[:, pl.ds(core * 256 + p * 64 + q * 16, 16), :]

    def c4(o, q):
        return rcopy(
            f3.at[q], out(c, pos1, q), s4.at[o - 1, q], q4.at[o - 1, q], dev1((pos1 - o + 4) % 4)
        )

    def cd_own(q):
        return rcopy(f3.at[q], out(c, pos1, q), sd.at[0, q], qd.at[0, q], mate)

    def cd(o, q):
        p = (pos1 + o) % 4
        return rcopy(out(c, p, q), out(c, p, q), sd.at[o, q], qd.at[o, q], mate)

    def keep(q):
        return pltpu.make_async_copy(f3.at[q], out(c, pos1, q), sl.at[q])

    for o in (2, 1, 3):
        c3(o).start()
    for k in (0, 1, 3, 2):
        q = (pos2 + k) % 4
        if k:
            rcopy(f3.at[pos2], f3.at[q], s3.at[k - 1], q3.at[k - 1], dev2(q)).wait_recv()
        for o in (1, 3):
            c4(o, q).start()
        cd_own(q).start()
        keep(q).start()

    def onward(o, q):
        ref = out(c, (pos1 + o) % 4, q)
        return rcopy(ref, ref, s4.at[1, q], q4.at[1, q], dev1((pos1 - o + 4) % 4))

    for k in (0, 1, 3, 2):
        q = (pos2 + k) % 4
        for o in (1, 3):
            p = (pos1 + o) % 4
            rcopy(f3.at[q], out(c, p, q), s4.at[o - 1, q], q4.at[o - 1, q], dev1(p)).wait_recv()
            if (o == 1) == (k < 2):
                onward(o, q).start()
            cd(o, q).start()
    for k in (0, 1, 3, 2):
        q = (pos2 + k) % 4
        p = (pos1 + 2) % 4
        rcopy(out(c, p, q), out(c, p, q), s4.at[1, q], q4.at[1, q], dev1(p)).wait_recv()
        cd(2, q).start()

    for o in range(1, 16):
        ca(o).wait_send()
    for o in range(1, 2 * n_mp):
        cb(o).wait_send()
    for j in range(SLOTS):
        halves(j).wait_send()
    for k in range(1, 4):
        p = (pos1 + k) % 4
        for q in range(4):
            c1(p, (pos1 - p + 4) % 4, q).wait_send()
        c2((pos2 + k) % 4).wait_send()
        c3(k).wait_send()
    for q in range(4):
        keep(q).wait()
        for o in (1, 3):
            c4(o, q).wait_send()
        for o in (1, 2, 3):
            cd(o, q).wait_send()
        cd_own(q).wait_send()
        onward(1, q).wait_send()
        for o in range(4):
            p = (pos2 + o) % 4
            rcopy(f3.at[q], out(1 - c, p, q), sd.at[o, q], qd.at[o, q], mate).wait_recv()


def call_tail(owner, product, sq, n_mp):
    dma = pltpu.SemaphoreType.DMA
    return pl.pallas_call(
        functools.partial(tail_kernel, n_mp),
        name="tail",
        out_shape=jax.ShapeDtypeStruct((KB, BS, BS), BF16),
        in_specs=[pl.BlockSpec(memory_space=pltpu.SMEM)] + [pl.BlockSpec(memory_space=pltpu.VMEM)] * 2,
        out_specs=pl.BlockSpec(memory_space=pl.ANY),
        scratch_shapes=[
            pltpu.VMEM((16, 8, TL), F32),
            pltpu.VMEM((2 * n_mp, 8, TL), F32),
            pltpu.VMEM((2 * SLOTS + 1, 256, BS), F32),
            pltpu.VMEM((4, 4, KB, 16, BS), BF16),
            pltpu.VMEM((3, 4, KB, 16, BS), BF16),
            pltpu.VMEM((3, KB, 16, BS), BF16),
            pltpu.VMEM((4, KB, 16, BS), BF16),
            dma((15,)), dma((15,)), dma((2 * n_mp - 1,)), dma((2 * n_mp - 1,)),
            dma((SLOTS,)), dma((SLOTS,)), dma((SLOTS,)),
            dma((3, 4)), dma((3, 4)), dma((3,)), dma((3,)), dma((3,)), dma((3,)),
            dma((3, 4)), dma((3, 4)), dma((4, 4)), dma((4, 4)), dma((4,)),
        ],
        compiler_params=pltpu.CompilerParams(
            collective_id=2, has_side_effects=True, vmem_limit_bytes=16 << 20
        ),
    )(owner, product, sq)


def per_device(grads, block_owner, refresh_to, accum_old, roots_old):
    n_mp = lax.axis_size("mp")
    new, gs, lroot, rroot = call_main(block_owner, grads[0], accum_old[0, 0])
    new_accum, roots, sq, product = call_product(
        block_owner, refresh_to[0], new, gs, lroot, rroot, roots_old[0, 0]
    )
    update = call_tail(block_owner, product, sq, n_mp)
    return (new_accum[None, None], roots[None, None], update)


def solution(mesh):
    in_specs = (
        P("dp", "mp", None, None),
        P("mp", None),
        P("dp", "mp", None),
        P("dp", "mp", None, None, None, None),
        P("dp", "mp", None, None, None, None),
    )
    out_specs = (
        P("dp", "mp", None, None, None, None),
        P("dp", "mp", None, None, None, None),
        P("mp", None, None),
    )
    return jax.shard_map(
        per_device, mesh=mesh, in_specs=in_specs, out_specs=out_specs, check_vma=False
    )
```
